32 devices in a mesh: dp: 4 (over z), seq: 4 (over x, core), rep: 2 (over y).
Axes of the slice: x: 2, y: 2, z: 4, core: 2. Of those that a mesh axis runs over, the one named last changes fastest.
Arguments:
- long_rows: bfloat16 [8, 1024, 768], P(('dp', 'rep'), 'seq'), may hold values from -6 to 6
- short_rows: bfloat16 [16, 256, 768], P(('dp', 'rep'), 'seq'), may hold values from -6 to 6
- long_memory: bfloat16 [8, 1024, 768], P(('dp', 'rep'), 'seq'), may hold values from -6 to 6
- short_memory: bfloat16 [16, 256, 768], P(('dp', 'rep'), 'seq'), may hold values from -6 to 6
- long_cotangent: bfloat16 [8, 1024, 768], P(('dp', 'rep'), 'seq'), may hold values from -6 to 6
- short_cotangent: bfloat16 [16, 256, 768], P(('dp', 'rep'), 'seq'), may hold values from -6 to 6
- long_lengths: int32 [8], P(('dp', 'rep')), may hold values from 769 to 1024, as said below
- short_lengths: int32 [16], P(('dp', 'rep')), may hold values from 193 to 256, as said below
- self_qkv: bfloat16 [3, 768, 768], replicated, may hold values from -0.21875 to 0.21875
- self_out: bfloat16 [768, 768], replicated, may hold values from -0.625 to 0.625
- self_bias: float32 [3, 768], replicated, may hold values from -0.6 to 0.6
- cross_qkv: bfloat16 [3, 768, 768], replicated, may hold values from -0.21875 to 0.21875
- cross_out: bfloat16 [768, 768], replicated, may hold values from -0.625 to 0.625
- cross_bias: float32 [3, 768], replicated, may hold values from -0.6 to 0.6
- norm_gain: float32 [3, 768], replicated, may hold values from 0.5 to 1.5
- norm_bias: float32 [3, 768], replicated, may hold values from -1.8 to 1.8
- up_proj: bfloat16 [768, 3072], replicated, may hold values from -0.21875 to 0.21875
- up_bias: float32 [3072], replicated, may hold values from -1.8 to 1.8
- down_proj: bfloat16 [3072, 768], replicated, may hold values from -0.109375 to 0.109375
- down_bias: float32 [768], replicated, may hold values from -1.8 to 1.8
Outputs:
- long_out: bfloat16 [8, 1024, 768], P(('dp', 'rep'), 'seq')
- short_out: bfloat16 [16, 256, 768], P(('dp', 'rep'), 'seq')
- long_grad: bfloat16 [8, 1024, 768], P(('dp', 'rep'), 'seq')
- short_grad: bfloat16 [16, 256, 768], P(('dp', 'rep'), 'seq')
- long_memory_grad: bfloat16 [8, 1024, 768], P(('dp', 'rep'), 'seq')
- short_memory_grad: bfloat16 [16, 256, 768], P(('dp', 'rep'), 'seq')
- self_qkv_grad: float32 [3, 768, 768], P(None, ('seq', 'rep'))
- self_out_grad: float32 [768, 768], P(('seq', 'rep'))
- self_bias_grad: float32 [3, 768], P(None, ('seq', 'rep'))
- cross_qkv_grad: float32 [3, 768, 768], P(None, ('seq', 'rep'))
- cross_out_grad: float32 [768, 768], P(('seq', 'rep'))
- cross_bias_grad: float32 [3, 768], P(None, ('seq', 'rep'))
- norm_gain_grad: float32 [3, 768], P(None, ('seq', 'rep'))
- norm_bias_grad: float32 [3, 768], P(None, ('seq', 'rep'))
- up_proj_grad: float32 [768, 3072], P(('seq', 'rep'))
- up_bias_grad: float32 [3072], P(('seq', 'rep'))
- down_proj_grad: float32 [3072, 768], P(('seq', 'rep'))
- down_bias_grad: float32 [768], P(('seq', 'rep'))
The draws below stay inside these ranges and needn't reach their ends.
Inputs may be any that keep to these rules, and one draw needn't show every extreme that they name: `long_lengths`: A row's length counts its leading real positions and those of its memory; one long row has exactly 1024. `short_lengths`: A row's length counts its leading real positions and those of its memory; one short row has exactly 256.
All inputs are finite; a program needn't handle non-finite values.
Results may differ from the reference program's by a relative error of at most 0.024.
Values may be sent and summed in bfloat16 or wider, within the bound.
A program may use at most 256 MiB of HBM per device.

```python
import jax
import jax.numpy as jnp
from jax import lax

D = 768
H = 12
HD = 64
FF = 3072
LONG = 1024
SHORT = 256
ROWS_L = 8
ROWS_S = 16


def draw_bucket(key, total_rows, seq_span):
    lowest = seq_span * 3 // 4 + 1
    first_key, second_key = jax.random.split(key)
    picked = jax.random.randint(first_key, (total_rows,), lowest, seq_span + 1, dtype=jnp.int32)
    chosen = jax.random.randint(second_key, (), 0, total_rows, dtype=jnp.int32)
    return jnp.where(jnp.arange(total_rows, dtype=jnp.int32) == chosen, seq_span, picked).astype(jnp.int32)


def draw_long_lengths(key, part):
    key = jax.random.fold_in(key, 3)
    return draw_bucket(key, ROWS_L, LONG)


def draw_short_lengths(key, part):
    key = jax.random.fold_in(key, 5)
    return draw_bucket(key, ROWS_S, SHORT)


def steps_of(key, dims, cuts, smallest, top_value):
    factor_of, own = 1.0, jax.random.fold_in(key, 6)
    for position, blocks in cuts:
        heights = jnp.exp(jax.random.uniform(jax.random.fold_in(own, position), (blocks,), jnp.float32, smallest / len(cuts), top_value / len(cuts)))
        factor_of = factor_of * jnp.repeat(heights, dims[position] // blocks).reshape([-1 if axis == position else 1 for axis in range(len(dims))])
    return factor_of


def normal_values(rng, extent, scale, reach, pieces=(), kind=jnp.bfloat16):
    drawn = scale * jax.random.normal(rng, extent, jnp.float32)
    if pieces:
        drawn = drawn * steps_of(rng, extent, pieces, -0.22, 0.18)
    return jnp.clip(drawn, -reach, reach).astype(kind)


def setup_inputs(seed: int = 0) -> dict:
    seeds = jax.random.split(jax.random.key(seed), 21)
    return {
        "long_rows": normal_values(seeds[0], (ROWS_L, LONG, D), 1.0, 6.0, ((0, 8), (1, 4))),
        "short_rows": normal_values(seeds[1], (ROWS_S, SHORT, D), 1.0, 6.0, ((0, 8), (1, 4))),
        "long_memory": normal_values(seeds[2], (ROWS_L, LONG, D), 1.0, 6.0, ((0, 8), (1, 4))),
        "short_memory": normal_values(seeds[3], (ROWS_S, SHORT, D), 1.0, 6.0, ((0, 8), (1, 4))),
        "long_cotangent": normal_values(seeds[4], (ROWS_L, LONG, D), 1.0, 6.0, ((0, 8), (1, 4))),
        "short_cotangent": normal_values(seeds[5], (ROWS_S, SHORT, D), 1.0, 6.0, ((0, 8), (1, 4))),
        "long_lengths": draw_long_lengths(jax.random.fold_in(seeds[20], 71), 0),
        "short_lengths": draw_short_lengths(jax.random.fold_in(seeds[20], 71), 0),
        "self_qkv": normal_values(seeds[8], (3, D, D), D ** -0.5, 0.21875),
        "self_out": normal_values(seeds[9], (D, D), (D // 8) ** -0.5, 0.625),
        "self_bias": normal_values(seeds[10], (3, D), 0.1, 0.6, (), jnp.float32),
        "cross_qkv": normal_values(seeds[11], (3, D, D), D ** -0.5, 0.21875),
        "cross_out": normal_values(seeds[12], (D, D), (D // 8) ** -0.5, 0.625),
        "cross_bias": normal_values(seeds[13], (3, D), 0.1, 0.6, (), jnp.float32),
        "norm_gain": jnp.clip(1.0 + 0.1 * jax.random.normal(seeds[14], (3, D), jnp.float32), 0.5, 1.5),
        "norm_bias": normal_values(seeds[15], (3, D), 0.3, 1.8, (), jnp.float32),
        "up_proj": normal_values(seeds[16], (D, FF), D ** -0.5, 0.21875),
        "up_bias": normal_values(seeds[17], (FF,), 0.3, 1.8, (), jnp.float32),
        "down_proj": normal_values(seeds[18], (FF, D), FF ** -0.5, 0.109375),
        "down_bias": normal_values(seeds[19], (D,), 0.3, 1.8, (), jnp.float32),
    }


@jax.custom_vjp
def low(v):
    return lax.optimization_barrier(v.astype(jnp.bfloat16)).astype(jnp.float32)

@jax.custom_vjp
def low_back(v):
    return v

def low_keep(v):
    return (low(v), None)

def low_pass(kept, grad):
    return (grad,)

def back_keep(v):
    return (v, None)

def back_low(kept, grad):
    return (low(grad),)
low.defvjp(low_keep, low_pass)
low_back.defvjp(back_keep, back_low)
highest = lax.Precision.HIGHEST
masked_score = -1000000000.0

def layer_norm(inputs, norm_scale, norm_shift):
    center = inputs - lax.optimization_barrier(jnp.mean(inputs, axis=-1, keepdims=True))
    spread = lax.optimization_barrier(jnp.mean(center * center, axis=-1, keepdims=True))
    return center * lax.rsqrt(spread + 1e-05) * norm_scale + norm_shift

def project(inputs, weight):
    return jnp.dot(inputs, weight, precision=highest, preferred_element_type=jnp.float32)

def attend(queries, key_rows, value_rows, length, causal):
    seq_len = queries.shape[0]
    queries = queries.reshape(seq_len, H, HD)
    key_rows = key_rows.reshape(seq_len, H, HD)
    value_rows = value_rows.reshape(seq_len, H, HD)
    raw_scores = low_back(jnp.einsum('qhd,khd->hqk', queries, key_rows, precision=highest))
    scores = raw_scores * HD ** (-0.5)
    key_pos = jnp.arange(seq_len, dtype=jnp.int32)[None, None, :]
    query_pos = jnp.arange(seq_len, dtype=jnp.int32)[None, :, None]
    allowed = key_pos < length
    if causal:
        allowed = jnp.logical_and(allowed, key_pos <= query_pos)
    scores = jnp.where(allowed, scores, masked_score)
    row_max = lax.optimization_barrier(jnp.max(scores, axis=-1, keepdims=True))
    weights = jnp.exp(scores - row_max)
    probs_all = weights / lax.optimization_barrier(jnp.sum(weights, axis=-1, keepdims=True))
    mixture = jnp.einsum('hqk,khd->qhd', low(probs_all), value_rows, precision=highest)
    return mixture.reshape(seq_len, H * HD)

def layer(params, one_row, memory, length):
    self_qkv, self_out, self_bias, cross_qkv, cross_out, cross_bias, norm_gain, norm_bias, up_proj, up_bias, down_proj, down_bias = params
    row_low = low(one_row)
    queries = low(low_back(project(row_low, self_qkv[0]) + self_bias[0]))
    key_rows = low(low_back(project(row_low, self_qkv[1])))
    value_rows = low(low_back(project(row_low, self_qkv[2]) + self_bias[1]))
    mixture = low(low_back(attend(queries, key_rows, value_rows, length, True)))
    branch = low_back(project(mixture, self_out) + self_bias[2])
    first_out = layer_norm(one_row + branch, norm_gain[0], norm_bias[0])
    first_low = low(first_out)
    memory_low = low(memory)
    cross_query = low(low_back(project(first_low, cross_qkv[0]) + cross_bias[0]))
    cross_keys = low(low_back(project(memory_low, cross_qkv[1])))
    cross_values = low(low_back(project(memory_low, cross_qkv[2]) + cross_bias[1]))
    cross_mix = low(low_back(attend(cross_query, cross_keys, cross_values, length, False)))
    cross_branch = low_back(project(cross_mix, cross_out) + cross_bias[2])
    second = layer_norm(first_out + cross_branch, norm_gain[1], norm_bias[1])
    hidden = low_back(project(low(second), up_proj) + up_bias)
    active = low(jax.nn.gelu(hidden, approximate=True))
    output = low_back(project(active, down_proj) + down_bias)
    return layer_norm(second + output, norm_gain[2], norm_bias[2])

def bucket(params, rows_all, memory_all, cotangent_all, lengths):

    def one_step(totals, item):
        one_row, memory, cotangent, length = item
        result, pullback = jax.vjp(lambda weights, inputs, context: layer(weights, inputs, context, length), params, one_row, memory)
        grads, row_grad, memory_grad = pullback(cotangent)
        totals = jax.tree.map(lambda former, latter: former + latter, totals, grads)
        return (totals, (result.astype(jnp.bfloat16), row_grad.astype(jnp.bfloat16), memory_grad.astype(jnp.bfloat16)))
    zeros_all = jax.tree.map(jnp.zeros_like, params)
    return lax.scan(one_step, zeros_all, (rows_all.astype(jnp.float32), memory_all.astype(jnp.float32), cotangent_all.astype(jnp.float32), lengths))

def reference(long_rows, short_rows, long_memory, short_memory, long_cotangent, short_cotangent, long_lengths, short_lengths, self_qkv, self_out, self_bias, cross_qkv, cross_out, cross_bias, norm_gain, norm_bias, up_proj, up_bias, down_proj, down_bias):
    params = (self_qkv.astype(jnp.float32), self_out.astype(jnp.float32), self_bias.astype(jnp.float32), cross_qkv.astype(jnp.float32), cross_out.astype(jnp.float32), cross_bias.astype(jnp.float32), norm_gain.astype(jnp.float32), norm_bias.astype(jnp.float32), up_proj.astype(jnp.float32), up_bias.astype(jnp.float32), down_proj.astype(jnp.float32), down_bias.astype(jnp.float32))
    long_totals, long_results = bucket(params, long_rows, long_memory, long_cotangent, long_lengths)
    short_totals, short_results = bucket(params, short_rows, short_memory, short_cotangent, short_lengths)
    totals = jax.tree.map(lambda former, latter: former + latter, long_totals, short_totals)
    return (long_results[0], short_results[0], long_results[1], short_results[1], long_results[2], short_results[2], totals[0], totals[1], totals[2], totals[3], totals[4], totals[5], totals[6], totals[7], totals[8], totals[9], totals[10], totals[11])
```

```python
import functools

import jax
import jax.numpy as jnp
from jax import lax
from jax.experimental import pallas as pl
from jax.experimental.pallas import tpu as pltpu
from jax.sharding import PartitionSpec as P

HD = 64
PAIR = 2 * HD
F32 = jnp.float32
BF16 = jnp.bfloat16
NEG = -1000000000.0
MIB = 1024 * 1024

ANY = pl.BlockSpec(memory_space=pl.ANY)
VMEM = pl.BlockSpec(memory_space=pltpu.VMEM)
SMEM = pl.BlockSpec(memory_space=pltpu.SMEM)


def dot(a, b):
    return jnp.dot(a, b, preferred_element_type=F32)


def dot_t(a, b):
    return lax.dot_general(a, b, (((1,), (1,)), ((), ())), preferred_element_type=F32)


def loop(count, body):
    lax.fori_loop(0, count, lambda i, c: (body(i), c)[1], 0)


def tile(j, width):
    return pl.ds(pl.multiple_of(j * width, width), width)


def norm_parts(z):
    center = z - jnp.mean(z, axis=-1, keepdims=True)
    rstd = lax.rsqrt(jnp.mean(center * center, axis=-1, keepdims=True) + 1e-05)
    return center * rstd, rstd


def norm_back(dy, gain, xhat, rstd):
    dyg = dy * gain
    mean_a = jnp.mean(dyg, axis=-1, keepdims=True)
    mean_b = jnp.mean(dyg * xhat, axis=-1, keepdims=True)
    return rstd * (dyg - mean_a - xhat * mean_b)


def col_sum(a):
    return jnp.sum(a.astype(F32), axis=0, keepdims=True)


def transpose_into(dst_ref, src_ref, rows, cols, row_off=0):
    def body(j):
        dst_ref[tile(j, 128), row_off : row_off + rows] = src_ref[
            row_off : row_off + rows, tile(j, 128)
        ].T

    loop(cols // 128, body)


class Copies:
    def __init__(self, sems):
        self.sems, self.used = sems, 0

    def start(self, src, dst):
        copy = pltpu.make_async_copy(src, dst, self.sems.at[self.used])
        self.used += 1
        copy.start()
        return copy


def head_masks(dtype):
    lane = lax.broadcasted_iota(jnp.int32, (1, PAIR), 1)
    low = (lane < HD).astype(F32)
    return low.astype(dtype), (1.0 - low).astype(dtype)


def stack_heads(a, masks):
    return jnp.concatenate([a * masks[0], a * masks[1]], axis=0)


def unstack_heads(out_t, width):
    sub = lax.broadcasted_iota(jnp.int32, (PAIR, width), 0)
    return jnp.where(sub < HD, out_t[:, :width], out_t[:, width:]).T


def key_positions(block, keys, queries, size, me):
    row = lax.broadcasted_iota(jnp.int32, (keys, queries), 0)
    if keys == size:
        return row + (block ^ me) * size
    return ((row // size) ^ me) * size + row % size


def limits(queries, size, me, length, causal):
    if not causal:
        return length - 1
    lane = lax.broadcasted_iota(jnp.int32, (1, queries), 1) % size
    return jnp.minimum(lane + me * size, length - 1)


def attend_forward(dims, causal, info, q_ref, k_ref, v_ref, o_ref, lse_l, lse_s, s_scr):
    T, LL, LS, NS, D, n = dims
    me = info[NS + 1]
    masks = head_masks(BF16)

    def pair(p):
        c = tile(p, PAIR)
        q2 = stack_heads(q_ref[0:LL, c], masks)
        lim = limits(2 * LL, LL, me, info[0], causal)
        top = None
        for r in range(n):
            s = dot_t(k_ref[r * T : r * T + LL, c], q2)
            s = jnp.where(key_positions(r, LL, 2 * LL, LL, me) <= lim, s, NEG)
            s_scr[r * LL : (r + 1) * LL, :] = s
            m = jnp.max(s, axis=0, keepdims=True)
            top = m if top is None else jnp.maximum(top, m)
        total, acc = None, None
        for r in range(n):
            w = jnp.exp(s_scr[r * LL : (r + 1) * LL, :] - top)
            t = jnp.sum(w, axis=0, keepdims=True)
            a = dot(v_ref[r * T : r * T + LL, c].T, w.astype(BF16))
            total = t if total is None else total + t
            acc = a if acc is None else acc + a
        acc = acc * (1.0 / total)
        o_ref[0:LL, c] = unstack_heads(acc, LL).astype(BF16)
        lse_l[p] = jnp.broadcast_to(top + jnp.log(total), (8, 2 * LL))
        for i in range(NS):
            off = LL + i * LS
            q2 = stack_heads(q_ref[off : off + LS, c], masks)
            kb = jnp.concatenate([k_ref[r * T + off : r * T + off + LS, c] for r in range(n)], 0)
            vb = jnp.concatenate([v_ref[r * T + off : r * T + off + LS, c] for r in range(n)], 0)
            s = dot_t(kb, q2)
            lim = limits(2 * LS, LS, me, info[1 + i], causal)
            s = jnp.where(key_positions(0, n * LS, 2 * LS, LS, me) <= lim, s, NEG)
            top = jnp.max(s, axis=0, keepdims=True)
            w = jnp.exp(s - top)
            total = jnp.sum(w, axis=0, keepdims=True)
            acc = dot(vb.T, w.astype(BF16)) * (1.0 / total)
            o_ref[off : off + LS, c] = unstack_heads(acc, LS).astype(BF16)
            lse_s[p * NS + i] = jnp.broadcast_to(top + jnp.log(total), (8, 2 * LS))

    loop(D // PAIR, pair)


def attend_backward(
    dims, causal, info, q_ref, k_ref, v_ref, o_ref, do_ref, lse_l, lse_s, dq_ref, dk_ref, dv_ref
):
    T, LL, LS, NS, D, n = dims
    me = info[NS + 1]
    masks = head_masks(BF16)
    ones = jnp.ones((8, PAIR), F32)

    def row_dots(do2, o):
        prod = do2.astype(F32) * jnp.concatenate([o, o], 0).astype(F32)
        full = lax.dot_general(
            ones,
            prod,
            (((1,), (1,)), ((), ())),
            precision=lax.Precision.HIGHEST,
            preferred_element_type=F32,
        )
        return full[0:1]

    def pair(p):
        c = tile(p, PAIR)
        q2 = stack_heads(q_ref[0:LL, c], masks)
        do2 = stack_heads(do_ref[0:LL, c], masks)
        delta = row_dots(do2, o_ref[0:LL, c])
        lse = lse_l[p][0:1]
        lim = limits(2 * LL, LL, me, info[0], causal)
        dq_t = None
        for r in range(n):
            rows = slice(r * T, r * T + LL)
            kb, vb = k_ref[rows, c], v_ref[rows, c]
            s = dot_t(kb, q2)
            s = jnp.where(key_positions(r, LL, 2 * LL, LL, me) <= lim, s, NEG)
            probs = jnp.exp(s - lse)
            ds = (probs * (dot_t(vb, do2) - delta)).astype(BF16)
            dv_ref[rows, c] = dot(probs.astype(BF16), do2).astype(BF16)
            dk_ref[rows, c] = dot(ds, q2).astype(BF16)
            part = dot(kb.T, ds)
            dq_t = part if dq_t is None else dq_t + part
        dq_ref[0:LL, c] = (unstack_heads(dq_t, LL) * HD**-0.5).astype(BF16)
        for i in range(NS):
            off = LL + i * LS
            q2 = stack_heads(q_ref[off : off + LS, c], masks)
            do2 = stack_heads(do_ref[off : off + LS, c], masks)
            delta = row_dots(do2, o_ref[off : off + LS, c])
            lse = lse_s[p * NS + i][0:1]
            kb = jnp.concatenate([k_ref[r * T + off : r * T + off + LS, c] for r in range(n)], 0)
            vb = jnp.concatenate([v_ref[r * T + off : r * T + off + LS, c] for r in range(n)], 0)
            s = dot_t(kb, q2)
            lim = limits(2 * LS, LS, me, info[1 + i], causal)
            s = jnp.where(key_positions(0, n * LS, 2 * LS, LS, me) <= lim, s, NEG)
            probs = jnp.exp(s - lse)
            ds = (probs * (dot_t(vb, do2) - delta)).astype(BF16)
            dv = dot(probs.astype(BF16), do2).astype(BF16)
            dk = dot(ds, q2).astype(BF16)
            for r in range(n):
                dv_ref[r * T + off : r * T + off + LS, c] = dv[r * LS : (r + 1) * LS]
                dk_ref[r * T + off : r * T + off + LS, c] = dk[r * LS : (r + 1) * LS]
            dq_ref[off : off + LS, c] = (unstack_heads(dot(kb.T, ds), LS) * HD**-0.5).astype(BF16)

    loop(D // PAIR, pair)


def forward_kernel(dims, cross, *refs):
    T, LL, LS, NS, D, n = dims
    refs = list(refs)
    info = refs.pop(0)
    blocks = [refs.pop(0) for _ in range(n)]
    w_hbm, wo_hbm, bias = refs.pop(0), refs.pop(0), refs.pop(0)
    if cross:
        z_in, gain, shift = refs.pop(0), refs.pop(0), refs.pop(0)
    q_out, k_out, v_out, o_out, lse_l, lse_s, z_out = [refs.pop(0) for _ in range(7)]
    blk, w, wo, k, v, s_scr, sems = refs
    copies = Copies(sems)
    loads = [copies.start(w_hbm.at[0], w.at[0])]
    loads += [copies.start(blocks[r], blk.at[r * T : (r + 1) * T]) for r in range(n)]
    loads += [copies.start(w_hbm.at[i], w.at[i]) for i in (1, 2)]
    loads.append(copies.start(wo_hbm, wo))
    if cross:
        xhat, _ = norm_parts(z_in[...])
        z_out[...] = xhat * gain[0:1] + shift[0:1]
        source = z_out
    else:
        loads[1].wait()
        source = blk
    loads[0].wait()

    def q_tile(j):
        c = tile(j, 256)
        q = dot(source[0:T, :].astype(BF16), w[0, :, c]) + bias[0:1, c]
        q_out[:, c] = (q.astype(BF16).astype(F32) * HD**-0.5).astype(BF16)

    loop(D // 256, q_tile)
    for item in loads[1 if cross else 2 : n + 3]:
        item.wait()

    def kv_tile(j):
        r, c = tile(j // (D // 256), T), tile(j % (D // 256), 256)
        x = blk[r, :]
        k[r, c] = dot(x, w[1, :, c]).astype(BF16)
        v[r, c] = (dot(x, w[2, :, c]) + bias[1:2, c]).astype(BF16)

    loop(n * (D // 256), kv_tile)
    stores = [copies.start(k, k_out), copies.start(v, v_out)]
    attend_forward(dims, not cross, info, q_out, k, v, o_out, lse_l, lse_s, s_scr)
    loads[n + 3].wait()

    def z_tile(j):
        c = tile(j, 256)
        z_out[:, c] = source[0:T, c].astype(F32) + dot(o_out[...], wo[:, c]) + bias[2:3, c]

    loop(D // 256, z_tile)
    for item in stores:
        item.wait()


def forward_call(dims, cross, info, blocks, w, wo, bias, extra):
    T, LL, LS, NS, D, n = dims
    pairs = D // PAIR
    extra_specs = [VMEM] * len(extra)
    return pl.pallas_call(
        functools.partial(forward_kernel, dims, cross),
        out_shape=[
            jax.ShapeDtypeStruct((T, D), BF16),
            jax.ShapeDtypeStruct((n * T, D), BF16),
            jax.ShapeDtypeStruct((n * T, D), BF16),
            jax.ShapeDtypeStruct((T, D), BF16),
            jax.ShapeDtypeStruct((pairs, 8, 2 * LL), F32),
            jax.ShapeDtypeStruct((pairs * NS, 8, 2 * LS), F32),
            jax.ShapeDtypeStruct((T, D), F32),
        ],
        in_specs=[SMEM] + [ANY] * n + [ANY, ANY, VMEM] + extra_specs,
        out_specs=[VMEM, ANY, ANY, VMEM, VMEM, VMEM, VMEM],
        scratch_shapes=[
            pltpu.VMEM((n * T, D), BF16),
            pltpu.VMEM((3, D, D), BF16),
            pltpu.VMEM((D, D), BF16),
            pltpu.VMEM((n * T, D), BF16),
            pltpu.VMEM((n * T, D), BF16),
            pltpu.VMEM((n * LL, 2 * LL), F32),
            pltpu.SemaphoreType.DMA((n + 6,)),
        ],
        compiler_params=pltpu.CompilerParams(vmem_limit_bytes=40 * MIB),
        cost_estimate=pl.CostEstimate(
            flops=20 * 10**9, bytes_accessed=20 * 10**6, transcendentals=4 * 10**6
        ),
        name="cross_forward" if cross else "self_forward",
    )(info, *blocks, w, wo, bias, *extra)


def feed_kernel(T, D, FF, chunks, *refs):
    (
        pos_a, pos_b, z2, cot, wup_hbm, wdown_hbm, upb, downb, gain, shift,
        y_out, dz2_out, gup_out, gdown_out, vec_out, upb_out,
        wup, wdown, h2t, g, gp, acc, dfs, gup, gdown, sems,
    ) = refs
    copies = Copies(sems)
    load_up = copies.start(wup_hbm, wup)
    load_down = copies.start(wdown_hbm, wdown)
    tile_f = FF // 8
    rows = D // chunks
    xhat2, rstd2 = norm_parts(z2[...])
    h2 = xhat2 * gain[1:2] + shift[1:2]
    h2b = h2.astype(BF16)
    dfs[...] = h2b
    acc[...] = h2 + downb[...]
    transpose_into(h2t, dfs, T, D)
    load_up.wait()
    load_down.wait()

    def up_tile(j):
        c = tile(j, tile_f)
        u = dot(dfs[...], wup[:, c]) + upb[:, c]
        sq = u * u
        th = jnp.tanh(0.7978845608028654 * u * (1.0 + 0.044715 * sq))
        half = 0.5 * (1.0 + th)
        act = (u * half).astype(BF16)
        g[:, c] = act
        gp[:, c] = half + (0.5 * 0.7978845608028654) * u * (1.0 - th * th) * (
            1.0 + (3.0 * 0.044715) * sq
        )
        acc[...] += dot(act, wdown[c, :])

    loop(8, up_tile)
    xhat3, rstd3 = norm_parts(acc[...])
    y_out[...] = (xhat3 * gain[2:3] + shift[2:3]).astype(BF16)
    dy = cot[...].astype(F32)
    vec_out[0:1] = col_sum(dy * xhat3)
    vec_out[1:2] = col_sum(dy)
    dz3 = norm_back(dy, gain[2:3], xhat3, rstd3)
    df = dz3.astype(BF16)
    dfs[...] = df
    acc[...] = dz3
    vec_out[2:3] = col_sum(df)

    def back_tile(j):
        c = tile(j, tile_f)
        dg = dot_t(dfs[...], wdown[c, :])
        du = (gp[:, c] * dg).astype(BF16)
        upb_out[j] = jnp.broadcast_to(col_sum(du), (8, tile_f))
        acc[...] += dot_t(du, wup[:, c])
        grad = dot(h2t[...], du).astype(BF16)
        for s in range(chunks):
            gup[pos_a[s], :, c] = grad[s * rows : (s + 1) * rows]
        gdown[pos_b[j]] = dot(g[:, c].T, dfs[...]).astype(BF16)

    loop(8, back_tile)
    stores = [copies.start(gup, gup_out), copies.start(gdown, gdown_out)]
    dh2 = acc[...]
    xhat2, rstd2 = norm_parts(z2[...])
    vec_out[3:4] = col_sum(dh2 * xhat2)
    vec_out[4:5] = col_sum(dh2)
    vec_out[5:8] = jnp.zeros((3, D), F32)
    dz2_out[...] = norm_back(dh2, gain[1:2], xhat2, rstd2)
    for item in stores:
        item.wait()


def feed_call(chunks, pos_a, pos_b, z2, cot, wup, wdown, upb, downb, gain, shift):
    T, D = z2.shape
    FF = wup.shape[1]
    return pl.pallas_call(
        functools.partial(feed_kernel, T, D, FF, chunks),
        out_shape=[
            jax.ShapeDtypeStruct((T, D), BF16),
            jax.ShapeDtypeStruct((T, D), F32),
            jax.ShapeDtypeStruct((chunks, D // chunks, FF), BF16),
            jax.ShapeDtypeStruct((8, FF // 8, D), BF16),
            jax.ShapeDtypeStruct((8, D), F32),
            jax.ShapeDtypeStruct((8, 8, FF // 8), F32),
        ],
        in_specs=[SMEM, SMEM, VMEM, VMEM, ANY, ANY, VMEM, VMEM, VMEM, VMEM],
        out_specs=[VMEM, VMEM, ANY, ANY, VMEM, VMEM],
        scratch_shapes=[
            pltpu.VMEM((D, FF), BF16),
            pltpu.VMEM((FF, D), BF16),
            pltpu.VMEM((D, T), BF16),
            pltpu.VMEM((T, FF), BF16),
            pltpu.VMEM((T, FF), F32),
            pltpu.VMEM((T, D), F32),
            pltpu.VMEM((T, D), BF16),
            pltpu.VMEM((chunks, D // chunks, FF), BF16),
            pltpu.VMEM((8, FF // 8, D), BF16),
            pltpu.SemaphoreType.DMA((4,)),
        ],
        compiler_params=pltpu.CompilerParams(vmem_limit_bytes=48 * MIB),
        cost_estimate=pl.CostEstimate(
            flops=30 * 10**9, bytes_accessed=25 * 10**6, transcendentals=2 * 10**6
        ),
        name="feed",
    )(pos_a, pos_b, z2, cot, wup, wdown, upb, downb, gain, shift)


def backward_kernel(dims, cross, chunks, *refs):
    T, LL, LS, NS, D, n = dims
    refs = list(refs)
    info, pos_a, pos_b = refs.pop(0), refs.pop(0), refs.pop(0)
    blocks = [refs.pop(0) for _ in range(n)]
    w_hbm, wo_hbm, k_hbm, v_hbm = [refs.pop(0) for _ in range(4)]
    dz, q, o, lse_l, lse_s = [refs.pop(0) for _ in range(5)]
    if cross:
        z_in, gain, shift = refs.pop(0), refs.pop(0), refs.pop(0)
    dblk_out, ga_out, gb_out, vec_out = [refs.pop(0) for _ in range(4)]
    dres_out = refs.pop(0) if cross else None
    blk, w, wo, k, v, dk, dv, dq, do, da, blk_t, o_t, dblk, ga, gb, sems = refs
    src, acc = do, dblk
    copies = Copies(sems)
    load_wo = copies.start(wo_hbm, wo)
    load_k, load_v = copies.start(k_hbm, k), copies.start(v_hbm, v)
    load_blk = [copies.start(blocks[r], blk.at[r * T : (r + 1) * T]) for r in range(n)]
    load_w = copies.start(w_hbm, w)
    rows = D // chunks
    tiles = D // 256

    def weight_grad(out, pos, slot, lhs_t, rhs, c):
        grad = dot(lhs_t, rhs).astype(BF16)
        for s in range(chunks):
            out[pos[s], slot * rows : (slot + 1) * rows, c] = grad[s * rows : (s + 1) * rows]

    da[...] = dz[...].astype(BF16)
    vec_out[2:3] = col_sum(da[...])
    transpose_into(o_t, o, T, D)
    load_wo.wait()

    def out_tile(j):
        c = tile(j, 256)
        do[:, c] = dot_t(da[...], wo[c, :]).astype(BF16)
        weight_grad(ga, pos_a, 0, o_t[...], da[:, c], c)

    loop(tiles, out_tile)
    load_k.wait()
    load_v.wait()
    attend_backward(dims, not cross, info, q, k, v, o, do, lse_l, lse_s, dq, dk, dv)
    for item in load_blk:
        item.wait()
    load_w.wait()
    for r in range(n):
        transpose_into(blk_t, blk, T, D, r * T)
    vec_out[0:1] = col_sum(dq[...])
    vec_out[1:2] = col_sum(dv[...])
    if cross:
        xhat, rstd = norm_parts(z_in[...])
        src[...] = (xhat * gain[0:1] + shift[0:1]).astype(BF16)
        transpose_into(o_t, src, T, D)
    else:
        o_t[...] = blk_t[:, 0:T]

    def grad_tile(j):
        c = tile(j, 256)
        weight_grad(ga, pos_a, 1, o_t[...], dq[:, c], c)
        weight_grad(gb, pos_b, 0, blk_t[...], dk[:, c], c)
        weight_grad(gb, pos_b, 1, blk_t[...], dv[:, c], c)

    loop(tiles, grad_tile)
    stores = [copies.start(ga, ga_out), copies.start(gb, gb_out)]

    def dblk_tile(j):
        r, c = tile(j // tiles, T), tile(j % tiles, 256)
        part = dot_t(dk[r, :], w[1, c, :]) + dot_t(dv[r, :], w[2, c, :])
        dblk[r, c] = part.astype(BF16)

    def dq_tile(j):
        c = tile(j, 256)
        part = dz[:, c] + dot_t(dq[...], w[0, c, :])
        if cross:
            dres_out[:, c] = part
        else:
            part = part + dot_t(dk[0:T, :], w[1, c, :]) + dot_t(dv[0:T, :], w[2, c, :])
            dblk[0:T, c] = part.astype(BF16)

    loop(n * tiles, dblk_tile)
    loop(tiles, dq_tile)
    stores.append(copies.start(dblk, dblk_out))
    vec_out[3:8] = jnp.zeros((5, D), F32)
    if cross:
        dh = dres_out[...]
        vec_out[3:4] = col_sum(dh * xhat)
        vec_out[4:5] = col_sum(dh)
        dres_out[...] = norm_back(dh, gain[0:1], xhat, rstd)
    for item in stores:
        item.wait()


def backward_call(dims, cross, chunks, info, pos_a, pos_b, blocks, w, wo, k, v, dz, q, o, lse_l, lse_s, extra):
    T, LL, LS, NS, D, n = dims
    full, own = (n * T, D), (T, D)
    grads = (chunks, 2 * (D // chunks), D)
    out_shape = [
        jax.ShapeDtypeStruct(full, BF16),
        jax.ShapeDtypeStruct(grads, BF16),
        jax.ShapeDtypeStruct(grads, BF16),
        jax.ShapeDtypeStruct((8, D), F32),
    ]
    out_specs = [ANY, ANY, ANY, VMEM]
    if cross:
        out_shape.append(jax.ShapeDtypeStruct(own, F32))
        out_specs.append(VMEM)
    return pl.pallas_call(
        functools.partial(backward_kernel, dims, cross, chunks),
        out_shape=out_shape,
        in_specs=[SMEM] * 3 + [ANY] * n + [ANY] * 4 + [VMEM] * (5 + len(extra)),
        out_specs=out_specs,
        scratch_shapes=[
            pltpu.VMEM(full, BF16),
            pltpu.VMEM((3, D, D), BF16),
            pltpu.VMEM((D, D), BF16),
            pltpu.VMEM(full, BF16),
            pltpu.VMEM(full, BF16),
            pltpu.VMEM(full, BF16),
            pltpu.VMEM(full, BF16),
            pltpu.VMEM(own, BF16),
            pltpu.VMEM(own, BF16),
            pltpu.VMEM(own, BF16),
            pltpu.VMEM((D, n * T), BF16),
            pltpu.VMEM((D, T), BF16),
            pltpu.VMEM(full, BF16),
            pltpu.VMEM(grads, BF16),
            pltpu.VMEM(grads, BF16),
            pltpu.SemaphoreType.DMA((n + 7,)),
        ],
        compiler_params=pltpu.CompilerParams(vmem_limit_bytes=48 * MIB),
        cost_estimate=pl.CostEstimate(
            flops=40 * 10**9, bytes_accessed=25 * 10**6, transcendentals=4 * 10**6
        ),
        name="cross_backward" if cross else "self_backward",
    )(info, pos_a, pos_b, *blocks, w, wo, k, v, dz, q, o, lse_l, lse_s, *extra)


def swap(a, axis, bit, size):
    return lax.ppermute(a, axis, [(i, i ^ bit) for i in range(size)])


def bits_of(size):
    return [1 << i for i in range(size.bit_length() - 1)]


def add_low(a, b):
    return (a.astype(F32) + b.astype(F32)).astype(BF16)


def halve(a, steps):
    for axis, bit, size in steps:
        half = a.shape[0] // 2
        a = add_low(a[:half], swap(a[half:], axis, bit, size))
    return a[0]


def all_sum(a, axis, size):
    rows, cols = a.shape
    me = lax.axis_index(axis)
    steps = bits_of(size)
    sent = []
    for bit in steps:
        mine = (me // bit) % 2
        a = a.reshape(2, a.shape[0] // 2, cols)
        keep = lax.dynamic_index_in_dim(a, mine, 0, keepdims=False)
        give = lax.dynamic_index_in_dim(a, 1 - mine, 0, keepdims=False)
        a = add_low(keep, swap(give, axis, bit, size))
        sent.append(mine)
    for bit, mine in zip(reversed(steps), reversed(sent)):
        other = swap(a, axis, bit, size)
        first = jnp.where(mine == 0, a, other)
        second = jnp.where(mine == 0, other, a)
        a = jnp.concatenate([first, second], axis=0)
    return a.reshape(rows, cols)


def on_device(
    sizes,
    long_rows,
    short_rows,
    long_memory,
    short_memory,
    long_cotangent,
    short_cotangent,
    long_lengths,
    short_lengths,
    self_qkv,
    self_out,
    self_bias,
    cross_qkv,
    cross_out,
    cross_bias,
    norm_gain,
    norm_bias,
    up_proj,
    up_bias,
    down_proj,
    down_bias,
):
    n_dp, n, n_rep = sizes
    count_l, LL, D = long_rows.shape
    NS, LS, _ = short_rows.shape
    FF = up_proj.shape[1]
    T = LL + NS * LS
    dims = (T, LL, LS, NS, D, n)
    shards = n * n_rep

    def flat(a, b):
        return jnp.concatenate([a.reshape(-1, D), b.reshape(-1, D)], axis=0)

    def gather(a):
        blocks = [a]
        for bit in reversed(bits_of(n)):
            got = [swap(b, "seq", bit, n) for b in blocks]
            blocks = blocks + got
        order = [0]
        for bit in reversed(bits_of(n)):
            order = order + [o ^ bit for o in order]
        return [blocks[order.index(r)] for r in range(n)]

    me = lax.axis_index("seq")
    mine = me * n_rep + lax.axis_index("rep")
    info = jnp.concatenate([long_lengths, short_lengths, me[None]]).astype(jnp.int32)

    index = jnp.arange(shards, dtype=jnp.int32) ^ mine
    rel_seq, rel_rep = index // n_rep, index % n_rep
    core, rest = rel_seq % 2, rel_seq // 2
    pos_a = core * (shards // 2) + rest * n_rep + rel_rep
    pos_b = core * (shards // 2) + rel_rep * (n // 2) + rest
    steps_core = [("seq", 1, n)]
    steps_x = [("seq", bit, n) for bit in reversed(bits_of(n)[1:])]
    steps_y = [("rep", bit, n_rep) for bit in reversed(bits_of(n_rep))]
    steps_a = steps_core + steps_x + steps_y
    steps_b = steps_core + steps_y + steps_x

    aligned = shards == 8
    chunks = 8
    table_a, table_b = pos_a, pos_b
    if not aligned:
        table_a = table_b = jnp.arange(chunks, dtype=jnp.int32)

    def ordered(a, pos):
        if aligned:
            return a
        c, r, w = a.shape
        parts = a.reshape(shards, (c * r) // shards, w)
        return jnp.zeros_like(parts).at[pos].set(parts)

    def ordered_two(a, pos):
        if aligned:
            return a
        c, r, w = a.shape
        parts = a.reshape(c, 2, r // 2, w).swapaxes(0, 1).reshape(2, shards, -1, w)
        parts = parts.swapaxes(0, 1).reshape(shards, -1, w)
        return jnp.zeros_like(parts).at[pos].set(parts)

    x = flat(long_rows, short_rows)
    m = flat(long_memory, short_memory)
    cot = flat(long_cotangent, short_cotangent)
    xs = gather(x)
    ms = gather(m)

    q1, k1, v1, o1, lse1l, lse1s, z1 = forward_call(
        dims, False, info, xs, self_qkv, self_out, self_bias, ()
    )
    norm = (norm_gain, norm_bias)
    q2, k2, v2, o2, lse2l, lse2s, z2 = forward_call(
        dims, True, info, ms, cross_qkv, cross_out, cross_bias, (z1,) + norm
    )
    y, dz2, g_up, g_down, vec_f, g_upb = feed_call(
        chunks, table_a, table_b, z2, cot, up_proj, down_proj, up_bias[None], down_bias[None], *norm
    )
    dm, gc_a, gc_b, vec_c, dz1 = backward_call(
        dims, True, chunks, info, table_a, table_b, ms, cross_qkv, cross_out, k2, v2, dz2, q2, o2,
        lse2l, lse2s, (z1,) + norm,
    )
    dx, gs_a, gs_b, vec_s = backward_call(
        dims, False, chunks, info, table_a, table_b, xs, self_qkv, self_out, k1, v1, dz1, q1, o1,
        lse1l, lse1s, (),
    )

    seq_steps = [("seq", 1, n)] + [("seq", bit, n) for bit in bits_of(n)[1:]]

    def rows_reduce(a):
        a = a.reshape(n, T, D)
        a = jnp.stack([a[i] for i in sorted(range(n), key=lambda i: (i % 2, i // 2))])
        return halve(a, seq_steps)

    up_share = all_sum(halve(ordered(g_up, pos_a), steps_a), "dp", n_dp)
    down_share = all_sum(halve(ordered(g_down, pos_b), steps_b), "dp", n_dp)
    ca_share = all_sum(halve(ordered_two(gc_a, pos_a), steps_a), "dp", n_dp)
    cb_share = all_sum(halve(ordered_two(gc_b, pos_b), steps_b), "dp", n_dp)
    dm = rows_reduce(dm)
    dx = rows_reduce(dx)
    sa_share = all_sum(halve(ordered_two(gs_a, pos_a), steps_a), "dp", n_dp)
    sb_share = all_sum(halve(ordered_two(gs_b, pos_b), steps_b), "dp", n_dp)

    small = jnp.concatenate(
        [
            vec_s[0:3], vec_c[0:3], vec_c[3:4], vec_f[3:4], vec_f[0:1], vec_c[4:5], vec_f[4:5],
            vec_f[1:2], vec_f[2:3], g_upb[:, 0, :].reshape(-1, D),
        ]
    )
    small = lax.psum(small, ("dp", "seq", "rep"))

    def part(a, width):
        return lax.dynamic_slice_in_dim(a, mine * width, width, axis=-1)

    width = D // shards
    rows = D // shards
    vecs = part(small[0:13], width)
    upb_grad = part(small[13:].reshape(-1), FF // shards)

    def unflat(a):
        return (
            a[:LL].reshape(count_l, LL, D),
            a[LL:].reshape(NS, LS, D),
        )

    y_l, y_s = unflat(y)
    dx_l, dx_s = unflat(dx)
    dm_l, dm_s = unflat(dm)

    def wide(a):
        return a.astype(F32)

    self_qkv_grad = wide(jnp.stack([sa_share[rows:], sb_share[:rows], sb_share[rows:]]))
    cross_qkv_grad = wide(jnp.stack([ca_share[rows:], cb_share[:rows], cb_share[rows:]]))
    return (
        y_l,
        y_s,
        dx_l,
        dx_s,
        dm_l,
        dm_s,
        self_qkv_grad,
        wide(sa_share[:rows]),
        vecs[0:3],
        cross_qkv_grad,
        wide(ca_share[:rows]),
        vecs[3:6],
        vecs[6:9],
        vecs[9:12],
        wide(up_share),
        upb_grad,
        wide(down_share),
        vecs[12],
    )


def solution(mesh):
    rows = P(("dp", "rep"), "seq", None)
    lengths = P(("dp", "rep"))
    share = ("seq", "rep")
    in_specs = (rows,) * 6 + (lengths,) * 2 + (P(),) * 12
    out_specs = (rows,) * 6 + (
        P(None, share, None),
        P(share, None),
        P(None, share),
        P(None, share, None),
        P(share, None),
        P(None, share),
        P(None, share),
        P(None, share),
        P(share, None),
        P(share),
        P(share, None),
        P(share),
    )
    sizes = (mesh.shape["dp"], mesh.shape["seq"], mesh.shape["rep"])
    return jax.shard_map(
        functools.partial(on_device, sizes),
        mesh=mesh,
        in_specs=in_specs,
        out_specs=out_specs,
        check_vma=False,
    )
```

```python
import functools

import jax
import jax.numpy as jnp
from jax import lax
from jax.experimental import pallas as pl
from jax.experimental.pallas import tpu as pltpu
from jax.sharding import PartitionSpec as P

HD = 64
PAIR = 2 * HD
F32 = jnp.float32
BF16 = jnp.bfloat16
NEG = -1000000000.0
MIB = 1024 * 1024
VEC_ROWS = 24

ANY = pl.BlockSpec(memory_space=pl.ANY)
VMEM = pl.BlockSpec(memory_space=pltpu.VMEM)
SMEM = pl.BlockSpec(memory_space=pltpu.SMEM)


def dot(a, b):
    return jnp.dot(a, b, preferred_element_type=F32)


def dot_t(a, b):
    return lax.dot_general(a, b, (((1,), (1,)), ((), ())), preferred_element_type=F32)


def loop(count, body, first=0):
    lax.fori_loop(first, count, lambda i, c: (body(i), c)[1], 0)


def tile(j, width):
    return pl.ds(pl.multiple_of(j * width, width), width)


def norm_parts(z):
    center = z - jnp.mean(z, axis=-1, keepdims=True)
    rstd = lax.rsqrt(jnp.mean(center * center, axis=-1, keepdims=True) + 1e-05)
    return center * rstd, rstd


def norm_back(dy, gain, xhat, rstd):
    dyg = dy * gain
    mean_a = jnp.mean(dyg, axis=-1, keepdims=True)
    mean_b = jnp.mean(dyg * xhat, axis=-1, keepdims=True)
    return rstd * (dyg - mean_a - xhat * mean_b)


def col_sum(a):
    return jnp.sum(a.astype(F32), axis=0, keepdims=True)


def transpose_into(dst_ref, src_ref, rows, cols, row_off=0):
    def body(j):
        dst_ref[tile(j, 128), row_off : row_off + rows] = src_ref[
            row_off : row_off + rows, tile(j, 128)
        ].T

    loop(cols // 128, body)


class Copies:
    def __init__(self, sems):
        self.sems, self.used = sems, 0

    def start(self, src, dst):
        copy = pltpu.make_async_copy(src, dst, self.sems.at[self.used])
        self.used += 1
        copy.start()
        return copy


def head_masks(dtype):
    lane = lax.broadcasted_iota(jnp.int32, (1, PAIR), 1)
    low = (lane < HD).astype(F32)
    return low.astype(dtype), (1.0 - low).astype(dtype)


def stack_heads(a, masks):
    return jnp.concatenate([a * masks[0], a * masks[1]], axis=0)


def unstack_heads(out_t, width):
    sub = lax.broadcasted_iota(jnp.int32, (PAIR, width), 0)
    return jnp.where(sub < HD, out_t[:, :width], out_t[:, width:]).T


def key_positions(block, keys, queries, size, me):
    row = lax.broadcasted_iota(jnp.int32, (keys, queries), 0)
    if keys == size:
        return row + (block ^ me) * size
    return ((row // size) ^ me) * size + row % size


def limits(queries, size, me, length, causal):
    if not causal:
        return length - 1
    lane = lax.broadcasted_iota(jnp.int32, (1, queries), 1) % size
    return jnp.minimum(lane + me * size, length - 1)


def attend_forward(dims, causal, info, q_ref, k_ref, v_ref, o_ref, lse_l, lse_s, s_scr):
    T, LL, LS, NS, D, n = dims
    me = info[NS + 1]
    masks = head_masks(BF16)

    def pair(p):
        c = tile(p, PAIR)
        q2 = stack_heads(q_ref[0:LL, c], masks)
        lim = limits(2 * LL, LL, me, info[0], causal)
        top = None
        for r in range(n):
            s = dot_t(k_ref[r * T : r * T + LL, c], q2)
            s = jnp.where(key_positions(r, LL, 2 * LL, LL, me) <= lim, s, NEG)
            s_scr[r * LL : (r + 1) * LL, :] = s
            m = jnp.max(s, axis=0, keepdims=True)
            top = m if top is None else jnp.maximum(top, m)
        total, acc = None, None
        for r in range(n):
            w = jnp.exp(s_scr[r * LL : (r + 1) * LL, :] - top)
            t = jnp.sum(w, axis=0, keepdims=True)
            a = dot(v_ref[r * T : r * T + LL, c].T, w.astype(BF16))
            total = t if total is None else total + t
            acc = a if acc is None else acc + a
        acc = acc * (1.0 / total)
        o_ref[0:LL, c] = unstack_heads(acc, LL).astype(BF16)
        lse_l[p] = jnp.broadcast_to(top + jnp.log(total), (8, 2 * LL))
        for i in range(NS):
            off = LL + i * LS
            q2 = stack_heads(q_ref[off : off + LS, c], masks)
            kb = jnp.concatenate([k_ref[r * T + off : r * T + off + LS, c] for r in range(n)], 0)
            vb = jnp.concatenate([v_ref[r * T + off : r * T + off + LS, c] for r in range(n)], 0)
            s = dot_t(kb, q2)
            lim = limits(2 * LS, LS, me, info[1 + i], causal)
            s = jnp.where(key_positions(0, n * LS, 2 * LS, LS, me) <= lim, s, NEG)
            top = jnp.max(s, axis=0, keepdims=True)
            w = jnp.exp(s - top)
            total = jnp.sum(w, axis=0, keepdims=True)
            acc = dot(vb.T, w.astype(BF16)) * (1.0 / total)
            o_ref[off : off + LS, c] = unstack_heads(acc, LS).astype(BF16)
            lse_s[p * NS + i] = jnp.broadcast_to(top + jnp.log(total), (8, 2 * LS))

    loop(D // PAIR, pair)


def attend_backward(
    dims,
    causal,
    info,
    q_ref,
    k_ref,
    v_ref,
    o_ref,
    do_ref,
    lse_l,
    lse_s,
    dq_ref,
    dk_ref,
    dv_ref,
    first,
    last,
):
    T, LL, LS, NS, D, n = dims
    me = info[NS + 1]
    masks = head_masks(BF16)
    ones = jnp.ones((8, PAIR), F32)

    def row_dots(do2, o):
        prod = do2.astype(F32) * jnp.concatenate([o, o], 0).astype(F32)
        full = lax.dot_general(
            ones,
            prod,
            (((1,), (1,)), ((), ())),
            precision=lax.Precision.HIGHEST,
            preferred_element_type=F32,
        )
        return full[0:1]

    def pair(p):
        c = tile(p, PAIR)
        q2 = stack_heads(q_ref[0:LL, c], masks)
        do2 = stack_heads(do_ref[0:LL, c], masks)
        delta = row_dots(do2, o_ref[0:LL, c])
        lse = lse_l[p][0:1]
        lim = limits(2 * LL, LL, me, info[0], causal)
        dq_t = None
        for r in range(n):
            rows = slice(r * T, r * T + LL)
            kb, vb = k_ref[rows, c], v_ref[rows, c]
            s = dot_t(kb, q2)
            s = jnp.where(key_positions(r, LL, 2 * LL, LL, me) <= lim, s, NEG)
            probs = jnp.exp(s - lse)
            ds = (probs * (dot_t(vb, do2) - delta)).astype(BF16)
            dv_ref[rows, c] = dot(probs.astype(BF16), do2).astype(BF16)
            dk_ref[rows, c] = dot(ds, q2).astype(BF16)
            part = dot(kb.T, ds)
            dq_t = part if dq_t is None else dq_t + part
        dq_ref[0:LL, c] = (unstack_heads(dq_t, LL) * HD**-0.5).astype(BF16)
        for i in range(NS):
            off = LL + i * LS
            q2 = stack_heads(q_ref[off : off + LS, c], masks)
            do2 = stack_heads(do_ref[off : off + LS, c], masks)
            delta = row_dots(do2, o_ref[off : off + LS, c])
            lse = lse_s[p * NS + i][0:1]
            kb = jnp.concatenate([k_ref[r * T + off : r * T + off + LS, c] for r in range(n)], 0)
            vb = jnp.concatenate([v_ref[r * T + off : r * T + off + LS, c] for r in range(n)], 0)
            s = dot_t(kb, q2)
            lim = limits(2 * LS, LS, me, info[1 + i], causal)
            s = jnp.where(key_positions(0, n * LS, 2 * LS, LS, me) <= lim, s, NEG)
            probs = jnp.exp(s - lse)
            ds = (probs * (dot_t(vb, do2) - delta)).astype(BF16)
            dv = dot(probs.astype(BF16), do2).astype(BF16)
            dk = dot(ds, q2).astype(BF16)
            for r in range(n):
                dv_ref[r * T + off : r * T + off + LS, c] = dv[r * LS : (r + 1) * LS]
                dk_ref[r * T + off : r * T + off + LS, c] = dk[r * LS : (r + 1) * LS]
            dq_ref[off : off + LS, c] = (unstack_heads(dot(kb.T, ds), LS) * HD**-0.5).astype(BF16)

    loop(last, pair, first)


def forward_kernel(dims, cross, *refs):
    T, LL, LS, NS, D, n = dims
    refs = list(refs)
    info = refs.pop(0)
    blocks = [refs.pop(0) for _ in range(n)]
    w_hbm, wo_hbm, bias = refs.pop(0), refs.pop(0), refs.pop(0)
    if cross:
        z_in, gain, shift = refs.pop(0), refs.pop(0), refs.pop(0)
    q_out, k_out, v_out, o_out, lse_l, lse_s, z_out, t_out = [refs.pop(0) for _ in range(8)]
    blk, w, wo, k, v, blk_t, s_scr, sems = refs
    copies = Copies(sems)
    loads = [copies.start(w_hbm.at[0], w.at[0])]
    loads += [copies.start(blocks[r], blk.at[r * T : (r + 1) * T]) for r in range(n)]
    loads += [copies.start(w_hbm.at[i], w.at[i]) for i in (1, 2)]
    loads.append(copies.start(wo_hbm, wo))
    if cross:
        xhat, _ = norm_parts(z_in[...])
        z_out[...] = xhat * gain[0:1] + shift[0:1]
        source = z_out
    else:
        loads[1].wait()
        source = blk
    loads[0].wait()

    def q_tile(j):
        c = tile(j, 256)
        q = dot(source[0:T, :].astype(BF16), w[0, :, c]) + bias[0:1, c]
        q_out[:, c] = (q.astype(BF16).astype(F32) * HD**-0.5).astype(BF16)

    loop(D // 256, q_tile)
    for item in loads[1 if cross else 2 : n + 3]:
        item.wait()

    def kv_tile(j):
        r, c = tile(j // (D // 256), T), tile(j % (D // 256), 256)
        x = blk[r, :]
        k[r, c] = dot(x, w[1, :, c]).astype(BF16)
        v[r, c] = (dot(x, w[2, :, c]) + bias[1:2, c]).astype(BF16)

    loop(n * (D // 256), kv_tile)
    stores = [copies.start(k, k_out), copies.start(v, v_out)]
    for r in range(n):
        transpose_into(blk_t, blk, T, D, r * T)
    stores.append(copies.start(blk_t, t_out))
    attend_forward(dims, not cross, info, q_out, k, v, o_out, lse_l, lse_s, s_scr)
    loads[n + 3].wait()

    def z_tile(j):
        c = tile(j, 256)
        z_out[:, c] = source[0:T, c].astype(F32) + dot(o_out[...], wo[:, c]) + bias[2:3, c]

    loop(D // 256, z_tile)
    for item in stores:
        item.wait()


def forward_call(dims, cross, info, blocks, w, wo, bias, extra):
    T, LL, LS, NS, D, n = dims
    pairs = D // PAIR
    extra_specs = [VMEM] * len(extra)
    return pl.pallas_call(
        functools.partial(forward_kernel, dims, cross),
        out_shape=[
            jax.ShapeDtypeStruct((T, D), BF16),
            jax.ShapeDtypeStruct((n * T, D), BF16),
            jax.ShapeDtypeStruct((n * T, D), BF16),
            jax.ShapeDtypeStruct((T, D), BF16),
            jax.ShapeDtypeStruct((pairs, 8, 2 * LL), F32),
            jax.ShapeDtypeStruct((pairs * NS, 8, 2 * LS), F32),
            jax.ShapeDtypeStruct((T, D), F32),
            jax.ShapeDtypeStruct((D, n * T), BF16),
        ],
        in_specs=[SMEM] + [ANY] * n + [ANY, ANY, VMEM] + extra_specs,
        out_specs=[VMEM, ANY, ANY, VMEM, VMEM, VMEM, VMEM, ANY],
        scratch_shapes=[
            pltpu.VMEM((n * T, D), BF16),
            pltpu.VMEM((3, D, D), BF16),
            pltpu.VMEM((D, D), BF16),
            pltpu.VMEM((n * T, D), BF16),
            pltpu.VMEM((n * T, D), BF16),
            pltpu.VMEM((D, n * T), BF16),
            pltpu.VMEM((n * LL, 2 * LL), F32),
            pltpu.SemaphoreType.DMA((n + 7,)),
        ],
        compiler_params=pltpu.CompilerParams(vmem_limit_bytes=40 * MIB),
        cost_estimate=pl.CostEstimate(
            flops=20 * 10**9, bytes_accessed=20 * 10**6, transcendentals=4 * 10**6
        ),
        name="cross_forward" if cross else "self_forward",
    )(info, *blocks, w, wo, bias, *extra)


def feed_kernel(T, D, FF, chunks, *refs):
    (
        pos_a, pos_b, z2, cot, wup_hbm, wdown_hbm, upb, downb, gain, shift,
        y_out, dz2_out, gup_out, gdown_out, vec_out,
        wup, wdown, h2t, g, gp, acc, dfs, gup, gdown, sems,
    ) = refs
    copies = Copies(sems)
    load_up = copies.start(wup_hbm, wup)
    load_down = copies.start(wdown_hbm, wdown)
    tile_f = FF // 8
    rows = D // chunks
    per_row = D // tile_f
    vec_out[...] = jnp.zeros(vec_out.shape, F32)
    xhat2, rstd2 = norm_parts(z2[...])
    h2 = xhat2 * gain[1:2] + shift[1:2]
    h2b = h2.astype(BF16)
    dfs[...] = h2b
    acc[...] = h2 + downb[...]
    transpose_into(h2t, dfs, T, D)
    load_up.wait()
    load_down.wait()

    def up_tile(j):
        c = tile(j, tile_f)
        u = dot(dfs[...], wup[:, c]) + upb[:, c]
        sq = u * u
        th = jnp.tanh(0.7978845608028654 * u * (1.0 + 0.044715 * sq))
        half = 0.5 * (1.0 + th)
        act = (u * half).astype(BF16)
        g[:, c] = act
        gp[:, c] = half + (0.5 * 0.7978845608028654) * u * (1.0 - th * th) * (
            1.0 + (3.0 * 0.044715) * sq
        )
        acc[...] += dot(act, wdown[c, :])

    loop(8, up_tile)
    xhat3, rstd3 = norm_parts(acc[...])
    y_out[...] = (xhat3 * gain[2:3] + shift[2:3]).astype(BF16)
    dy = cot[...].astype(F32)
    vec_out[8:9] = col_sum(dy * xhat3)
    vec_out[11:12] = col_sum(dy)
    dz3 = norm_back(dy, gain[2:3], xhat3, rstd3)
    df = dz3.astype(BF16)
    dfs[...] = df
    acc[...] = dz3
    vec_out[12:13] = col_sum(df)

    def back_tile(j):
        c = tile(j, tile_f)
        dg = dot_t(dfs[...], wdown[c, :])
        du = (gp[:, c] * dg).astype(BF16)
        vec_out[pl.ds(13 + j // per_row, 1), tile(j % per_row, tile_f)] = col_sum(du)
        acc[...] += dot_t(du, wup[:, c])
        grad = dot(h2t[...], du).astype(BF16)
        block = pl.ds(pl.multiple_of((j // per_row) * rows, rows), rows)
        for s in range(chunks):
            gup[pos_a[s], block, tile(j % per_row, tile_f)] = grad[s * rows : (s + 1) * rows]
        gdown[pos_b[j]] = dot(g[:, c].T, dfs[...]).astype(BF16)

    loop(8, back_tile)
    stores = [copies.start(gup, gup_out), copies.start(gdown, gdown_out)]
    dh2 = acc[...]
    xhat2, rstd2 = norm_parts(z2[...])
    vec_out[7:8] = col_sum(dh2 * xhat2)
    vec_out[10:11] = col_sum(dh2)
    dz2_out[...] = norm_back(dh2, gain[1:2], xhat2, rstd2)
    for item in stores:
        item.wait()


def feed_call(chunks, pos_a, pos_b, z2, cot, wup, wdown, upb, downb, gain, shift):
    T, D = z2.shape
    FF = wup.shape[1]
    return pl.pallas_call(
        functools.partial(feed_kernel, T, D, FF, chunks),
        out_shape=[
            jax.ShapeDtypeStruct((T, D), BF16),
            jax.ShapeDtypeStruct((T, D), F32),
            jax.ShapeDtypeStruct((chunks, FF // chunks, D), BF16),
            jax.ShapeDtypeStruct((8, FF // 8, D), BF16),
            jax.ShapeDtypeStruct((VEC_ROWS, D), F32),
        ],
        in_specs=[SMEM, SMEM, VMEM, VMEM, ANY, ANY, VMEM, VMEM, VMEM, VMEM],
        out_specs=[VMEM, VMEM, ANY, ANY, VMEM],
        scratch_shapes=[
            pltpu.VMEM((D, FF), BF16),
            pltpu.VMEM((FF, D), BF16),
            pltpu.VMEM((D, T), BF16),
            pltpu.VMEM((T, FF), BF16),
            pltpu.VMEM((T, FF), F32),
            pltpu.VMEM((T, D), F32),
            pltpu.VMEM((T, D), BF16),
            pltpu.VMEM((chunks, FF // chunks, D), BF16),
            pltpu.VMEM((8, FF // 8, D), BF16),
            pltpu.SemaphoreType.DMA((4,)),
        ],
        compiler_params=pltpu.CompilerParams(vmem_limit_bytes=48 * MIB),
        cost_estimate=pl.CostEstimate(
            flops=30 * 10**9, bytes_accessed=25 * 10**6, transcendentals=2 * 10**6
        ),
        name="feed",
    )(pos_a, pos_b, z2, cot, wup, wdown, upb, downb, gain, shift)


def backward_phase(dims, cross, chunks, info, loads, hbm, data, scratch, vec, order, point, dms):
    T, LL, LS, NS, D, n = dims
    dz, z_in, gain, shift, lse_l, lse_s = data
    q, o, w, wo, k, v, dk, dv, dq, do, da, blk_t, o_t, dblk, ga, gb = scratch
    pos_a, pos_b = order
    load_wo, load_o, load_q, load_k, load_v, load_t, load_w = loads
    rows = D // chunks
    tiles = D // 256
    base = 3 if cross else 0

    def weight_grad(out, pos, slot, lhs_t, rhs, c):
        grad = dot(lhs_t, rhs).astype(BF16)
        for s in range(chunks):
            out[pos[s], slot * rows : (slot + 1) * rows, c] = grad[s * rows : (s + 1) * rows]

    da[...] = dz[...].astype(BF16)
    vec[base + 2 : base + 3] = col_sum(da[...])
    load_o.wait()
    transpose_into(o_t, o, T, D)
    load_wo.wait()

    def out_tile(j):
        c = tile(j, 256)
        do[:, c] = dot_t(da[...], wo[c, :]).astype(BF16)
        weight_grad(ga, pos_a, 0, o_t[...], da[:, c], c)

    loop(tiles, out_tile)
    point(0)
    for item in (load_q, load_k, load_v):
        item.wait()
    for i in range(3):
        attend_backward(
            dims, not cross, info, q, k, v, o, do, lse_l, lse_s, dq, dk, dv, 2 * i, 2 * i + 2
        )
        point(i + 1)
    load_t.wait()
    load_w.wait()
    vec[base : base + 1] = col_sum(dq[...])
    vec[base + 1 : base + 2] = col_sum(dv[...])
    if cross:
        xhat, rstd = norm_parts(z_in[...])
        do[...] = (xhat * gain[0:1] + shift[0:1]).astype(BF16)
        transpose_into(o_t, do, T, D)
    else:
        o_t[...] = blk_t[:, 0:T]

    def grad_tile(j):
        c = tile(j, 256)
        weight_grad(ga, pos_a, 1, o_t[...], dq[:, c], c)
        weight_grad(gb, pos_b, 0, blk_t[...], dk[:, c], c)
        weight_grad(gb, pos_b, 1, blk_t[...], dv[:, c], c)

    loop(tiles, grad_tile)
    point(4)

    def dblk_tile(i, j):
        c = tile(j, 256)
        rows_in = slice(i * T, (i + 1) * T)
        part = dot_t(dk[rows_in, :], w[1, c, :]) + dot_t(dv[rows_in, :], w[2, c, :])
        if i == 0:
            part_q = dz[:, c] + dot_t(dq[...], w[0, c, :])
            if cross:
                dz[:, c] = part_q
            else:
                part = part + part_q
        at = dms.index(i)
        dblk[at * T : (at + 1) * T, c] = part.astype(BF16)

    for i in reversed(dms):
        loop(tiles, functools.partial(dblk_tile, i))
    point(5)
    if cross:
        dh = dz[...]
        vec[6:7] = col_sum(dh * xhat)
        vec[9:10] = col_sum(dh)
        dz[...] = norm_back(dh, gain[0:1], xhat, rstd)


def flip(index, bit):
    return index + bit - 2 * bit * ((index // bit) % 2)


class Link:
    def __init__(self, send_sems, recv_sems):
        self.send_sems, self.recv_sems, self.used = send_sems, recv_sems, 0

    def start(self, src, dst, axis, bit):
        copy = pltpu.make_async_remote_copy(
            src_ref=src,
            dst_ref=dst,
            send_sem=self.send_sems.at[self.used],
            recv_sem=self.recv_sems.at[self.used],
            device_id={axis: flip(lax.axis_index(axis), bit)},
            device_id_type=pl.DeviceIdType.MESH,
        )
        self.used += 1
        copy.start()
        return copy


def add_rows(dst, dst_at, a, a_at, b, b_at, count, step=96):
    def body(i):
        def at(start):
            return pl.ds(pl.multiple_of(start + i * step, 16), step)

        total = a[at(a_at), :].astype(F32) + b[at(b_at), :].astype(F32)
        dst[at(dst_at), :] = total.astype(dst.dtype)

    loop(count // step, body)


class Share:
    def __init__(self, link, theirs, acc, recv, res, size, path, dp_bits):
        self.link, self.theirs, self.acc, self.recv, self.res = link, theirs, acc, recv, res
        self.size, self.path, self.dp_bits = size, path, dp_bits
        self.stage, self.copy, self.at = 0, None, 0
        self.off, self.count = 0, size
        self.kept = []

    def advance(self):
        stage, path, dp_bits = self.stage, self.path, self.dp_bits
        self.stage += 1
        halves = len(path)
        if stage == 0:
            rows = self.size << (halves - 1)
            self.land, self.rows = self.at, rows
            self.at += rows
            land = self.recv.at[0:rows]
            if len(self.theirs.shape) == 3:
                land = land.reshape(self.theirs.shape)
            self.copy = self.link.start(self.theirs, land, *path[0])
            return
        self.copy.wait()
        if stage <= halves + len(dp_bits):
            last = stage == halves + len(dp_bits)
            dst = self.res if last else self.acc
            add_rows(dst, self.off, self.acc, self.off, self.recv, self.land, self.rows, 48)
        if stage < halves:
            rows = self.size << (halves - 1 - stage)
            self.land, self.rows = self.at, rows
            self.at += rows
            src = self.acc.at[rows : 2 * rows]
            dst = self.recv.at[self.land : self.land + rows]
            self.copy = self.link.start(src, dst, *path[stage])
        elif stage < halves + len(dp_bits):
            bit = dp_bits[stage - halves]
            mine = (lax.axis_index("dp") // bit) % 2
            self.count //= 2
            give = self.off + (1 - mine) * self.count
            self.off = self.off + mine * self.count
            self.kept.append((self.off, self.count, bit))
            self.land, self.rows = self.at, self.count
            self.at += self.count
            src = self.acc.at[pl.ds(pl.multiple_of(give, 16), self.count)]
            dst = self.recv.at[self.land : self.land + self.count]
            self.copy = self.link.start(src, dst, "dp", bit)
        elif self.kept:
            off, count, bit = self.kept.pop()
            part = self.res.at[pl.ds(pl.multiple_of(off, 16), count)]
            self.copy = self.link.start(part, part, "dp", bit)

    def finish(self):
        while self.kept:
            self.advance()
        self.copy.wait()


class Rows:
    def __init__(self, link, copies, blocks, recv, out, size, path):
        self.link, self.copies, self.blocks, self.recv, self.out = link, copies, blocks, recv, out
        self.size, self.path, self.stage, self.at = size, path, 0, 0

    def advance(self):
        stage, path = self.stage, self.path
        self.stage += 1
        if stage > 0:
            self.copy.wait()
            add_rows(self.blocks, 0, self.blocks, 0, self.recv, self.land, self.rows)
        if stage == len(path):
            self.store = self.copies.start(self.blocks.at[0 : self.rows], self.out)
        if stage < len(path):
            rows = self.size << (len(path) - 1 - stage)
            self.land, self.rows = self.at, rows
            self.at += rows
            src = self.blocks.at[rows : 2 * rows]
            dst = self.recv.at[self.land : self.land + rows]
            self.copy = self.link.start(src, dst, *path[stage])


class Small:
    def __init__(self, link, vec, recv, path):
        self.link, self.vec, self.recv, self.path, self.stage = link, vec, recv, path, 0

    def advance(self):
        stage, path = self.stage, self.path
        self.stage += 1
        if stage > 0:
            self.copy.wait()
            self.vec[stage] = self.vec[stage - 1] + self.recv[stage - 1]
        if stage < len(path):
            self.copy = self.link.start(self.vec.at[stage], self.recv.at[stage], *path[stage])


PATH_A = (("seq", 1), ("seq", 2), ("rep", 1))
PATH_B = (("seq", 1), ("rep", 1), ("seq", 2))
PATH_ROWS = (("seq", 1), ("seq", 2))
DP_BITS = (1, 2)
PATH_ALL = PATH_A + (("dp", 1), ("dp", 2))


def xor_orders(chunks):
    seq, rep = lax.axis_index("seq"), lax.axis_index("rep")
    pos_a, pos_b = [], []
    for s in range(chunks):
        x = (s // 4 + seq // 2) % 2
        core = (s // 2 + seq) % 2
        y = (s + rep) % 2
        pos_a.append(core * 4 + x * 2 + y)
        pos_b.append(core * 4 + y * 2 + x)
    return pos_a, pos_b


def backward_kernel(dims, chunks, linked, *refs):
    T, LL, LS, NS, D, n = dims
    refs = list(refs)

    def take(count):
        out = refs[:count]
        del refs[:count]
        return out

    info, dz2_hbm = take(2)
    cross_hbm, self_hbm = take(7), take(7)
    gup, gdown = take(2)
    z1, gain, shift, lse2l, lse2s, lse1l, lse1s, vec_in = take(8)
    if linked:
        shares_out, dm_out, dx_out, vec_out = take(4)
    else:
        gc_out, gs_out, dm_out, dx_out, vec_out = take(5)
    q, o, w, wo, k, v, dk, dv, dq, do, da, blk_t, o_t, dblk, dres = take(15)
    gc, gs, vec, sems = take(4)
    if linked:
        accs, recvs, res, vec_recv, send_sems, recv_sems = take(6)

    copies = Copies(sems)
    load_dz = copies.start(dz2_hbm, dres)

    def load(hbm):
        w_hbm, wo_hbm, k_hbm, v_hbm, q_hbm, o_hbm, t_hbm = hbm
        pairs = ((wo_hbm, wo), (o_hbm, o), (q_hbm, q), (k_hbm, k), (v_hbm, v), (t_hbm, blk_t), (w_hbm, w))
        return [copies.start(src, dst) for src, dst in pairs]

    vec[0] = vec_in[...]
    tasks = {}
    if linked:
        half = chunks // 2
        size = 2 * (D // chunks)
        barrier = pltpu.get_barrier_semaphore()
        for axis, bit in PATH_ALL:
            pl.semaphore_signal(
                barrier,
                inc=1,
                device_id={axis: flip(lax.axis_index(axis), bit)},
                device_id_type=pl.DeviceIdType.MESH,
            )
        pl.semaphore_wait(barrier, len(PATH_ALL))
        link = Link(send_sems, recv_sems)
        own = []
        for i in range(4):
            grad = gup if i < 2 else gdown
            rows = slice((i % 2) * size, (i % 2 + 1) * size)
            path = PATH_B if i >= 2 else PATH_A
            own.append([copies.start(grad.at[c, rows], accs.at[i, c * size : (c + 1) * size]) for c in range(half)])
            tasks[i] = Share(link, grad.at[half:, rows], accs.at[i], recvs.at[i], res.at[i], size, path, DP_BITS)
        order = xor_orders(chunks)

        def grad_tasks(g, first):
            for i in range(2):
                path = PATH_B if i else PATH_A
                slot = first if first < 6 else 0
                tasks[first + i] = Share(
                    link, g.at[i, half * size :], g.at[i], recvs.at[slot + i], res.at[first + i],
                    size, path, DP_BITS,
                )

        grad_tasks(gc, 4)
        grad_tasks(gs, 6)
        tasks["dm"] = Rows(link, copies, dblk, recvs.at[2], dm_out, T, PATH_ROWS)
        tasks["dx"] = Rows(link, copies, dblk, recvs.at[2], dx_out, T, PATH_ROWS)
        tasks["vec"] = Small(link, vec, vec_recv, PATH_ALL)
    else:
        static = list(range(chunks))
        order = (static, static)

    loads_c = load(cross_hbm)
    if linked:
        for i in range(4):
            tasks[i].advance()
        for group in own:
            for item in group:
                item.wait()

    plan = {
        ("c", 0): (0, 2),
        ("c", 1): (),
        ("c", 2): (0, 2, 1, 3),
        ("c", 3): (),
        ("c", 4): (0, 2, 4, 5),
        ("c", 5): (1, 3, 0, 2, 4, 5, "dm"),
        ("c", 6): (0, 2, "dm"),
        ("s", 0): (1, 3, 0, 2),
        ("s", 1): (1, 3),
        ("s", 2): (1, 3, 4, 5),
        ("s", 3): (4, 5, 1, 3),
        ("s", 4): (4, 5, 6, 7, "vec"),
        ("s", 5): (6, 7, 4, 5, "dx", "vec"),
        ("s", 6): (6, 7, "dx", 4, 5, "vec", "vec", 6, 7, "vec", 6, 7, "vec", 6, 7, "dx", 6, 7),
    }

    def point(phase, i):
        if linked:
            for name in plan[phase, i]:
                tasks[name].advance()

    def chunked(g):
        return [g.at[i].reshape(chunks, 2 * (D // chunks), D) for i in range(2)]

    dms = sorted(range(n), key=lambda r: (r % 2, r // 2))
    scratch = [q, o, w, wo, k, v, dk, dv, dq, do, da, blk_t, o_t, dblk]
    load_dz.wait()
    backward_phase(
        dims, True, chunks, info, loads_c, None, (dres, z1, gain, shift, lse2l, lse2s),
        scratch + chunked(gc), vec.at[0], order, functools.partial(point, "c"), dms,
    )
    loads_s = load(self_hbm)
    point("c", 6)
    if not linked:
        stores = [copies.start(gc, gc_out)]
        done = copies.start(dblk, dm_out)
        done.wait()

    def self_point(i):
        if linked and i == 4:
            tasks["dm"].advance()
            tasks["dm"].store.wait()
        point("s", i)

    backward_phase(
        dims, False, chunks, info, loads_s, None, (dres, None, None, None, lse1l, lse1s),
        scratch + chunked(gs), vec.at[0], order, self_point, dms,
    )
    if linked:
        point("s", 6)
        for i in range(8):
            tasks[i].finish()
        copies.start(res, shares_out).wait()
        tasks["dx"].store.wait()
        vec_out[...] = vec[len(PATH_ALL)]
    else:
        vec_out[...] = vec[0]
        stores += [copies.start(gs, gs_out), copies.start(dblk, dx_out)]
        for item in stores:
            item.wait()


def backward_call(dims, chunks, linked, info, dz2, cross_hbm, self_hbm, gup, gdown, small):
    T, LL, LS, NS, D, n = dims
    full, own = (n * T, D), (T, D)
    size = 2 * (D // chunks)
    grads = (2, chunks * size, D)
    vec = jax.ShapeDtypeStruct((VEC_ROWS, D), F32)
    steps = len(PATH_ALL)
    if linked:
        out_shape = [
            jax.ShapeDtypeStruct((8, size, D), BF16),
            jax.ShapeDtypeStruct(own, BF16),
            jax.ShapeDtypeStruct(own, BF16),
            vec,
        ]
        out_specs = [ANY, ANY, ANY, VMEM]
        landing = 7 * size + 3 * size // 4
        extra = [
            pltpu.VMEM((4, chunks // 2 * size, D), BF16),
            pltpu.VMEM((6, landing, D), BF16),
            pltpu.VMEM((8, size, D), BF16),
            pltpu.VMEM((steps, VEC_ROWS, D), F32),
            pltpu.SemaphoreType.DMA((8 * 7 + 4 + steps,)),
            pltpu.SemaphoreType.DMA((8 * 7 + 4 + steps,)),
        ]
    else:
        out_shape = [
            jax.ShapeDtypeStruct(grads, BF16),
            jax.ShapeDtypeStruct(grads, BF16),
            jax.ShapeDtypeStruct(full, BF16),
            jax.ShapeDtypeStruct(full, BF16),
            vec,
        ]
        out_specs = [ANY, ANY, ANY, ANY, VMEM]
        extra = []
    params = {"collective_id": 0} if linked else {}
    return pl.pallas_call(
        functools.partial(backward_kernel, dims, chunks, linked),
        out_shape=out_shape,
        in_specs=[SMEM] + [ANY] * 17 + [VMEM] * 8,
        out_specs=out_specs,
        scratch_shapes=[
            pltpu.VMEM(own, BF16),
            pltpu.VMEM(own, BF16),
            pltpu.VMEM((3, D, D), BF16),
            pltpu.VMEM((D, D), BF16),
            pltpu.VMEM(full, BF16),
            pltpu.VMEM(full, BF16),
            pltpu.VMEM(full, BF16),
            pltpu.VMEM(full, BF16),
            pltpu.VMEM(own, BF16),
            pltpu.VMEM(own, BF16),
            pltpu.VMEM(own, BF16),
            pltpu.VMEM((D, n * T), BF16),
            pltpu.VMEM((D, T), BF16),
            pltpu.VMEM(full, BF16),
            pltpu.VMEM(own, F32),
            pltpu.VMEM(grads, BF16),
            pltpu.VMEM(grads, BF16),
            pltpu.VMEM((steps + 1, VEC_ROWS, D), F32),
            pltpu.SemaphoreType.DMA((40,)),
        ]
        + extra,
        compiler_params=pltpu.CompilerParams(
            vmem_limit_bytes=60 * MIB, has_side_effects=True, **params
        ),
        cost_estimate=pl.CostEstimate(
            flops=80 * 10**9, bytes_accessed=50 * 10**6, transcendentals=8 * 10**6
        ),
        name="backward",
    )(info, dz2, *cross_hbm, *self_hbm, gup, gdown, *small)


def swap(a, axis, bit, size):
    return lax.ppermute(a, axis, [(i, i ^ bit) for i in range(size)])


def bits_of(size):
    return [1 << i for i in range(size.bit_length() - 1)]


def add_low(a, b):
    return (a.astype(F32) + b.astype(F32)).astype(BF16)


def halve(a, steps):
    for axis, bit, size in steps:
        half = a.shape[0] // 2
        a = add_low(a[:half], swap(a[half:], axis, bit, size))
    return a[0]


def all_sum(a, axis, size):
    rows, cols = a.shape
    me = lax.axis_index(axis)
    steps = bits_of(size)
    sent = []
    for bit in steps:
        mine = (me // bit) % 2
        a = a.reshape(2, a.shape[0] // 2, cols)
        keep = lax.dynamic_index_in_dim(a, mine, 0, keepdims=False)
        give = lax.dynamic_index_in_dim(a, 1 - mine, 0, keepdims=False)
        a = add_low(keep, swap(give, axis, bit, size))
        sent.append(mine)
    for bit, mine in zip(reversed(steps), reversed(sent)):
        other = swap(a, axis, bit, size)
        first = jnp.where(mine == 0, a, other)
        second = jnp.where(mine == 0, other, a)
        a = jnp.concatenate([first, second], axis=0)
    return a.reshape(rows, cols)


def on_device(
    sizes,
    long_rows,
    short_rows,
    long_memory,
    short_memory,
    long_cotangent,
    short_cotangent,
    long_lengths,
    short_lengths,
    self_qkv,
    self_out,
    self_bias,
    cross_qkv,
    cross_out,
    cross_bias,
    norm_gain,
    norm_bias,
    up_proj,
    up_bias,
    down_proj,
    down_bias,
):
    n_dp, n, n_rep = sizes
    count_l, LL, D = long_rows.shape
    NS, LS, _ = short_rows.shape
    FF = up_proj.shape[1]
    T = LL + NS * LS
    dims = (T, LL, LS, NS, D, n)
    shards = n * n_rep

    def flat(a, b):
        return jnp.concatenate([a.reshape(-1, D), b.reshape(-1, D)], axis=0)

    def gather(a):
        blocks = [a]
        for bit in reversed(bits_of(n)):
            got = [swap(b, "seq", bit, n) for b in blocks]
            blocks = blocks + got
        order = [0]
        for bit in reversed(bits_of(n)):
            order = order + [o ^ bit for o in order]
        return [blocks[order.index(r)] for r in range(n)]

    me = lax.axis_index("seq")
    mine = me * n_rep + lax.axis_index("rep")
    info = jnp.concatenate([long_lengths, short_lengths, me[None]]).astype(jnp.int32)

    index = jnp.arange(shards, dtype=jnp.int32) ^ mine
    rel_seq, rel_rep = index // n_rep, index % n_rep
    core, rest = rel_seq % 2, rel_seq // 2
    pos_a = core * (shards // 2) + rest * n_rep + rel_rep
    pos_b = core * (shards // 2) + rel_rep * (n // 2) + rest
    chunks = 8
    linked = (n_dp, n, n_rep) == (4, 4, 2)
    if linked:
        table_a, table_b = pos_a, pos_b
    else:
        table_a = table_b = jnp.arange(chunks, dtype=jnp.int32)

    x = flat(long_rows, short_rows)
    m = flat(long_memory, short_memory)
    cot = flat(long_cotangent, short_cotangent)
    xs = gather(x)
    ms = gather(m)

    q1, k1, v1, o1, lse1l, lse1s, z1, xt = forward_call(
        dims, False, info, xs, self_qkv, self_out, self_bias, ()
    )
    norm = (norm_gain, norm_bias)
    q2, k2, v2, o2, lse2l, lse2s, z2, mt = forward_call(
        dims, True, info, ms, cross_qkv, cross_out, cross_bias, (z1,) + norm
    )
    y, dz2, g_up, g_down, vec_f = feed_call(
        chunks, table_a, table_b, z2, cot, up_proj, down_proj, up_bias[None], down_bias[None], *norm
    )
    results = backward_call(
        dims,
        chunks,
        linked,
        info,
        dz2,
        (cross_qkv, cross_out, k2, v2, q2, o2, mt),
        (self_qkv, self_out, k1, v1, q1, o1, xt),
        g_up,
        g_down,
        (z1, *norm, lse2l, lse2s, lse1l, lse1s, vec_f),
    )
    rows = D // shards
    if linked:
        shares, dm, dx, small = results
        up_share = shares[0:2].reshape(4, rows, D).swapaxes(0, 1).reshape(rows, FF)
        down_share = shares[2:4].reshape(FF // shards, D)
        cross_share = shares[4:6].reshape(4, rows, D)
        self_share = shares[6:8].reshape(4, rows, D)
    else:
        gc, gs, dm, dx, small = results
        steps_core = [("seq", 1, n)]
        steps_x = [("seq", bit, n) for bit in reversed(bits_of(n)[1:])]
        steps_y = [("rep", bit, n_rep) for bit in reversed(bits_of(n_rep))]

        def reduce_all(a, pos, steps):
            parts = a.reshape(shards, a.shape[0] // shards, a.shape[1])
            parts = jnp.zeros_like(parts).at[pos].set(parts)
            return all_sum(halve(parts, steps), "dp", n_dp)

        def natural(a, slots):
            a = a.reshape(chunks, slots, D // chunks, D).swapaxes(0, 1)
            return a.reshape(slots, D, D)

        order_a = (pos_a, steps_core + steps_x + steps_y)
        order_b = (pos_b, steps_core + steps_y + steps_x)
        g_up = natural(g_up, FF // D).swapaxes(0, 1).reshape(D, FF)
        up_share = reduce_all(g_up, *order_a)
        down_share = reduce_all(g_down.reshape(FF, D), *order_b)

        def four(g):
            mats = jnp.concatenate([natural(g[0], 2), natural(g[1], 2)])
            return jnp.stack([reduce_all(mats[i], *order_a) for i in range(4)])

        cross_share, self_share = four(gc), four(gs)
        seq_steps = [("seq", bit, n) for bit in bits_of(n)]
        dm = halve(dm.reshape(n, T, D), seq_steps)
        dx = halve(dx.reshape(n, T, D), seq_steps)
        small = lax.psum(small, ("dp", "seq", "rep"))

    def part(a, width):
        return lax.dynamic_slice_in_dim(a, mine * width, width, axis=-1)

    vecs = part(small[0:13], D // shards)
    upb_grad = part(small[13:17].reshape(-1), FF // shards)

    def unflat(a):
        return (
            a[:LL].reshape(count_l, LL, D),
            a[LL:].reshape(NS, LS, D),
        )

    y_l, y_s = unflat(y)
    dx_l, dx_s = unflat(dx)
    dm_l, dm_s = unflat(dm)
    cross_grad = cross_share.astype(F32)
    self_grad = self_share.astype(F32)
    return (
        y_l,
        y_s,
        dx_l,
        dx_s,
        dm_l,
        dm_s,
        self_grad[1:4],
        self_grad[0],
        vecs[0:3],
        cross_grad[1:4],
        cross_grad[0],
        vecs[3:6],
        vecs[6:9],
        vecs[9:12],
        up_share.astype(F32),
        upb_grad,
        down_share.astype(F32),
        vecs[12],
    )


def solution(mesh):
    rows = P(("dp", "rep"), "seq", None)
    lengths = P(("dp", "rep"))
    share = ("seq", "rep")
    in_specs = (rows,) * 6 + (lengths,) * 2 + (P(),) * 12
    out_specs = (rows,) * 6 + (
        P(None, share, None),
        P(share, None),
        P(None, share),
        P(None, share, None),
        P(share, None),
        P(None, share),
        P(None, share),
        P(None, share),
        P(share, None),
        P(share),
        P(share, None),
        P(share),
    )
    sizes = (mesh.shape["dp"], mesh.shape["seq"], mesh.shape["rep"])
    return jax.shard_map(
        functools.partial(on_device, sizes),
        mesh=mesh,
        in_specs=in_specs,
        out_specs=out_specs,
        check_vma=False,
    )
```

```python
import functools

import jax
import jax.numpy as jnp
from jax import lax
from jax.experimental import pallas as pl
from jax.experimental.pallas import tpu as pltpu
from jax.sharding import PartitionSpec as P

HD = 64
PAIR = 2 * HD
F32 = jnp.float32
BF16 = jnp.bfloat16
NEG = -1000000000.0
MIB = 1024 * 1024
VEC_ROWS = 24

HBM = pl.BlockSpec(memory_space=pltpu.HBM)
VMEM = pl.BlockSpec(memory_space=pltpu.VMEM)
SMEM = pl.BlockSpec(memory_space=pltpu.SMEM)


def dot(a, b):
    return jnp.dot(a, b, preferred_element_type=F32)


def dot_t(a, b):
    return lax.dot_general(a, b, (((1,), (1,)), ((), ())), preferred_element_type=F32)


def loop(count, body, first=0):
    lax.fori_loop(first, count, lambda i, c: (body(i), c)[1], 0)


def tile(j, width):
    return pl.ds(pl.multiple_of(j * width, width), width)


def norm_parts(z):
    center = z - jnp.mean(z, axis=-1, keepdims=True)
    rstd = lax.rsqrt(jnp.mean(center * center, axis=-1, keepdims=True) + 1e-05)
    return center * rstd, rstd


def norm_back(dy, gain, xhat, rstd):
    dyg = dy * gain
    mean_a = jnp.mean(dyg, axis=-1, keepdims=True)
    mean_b = jnp.mean(dyg * xhat, axis=-1, keepdims=True)
    return rstd * (dyg - mean_a - xhat * mean_b)


def col_sum(a):
    return jnp.sum(a.astype(F32), axis=0, keepdims=True)


def transpose_into(dst_ref, src_ref, rows, cols, row_off=0):
    def body(j):
        dst_ref[tile(j, 128), row_off : row_off + rows] = src_ref[
            row_off : row_off + rows, tile(j, 128)
        ].T

    loop(cols // 128, body)


class Copies:
    def __init__(self, sems):
        self.sems, self.used = sems, 0

    def start(self, src, dst):
        copy = pltpu.make_async_copy(src, dst, self.sems.at[self.used])
        self.used += 1
        copy.start()
        return copy


def head_masks(dtype):
    lane = lax.broadcasted_iota(jnp.int32, (1, PAIR), 1)
    low = (lane < HD).astype(F32)
    return low.astype(dtype), (1.0 - low).astype(dtype)


def stack_heads(a, masks):
    return jnp.concatenate([a * masks[0], a * masks[1]], axis=0)


def unstack_heads(out_t, width):
    sub = lax.broadcasted_iota(jnp.int32, (PAIR, width), 0)
    return jnp.where(sub < HD, out_t[:, :width], out_t[:, width:]).T


def key_positions(block, keys, queries, size, me):
    row = lax.broadcasted_iota(jnp.int32, (keys, queries), 0)
    if keys == size:
        return row + (block ^ me) * size
    return ((row // size) ^ me) * size + row % size


def limits(queries, size, me, length, causal):
    if not causal:
        return length - 1
    lane = lax.broadcasted_iota(jnp.int32, (1, queries), 1) % size
    return jnp.minimum(lane + me * size, length - 1)


def attend_forward(dims, causal, info, q_ref, k_ref, v_ref, o_ref, lse_l, lse_s, s_scr):
    T, LL, LS, NS, D, n = dims
    me = info[NS + 1]
    masks = head_masks(BF16)

    def pair(p):
        c = tile(p, PAIR)
        q2 = stack_heads(q_ref[0:LL, c], masks)
        lim = limits(2 * LL, LL, me, info[0], causal)
        top = None
        for r in range(n):
            s = dot_t(k_ref[r * T : r * T + LL, c], q2)
            s = jnp.where(key_positions(r, LL, 2 * LL, LL, me) <= lim, s, NEG)
            s_scr[r * LL : (r + 1) * LL, :] = s
            m = jnp.max(s, axis=0, keepdims=True)
            top = m if top is None else jnp.maximum(top, m)
        total, acc = None, None
        for r in range(n):
            w = jnp.exp(s_scr[r * LL : (r + 1) * LL, :] - top)
            t = jnp.sum(w, axis=0, keepdims=True)
            a = dot(v_ref[r * T : r * T + LL, c].T, w.astype(BF16))
            total = t if total is None else total + t
            acc = a if acc is None else acc + a
        acc = acc * (1.0 / total)
        o_ref[0:LL, c] = unstack_heads(acc, LL).astype(BF16)
        lse_l[p] = jnp.broadcast_to(top + jnp.log(total), (8, 2 * LL))
        for i in range(NS):
            off = LL + i * LS
            q2 = stack_heads(q_ref[off : off + LS, c], masks)
            kb = jnp.concatenate([k_ref[r * T + off : r * T + off + LS, c] for r in range(n)], 0)
            vb = jnp.concatenate([v_ref[r * T + off : r * T + off + LS, c] for r in range(n)], 0)
            s = dot_t(kb, q2)
            lim = limits(2 * LS, LS, me, info[1 + i], causal)
            s = jnp.where(key_positions(0, n * LS, 2 * LS, LS, me) <= lim, s, NEG)
            top = jnp.max(s, axis=0, keepdims=True)
            w = jnp.exp(s - top)
            total = jnp.sum(w, axis=0, keepdims=True)
            acc = dot(vb.T, w.astype(BF16)) * (1.0 / total)
            o_ref[off : off + LS, c] = unstack_heads(acc, LS).astype(BF16)
            lse_s[p * NS + i] = jnp.broadcast_to(top + jnp.log(total), (8, 2 * LS))

    loop(D // PAIR, pair)


def attend_backward(
    dims,
    causal,
    info,
    q_ref,
    k_ref,
    v_ref,
    o_ref,
    do_ref,
    lse_l,
    lse_s,
    dq_ref,
    dk_ref,
    dv_ref,
    first,
    last,
):
    T, LL, LS, NS, D, n = dims
    me = info[NS + 1]
    masks = head_masks(BF16)
    ones = jnp.ones((8, PAIR), F32)

    def row_dots(do2, o):
        prod = do2.astype(F32) * jnp.concatenate([o, o], 0).astype(F32)
        full = lax.dot_general(
            ones,
            prod,
            (((1,), (1,)), ((), ())),
            precision=lax.Precision.HIGHEST,
            preferred_element_type=F32,
        )
        return full[0:1]

    def pair(p):
        c = tile(p, PAIR)
        q2 = stack_heads(q_ref[0:LL, c], masks)
        do2 = stack_heads(do_ref[0:LL, c], masks)
        delta = row_dots(do2, o_ref[0:LL, c])
        lse = lse_l[p][0:1]
        lim = limits(2 * LL, LL, me, info[0], causal)
        dq_t = None
        for r in range(n):
            rows = slice(r * T, r * T + LL)
            kb, vb = k_ref[rows, c], v_ref[rows, c]
            s = dot_t(kb, q2)
            s = jnp.where(key_positions(r, LL, 2 * LL, LL, me) <= lim, s, NEG)
            probs = jnp.exp(s - lse)
            ds = (probs * (dot_t(vb, do2) - delta)).astype(BF16)
            dv_ref[rows, c] = dot(probs.astype(BF16), do2).astype(BF16)
            dk_ref[rows, c] = dot(ds, q2).astype(BF16)
            part = dot(kb.T, ds)
            dq_t = part if dq_t is None else dq_t + part
        dq_ref[0:LL, c] = (unstack_heads(dq_t, LL) * HD**-0.5).astype(BF16)
        for i in range(NS):
            off = LL + i * LS
            q2 = stack_heads(q_ref[off : off + LS, c], masks)
            do2 = stack_heads(do_ref[off : off + LS, c], masks)
            delta = row_dots(do2, o_ref[off : off + LS, c])
            lse = lse_s[p * NS + i][0:1]
            kb = jnp.concatenate([k_ref[r * T + off : r * T + off + LS, c] for r in range(n)], 0)
            vb = jnp.concatenate([v_ref[r * T + off : r * T + off + LS, c] for r in range(n)], 0)
            s = dot_t(kb, q2)
            lim = limits(2 * LS, LS, me, info[1 + i], causal)
            s = jnp.where(key_positions(0, n * LS, 2 * LS, LS, me) <= lim, s, NEG)
            probs = jnp.exp(s - lse)
            ds = (probs * (dot_t(vb, do2) - delta)).astype(BF16)
            dv = dot(probs.astype(BF16), do2).astype(BF16)
            dk = dot(ds, q2).astype(BF16)
            for r in range(n):
                dv_ref[r * T + off : r * T + off + LS, c] = dv[r * LS : (r + 1) * LS]
                dk_ref[r * T + off : r * T + off + LS, c] = dk[r * LS : (r + 1) * LS]
            dq_ref[off : off + LS, c] = (unstack_heads(dot(kb.T, ds), LS) * HD**-0.5).astype(BF16)

    loop(last, pair, first)


def flip(index, bit):
    return index + bit - 2 * bit * ((index // bit) % 2)


class Link:
    def __init__(self, send_sems, recv_sems):
        self.send_sems, self.recv_sems, self.used = send_sems, recv_sems, 0

    def start(self, src, dst, axis, bit):
        copy = pltpu.make_async_remote_copy(
            src_ref=src,
            dst_ref=dst,
            send_sem=self.send_sems.at[self.used],
            recv_sem=self.recv_sems.at[self.used],
            device_id={axis: flip(lax.axis_index(axis), bit)},
            device_id_type=pl.DeviceIdType.MESH,
        )
        self.used += 1
        copy.start()
        return copy


PATH_A = (("seq", 1), ("seq", 2), ("rep", 1))
PATH_B = (("seq", 1), ("rep", 1), ("seq", 2))
PATH_ROWS = (("seq", 1), ("seq", 2))
DP_BITS = (1, 2)
PATH_ALL = PATH_A + (("dp", 1), ("dp", 2))
TILE = 256
FFN_ROWS = 384
FEED_TASKS = ("u0", "u1", "u2", "w0", "w1", "w2")
FIRST = ("u0", "w0", "u1", "w1", "u2", "w2")
X_FIRST = ("u0", "u1", "c0", "s0", "s2")
PATHS = {
    kind + str(i): PATH_A if kind + str(i) in X_FIRST else PATH_B for kind in "uwcs" for i in range(3)
}
SELF_SLOTS = (3, 0, 1)
PLAN = (
    ("u0", "w0", "u1", "w1"),
    ("u2", "w2"),
    ("c0",),
    ("u0", "w0", "c0"),
    ("c1",),
    ("u1", "w1", "c1", "w0"),
    ("c2",),
    (),
    ("u2", "w0", "c2"),
    ("c0",),
    ("dm", "w0"),
    ("w1", "w2", "dm", "w0", "u2", "u0"),
    ("w1", "w0", "u1", "w2", "u2"),
    ("s0", "u0"),
    ("w1", "u1", "s0", "u2", "w2", "c1", "u0"),
    ("s1", "dm", "w1"),
    ("u1", "s1", "c2", "w1", "u2", "w2", "c0", "s0", "u0"),
    ("s2", "vec", "u1", "u2"),
    ("c1", "w2", "c0", "s2", "vec"),
    ("u0",),
    ("c2", "s1", "c0", "u1"),
    ("dx", "c1"),
)
FINAL = (
    "s0", "w2", "c0", "dx", "c2", "c1", "s2", "s0", "vec", "c0",
    "c2", "c1", "s1", "s2", "s0", "vec", "c1", "c2", "s1", "s0",
    "s2", "vec", "s1", "c2", "s2", "dx", "s0", "vec", "s1", "s2",
    "s1", "s2",
)


class Gather:
    def __init__(self, link, ref, rows):
        self.link, self.ref, self.rows = link, ref, rows

    def block(self, r, part=None):
        first, count = r * self.rows, self.rows
        if part is not None:
            count = self.rows // 2
            first = first + part * count
        return self.ref.at[first : first + count]

    def send_core(self):
        self.core = self.link.start(self.block(0), self.block(1), "seq", 1)

    def send_far(self):
        self.far = [
            self.link.start(self.block(0, p), self.block(2, p), "seq", 2) for p in range(2)
        ]

    def relay(self):
        self.relayed = []
        for p in range(2):
            self.far[p].wait()
            self.relayed.append(self.link.start(self.block(2, p), self.block(3, p), "seq", 1))

    def end(self):
        for copy in self.relayed:
            copy.wait()


def greet(pairs):
    barrier = pltpu.get_barrier_semaphore()
    for axis, bit in pairs:
        pl.semaphore_signal(
            barrier,
            inc=1,
            device_id={axis: flip(lax.axis_index(axis), bit)},
            device_id_type=pl.DeviceIdType.MESH,
        )
    pl.semaphore_wait(barrier, len(pairs))


def forward_kernel(dims, *refs):
    T, LL, LS, NS, D, n = dims
    refs = list(refs)

    def take(count):
        out = refs[:count]
        del refs[:count]
        return out

    info, xl, xs, ml, ms = take(5)
    ws_hbm, wos_hbm, wc_hbm, woc_hbm, bias_s, bias_c, gain, shift = take(8)
    q1, k1_out, v1_out, o1, lse1l, lse1s, z1, t1_out = take(8)
    q2, k2_out, v2_out, o2, lse2l, lse2s, z2, t2_out = take(8)
    x, m, ws, wos, wc, woc, k1, v1, k2, v2, blk_t, s_scr, sems, send_sems, recv_sems = refs
    copies = Copies(sems)
    load_x = [copies.start(xl, x.at[0:LL]), copies.start(xs, x.at[LL:T])]
    load_ws = copies.start(ws_hbm, ws)
    load_m = [copies.start(ml, m.at[0:LL]), copies.start(ms, m.at[LL:T])]
    load_wc = copies.start(wc_hbm, wc)
    load_wos, load_woc = copies.start(wos_hbm, wos), copies.start(woc_hbm, woc)
    greet(PATH_ROWS)
    link = Link(send_sems, recv_sems)
    rows_x, rows_m = Gather(link, x, T), Gather(link, m, T)
    for item in load_x:
        item.wait()
    rows_x.send_far()
    rows_x.send_core()
    for item in load_m:
        item.wait()
    rows_m.send_core()

    def queries(source, w, bias, q):
        def body(j):
            c = tile(j, TILE)
            out = dot(source[0:T, :].astype(BF16), w[0, :, c]) + bias[0:1, c]
            q[:, c] = (out.astype(BF16).astype(F32) * HD**-0.5).astype(BF16)

        loop(D // TILE, body)

    def keys_values(source, w, bias, k, v, r):
        rows = slice(r * T, (r + 1) * T)

        def body(j):
            c = tile(j, TILE)
            k[rows, c] = dot(source[rows, :], w[1, :, c]).astype(BF16)
            v[rows, c] = (dot(source[rows, :], w[2, :, c]) + bias[1:2, c]).astype(BF16)

        loop(D // TILE, body)

    def residual(source, o, wo, bias, z):
        def body(j):
            c = tile(j, TILE)
            z[:, c] = source[0:T, c].astype(F32) + dot(o[...], wo[:, c]) + bias[2:3, c]

        loop(D // TILE, body)

    load_ws.wait()
    queries(x, ws, bias_s, q1)
    keys_values(x, ws, bias_s, k1, v1, 0)
    transpose_into(blk_t, x, T, D, 0)
    load_wc.wait()
    keys_values(m, wc, bias_c, k2, v2, 0)
    rows_x.core.wait()
    keys_values(x, ws, bias_s, k1, v1, 1)
    transpose_into(blk_t, x, T, D, T)
    rows_m.core.wait()
    keys_values(m, wc, bias_c, k2, v2, 1)
    rows_x.relay()
    rows_m.send_far()
    keys_values(x, ws, bias_s, k1, v1, 2)
    transpose_into(blk_t, x, T, D, 2 * T)
    rows_x.end()
    keys_values(x, ws, bias_s, k1, v1, 3)
    transpose_into(blk_t, x, T, D, 3 * T)
    stores = [copies.start(k1, k1_out), copies.start(v1, v1_out)]
    store_t = copies.start(blk_t, t1_out)
    attend_forward(dims, True, info, q1, k1, v1, o1, lse1l, lse1s, s_scr)
    load_wos.wait()
    residual(x, o1, wos, bias_s, z1)
    rows_m.relay()
    xhat, _ = norm_parts(z1[...])
    z2[...] = xhat * gain[0:1] + shift[0:1]
    queries(z2, wc, bias_c, q2)
    keys_values(m, wc, bias_c, k2, v2, 2)
    store_t.wait()
    for r in range(3):
        transpose_into(blk_t, m, T, D, r * T)
    rows_m.end()
    keys_values(m, wc, bias_c, k2, v2, 3)
    transpose_into(blk_t, m, T, D, 3 * T)
    stores += [copies.start(k2, k2_out), copies.start(v2, v2_out), copies.start(blk_t, t2_out)]
    attend_forward(dims, False, info, q2, k2, v2, o2, lse2l, lse2s, s_scr)
    load_woc.wait()
    residual(z2, o2, woc, bias_c, z2)
    for item in stores:
        item.wait()


def forward_call(dims, *operands):
    T, LL, LS, NS, D, n = dims
    pairs = D // PAIR
    full, own = (n * T, D), (T, D)
    outs = [
        jax.ShapeDtypeStruct(own, BF16),
        jax.ShapeDtypeStruct(full, BF16),
        jax.ShapeDtypeStruct(full, BF16),
        jax.ShapeDtypeStruct(own, BF16),
        jax.ShapeDtypeStruct((pairs, 8, 2 * LL), F32),
        jax.ShapeDtypeStruct((pairs * NS, 8, 2 * LS), F32),
        jax.ShapeDtypeStruct(own, F32),
        jax.ShapeDtypeStruct((D, n * T), BF16),
    ]
    return pl.pallas_call(
        functools.partial(forward_kernel, dims),
        out_shape=outs + outs,
        in_specs=[SMEM] + [HBM] * 8 + [VMEM] * 4,
        out_specs=[VMEM, HBM, HBM, VMEM, VMEM, VMEM, VMEM, HBM] * 2,
        scratch_shapes=[pltpu.VMEM(full, BF16)] * 2
        + [pltpu.VMEM((3, D, D), BF16), pltpu.VMEM((D, D), BF16)] * 2
        + [pltpu.VMEM(full, BF16)] * 4
        + [
            pltpu.VMEM((D, n * T), BF16),
            pltpu.VMEM((n * LL, 2 * LL), F32),
            pltpu.SemaphoreType.DMA((16,)),
            pltpu.SemaphoreType.DMA((10,)),
            pltpu.SemaphoreType.DMA((10,)),
        ],
        compiler_params=pltpu.CompilerParams(
            collective_id=1, has_side_effects=True, vmem_limit_bytes=58 * MIB
        ),
        cost_estimate=pl.CostEstimate(
            flops=20 * 10**9, bytes_accessed=40 * 10**6, transcendentals=8 * 10**6
        ),
        name="forward",
    )(*operands)


def feed_kernel(T, D, FF, chunks, *refs):
    (
        pos, z2, cot_l, cot_s, wup_hbm, wdown_hbm, upb, downb, gain, shift,
        yl_out, ys_out, dz2_out, gup_out, gdown_out, vec_out,
        wup, wdown, h2t, g, gp, acc, dfs, gup, gdown, sems,
    ) = refs
    copies = Copies(sems)
    load_up = copies.start(wup_hbm, wup)
    load_down = copies.start(wdown_hbm, wdown)
    wide = TILE
    rows = D // chunks
    per_row = D // wide
    vec_out[...] = jnp.zeros(vec_out.shape, F32)
    xhat2, rstd2 = norm_parts(z2[...])
    h2 = xhat2 * gain[1:2] + shift[1:2]
    h2b = h2.astype(BF16)
    dfs[...] = h2b
    acc[...] = h2 + downb[...]
    transpose_into(h2t, dfs, T, D)
    load_up.wait()
    load_down.wait()

    def up_tile(j):
        c = tile(j, wide)
        u = dot(dfs[...], wup[:, c]) + upb[:, c]
        sq = u * u
        th = jnp.tanh(0.7978845608028654 * u * (1.0 + 0.044715 * sq))
        half = 0.5 * (1.0 + th)
        act = (u * half).astype(BF16)
        g[:, c] = act
        gp[:, c] = half + (0.5 * 0.7978845608028654) * u * (1.0 - th * th) * (
            1.0 + (3.0 * 0.044715) * sq
        )
        acc[...] += dot(act, wdown[c, :])

    loop(FF // wide, up_tile)
    xhat3, rstd3 = norm_parts(acc[...])
    y = (xhat3 * gain[2:3] + shift[2:3]).astype(BF16)
    LL = yl_out.shape[0]
    yl_out[...], ys_out[...] = y[:LL], y[LL:]
    dy = jnp.concatenate([cot_l[...], cot_s[...]], axis=0).astype(F32)
    vec_out[8:9] = col_sum(dy * xhat3)
    vec_out[11:12] = col_sum(dy)
    dz3 = norm_back(dy, gain[2:3], xhat3, rstd3)
    df = dz3.astype(BF16)
    dfs[...] = df
    acc[...] = dz3
    vec_out[12:13] = col_sum(df)

    def back_tile(j):
        c = tile(j, wide)
        dg = dot_t(dfs[...], wdown[c, :])
        du = (gp[:, c] * dg).astype(BF16)
        vec_out[pl.ds(13 + j // per_row, 1), tile(j % per_row, wide)] = col_sum(du)
        acc[...] += dot_t(du, wup[:, c])
        up = dot(h2t[...], du).astype(BF16)
        down = dot(g[:, c].T, dfs[...]).astype(BF16)
        block = pl.ds(pl.multiple_of((j // per_row) * rows, rows), rows)
        t = j % per_row
        for s in range(chunks):
            gup[t, pos[t, s], block, :] = up[s * rows : (s + 1) * rows]
        for i in range(wide // PAIR):
            piece = j * (wide // PAIR) + i
            at = tile(piece % (FF // chunks // PAIR), PAIR)
            s = piece // (FF // chunks // PAIR)
            for t in range(D // wide):
                part = down[i * PAIR : (i + 1) * PAIR, t * wide : (t + 1) * wide]
                gdown[t, pos[per_row + t, s], at, :] = part

    loop(FF // wide, back_tile)
    stores = [copies.start(gup, gup_out), copies.start(gdown, gdown_out)]
    dh2 = acc[...]
    xhat2, rstd2 = norm_parts(z2[...])
    vec_out[7:8] = col_sum(dh2 * xhat2)
    vec_out[10:11] = col_sum(dh2)
    dz2_out[...] = norm_back(dh2, gain[1:2], xhat2, rstd2)
    for item in stores:
        item.wait()


def feed_call(chunks, pos, z2, cot_l, cot_s, wup, wdown, upb, downb, gain, shift):
    T, D = z2.shape
    FF = wup.shape[1]
    return pl.pallas_call(
        functools.partial(feed_kernel, T, D, FF, chunks),
        out_shape=[
            jax.ShapeDtypeStruct(cot_l.shape, BF16),
            jax.ShapeDtypeStruct(cot_s.shape, BF16),
            jax.ShapeDtypeStruct((T, D), F32),
            jax.ShapeDtypeStruct((D // TILE, chunks, FF // chunks, TILE), BF16),
            jax.ShapeDtypeStruct((D // TILE, chunks, FF // chunks, TILE), BF16),
            jax.ShapeDtypeStruct((VEC_ROWS, D), F32),
        ],
        in_specs=[SMEM, VMEM, VMEM, VMEM, HBM, HBM, VMEM, VMEM, VMEM, VMEM],
        out_specs=[VMEM, VMEM, VMEM, HBM, HBM, VMEM],
        scratch_shapes=[
            pltpu.VMEM((D, FF), BF16),
            pltpu.VMEM((FF, D), BF16),
            pltpu.VMEM((D, T), BF16),
            pltpu.VMEM((T, FF), BF16),
            pltpu.VMEM((T, FF), F32),
            pltpu.VMEM((T, D), F32),
            pltpu.VMEM((T, D), BF16),
            pltpu.VMEM((D // TILE, chunks, FF // chunks, TILE), BF16),
            pltpu.VMEM((D // TILE, chunks, FF // chunks, TILE), BF16),
            pltpu.SemaphoreType.DMA((4,)),
        ],
        compiler_params=pltpu.CompilerParams(vmem_limit_bytes=58 * MIB),
        cost_estimate=pl.CostEstimate(
            flops=30 * 10**9, bytes_accessed=25 * 10**6, transcendentals=2 * 10**6
        ),
        name="feed",
    )(pos, z2, cot_l, cot_s, wup, wdown, upb, downb, gain, shift)


def backward_phase(dims, cross, chunks, info, loads, data, scratch, vec, orders, tick, free):
    T, LL, LS, NS, D, n = dims
    dz, z_in, gain, shift, lse_l, lse_s = data
    q, o, w, wo, k, v, dq, do, da, blk_t, o_t, src_t, dblk, grads = scratch
    rows = D // chunks
    base = 3 if cross else 0

    def weight_grad(i, slot, lhs_t, rhs):
        grad = dot(lhs_t, rhs).astype(BF16)
        out = grads.at[i].reshape(chunks, 4 * rows, TILE)
        for s in range(chunks):
            out[orders[i][s], slot * rows : (slot + 1) * rows, :] = grad[s * rows : (s + 1) * rows]

    da[...] = dz[...].astype(BF16)
    vec[base + 2 : base + 3] = col_sum(da[...])
    loads["o"].wait()
    transpose_into(o_t, o, T, D)
    loads["wo"].wait()
    for i in range(D // TILE):
        c = slice(i * TILE, (i + 1) * TILE)
        do[:, c] = dot_t(da[...], wo[c, :]).astype(BF16)
        weight_grad(i, 0, o_t[...], da[:, c])
    free("wo")
    if cross:
        xhat, _ = norm_parts(z_in[...])
        da[...] = (xhat * gain[0:1] + shift[0:1]).astype(BF16)
        transpose_into(src_t, da, T, D)
    tick()
    for name in ("q", "k", "v", "t"):
        loads[name].wait()
    if not cross:
        src_t[...] = blk_t[:, 0:T]
    pairs = TILE // PAIR
    for i in range(D // TILE):
        c = slice(i * TILE, (i + 1) * TILE)
        attend_backward(
            dims, not cross, info, q, k, v, o, do, lse_l, lse_s, dq, k, v, pairs * i, pairs * (i + 1)
        )
        tick()
        vec[base : base + 1, c] = col_sum(dq[:, c])
        vec[base + 1 : base + 2, c] = col_sum(v[:, c])
        weight_grad(i, 1, src_t[...], dq[:, c])
        weight_grad(i, 2, blk_t[...], k[:, c])
        weight_grad(i, 3, blk_t[...], v[:, c])
        tick()
    for name in ("q", "o", "t"):
        free(name)
    loads["w"].wait()
    free("dblk")

    def dblk_tile(i, at, j):
        c = tile(j, TILE)
        rows_in = slice(i * T, (i + 1) * T)
        part = dot_t(k[rows_in, :], w[1, c, :]) + dot_t(v[rows_in, :], w[2, c, :])
        if i == 0:
            part_q = dz[:, c] + dot_t(dq[...], w[0, c, :])
            if cross:
                dz[:, c] = part_q
            else:
                part = part + part_q
        dblk[at * T : (at + 1) * T, c] = part.astype(BF16)

    kept_first = sorted(range(n), key=lambda r: (r % 2, r // 2))
    for at in reversed(range(n)):
        loop(D // TILE, functools.partial(dblk_tile, kept_first[at], at))
        if at > 0:
            tick()
    for name in ("k", "v", "w"):
        free(name)
    tick()
    if cross:
        dh = dz[...]
        xhat, rstd = norm_parts(z_in[...])
        vec[6:7] = col_sum(dh * xhat)
        vec[9:10] = col_sum(dh)
        dz[...] = norm_back(dh, gain[0:1], xhat, rstd)


def add_rows(dst, dst_at, a, a_at, b, b_at, count, step=96):
    def body(i):
        def at(start):
            return pl.ds(pl.multiple_of(start + i * step, 16), step)

        total = a[at(a_at), :].astype(F32) + b[at(b_at), :].astype(F32)
        dst[at(dst_at), :] = total.astype(dst.dtype)

    loop(count // step, body)


class Share:
    def __init__(self, link, theirs, acc, recv, res, size, path, dp_bits):
        self.link, self.theirs, self.acc, self.recv, self.res = link, theirs, acc, recv, res
        self.size, self.path, self.dp_bits = size, path, dp_bits
        self.stage, self.copy, self.at = 0, None, 0
        self.off, self.count = 0, size
        self.kept, self.last = [], len(path) + 2 * len(dp_bits)

    def advance(self):
        stage, path, dp_bits = self.stage, self.path, self.dp_bits
        if stage > self.last:
            return
        self.stage += 1
        halves = len(path)
        if stage == 0:
            rows = self.size << (halves - 1)
            self.land, self.rows = self.at, rows
            self.at += rows
            land = self.recv.at[0:rows]
            if len(self.theirs.shape) == 3:
                land = land.reshape(*self.theirs.shape)
            self.copy = self.link.start(self.theirs, land, *path[0])
            return
        self.copy.wait()
        if stage <= halves + len(dp_bits):
            last = stage == halves + len(dp_bits)
            dst = self.res if last else self.acc
            add_rows(dst, self.off, self.acc, self.off, self.recv, self.land, self.rows, 48)
        if stage < halves:
            rows = self.size << (halves - 1 - stage)
            self.land, self.rows = self.at, rows
            self.at += rows
            src = self.acc.at[rows : 2 * rows]
            dst = self.recv.at[self.land : self.land + rows]
            self.copy = self.link.start(src, dst, *path[stage])
        elif stage < halves + len(dp_bits):
            bit = dp_bits[stage - halves]
            mine = (lax.axis_index("dp") // bit) % 2
            self.count //= 2
            give = self.off + (1 - mine) * self.count
            self.off = self.off + mine * self.count
            self.kept.append((self.off, self.count, bit))
            self.land, self.rows = self.at, self.count
            self.at += self.count
            src = self.acc.at[pl.ds(pl.multiple_of(give, 16), self.count)]
            dst = self.recv.at[self.land : self.land + self.count]
            self.copy = self.link.start(src, dst, "dp", bit)
        elif self.kept:
            off, count, bit = self.kept.pop()
            part = self.res.at[pl.ds(pl.multiple_of(off, 16), count)]
            self.copy = self.link.start(part, part, "dp", bit)


class Rows:
    def __init__(self, link, copies, blocks, recv, lands, out, size, path):
        self.link, self.copies, self.blocks, self.recv, self.out = link, copies, blocks, recv, out
        self.size, self.path, self.stage, self.lands, self.last = size, path, 0, lands, len(path)

    def advance(self):
        stage, path = self.stage, self.path
        if stage > self.last:
            return
        self.stage += 1
        if stage > 0:
            self.copy.wait()
            add_rows(self.blocks, 0, self.blocks, 0, self.recv, self.land, self.rows)
        if stage == len(path):
            self.store = self.copies.start(self.blocks.at[0 : self.rows], self.out)
        if stage < len(path):
            rows = self.size << (len(path) - 1 - stage)
            self.land, self.rows = self.lands[stage], rows
            src = self.blocks.at[rows : 2 * rows]
            dst = self.recv.at[self.land : self.land + rows]
            self.copy = self.link.start(src, dst, *path[stage])


class Small:
    def __init__(self, link, vec, recv, path):
        self.link, self.vec, self.recv, self.path, self.stage = link, vec, recv, path, 0
        self.last = len(path)

    def advance(self):
        stage, path = self.stage, self.path
        if stage > self.last:
            return
        self.stage += 1
        if stage > 0:
            self.copy.wait()
            self.vec[stage] = self.vec[stage - 1] + self.recv[stage - 1]
        if stage < len(path):
            self.copy = self.link.start(self.vec.at[stage], self.recv.at[stage], *path[stage])


def xor_order(path, chunks):
    seq, rep = lax.axis_index("seq"), lax.axis_index("rep")
    out = []
    for s in range(chunks):
        x = (s // 4 + seq // 2) % 2
        core = (s // 2 + seq) % 2
        y = (s + rep) % 2
        out.append(core * 4 + (x * 2 + y if path is PATH_A else y * 2 + x))
    return out


def backward_kernel(dims, chunks, linked, *refs):
    T, LL, LS, NS, D, n = dims
    refs = list(refs)

    def take(count):
        out = refs[:count]
        del refs[:count]
        return out

    info, dz2_hbm = take(2)
    cross_hbm, self_hbm = take(7), take(7)
    gup, gdown = take(2)
    z1, gain, shift, lse2l, lse2s, lse1l, lse1s, vec_in = take(8)
    if linked:
        shares_out, dm_out, dx_out, vec_out = take(4)
    else:
        gc_out, gs_out, dm_out, dx_out, vec_out = take(5)
    q, o, w, wo, k, v, dq, do, da, blk_t, o_t, src_t, dblk, dres = take(14)
    gc, gs, vec, sems = take(4)
    if linked:
        accs, recvs, rows_recv, res, vec_recv, send_sems, recv_sems = take(7)

    copies = Copies(sems)
    load_dz = copies.start(dz2_hbm, dres)
    homes = {"wo": wo, "o": o, "q": q, "k": k, "v": v, "t": blk_t, "w": w}
    sources_c = dict(zip(("w", "wo", "k", "v", "q", "o", "t"), cross_hbm))
    sources_s = dict(zip(("w", "wo", "k", "v", "q", "o", "t"), self_hbm))
    vec[0] = vec_in[...]
    tiles = D // TILE
    tasks = {}
    loads_c = {}
    if linked:
        half = chunks // 2
        size = FFN_ROWS
        greet(PATH_ALL)
        link = Link(send_sems, recv_sems)
        own = []
        for i, name in enumerate(FEED_TASKS):
            grad = (gup if i < tiles else gdown).at[i % tiles]
            tasks[name] = Share(
                link, grad.at[half:], accs.at[i], recvs.at[i], res.at[i], size, PATHS[name], DP_BITS
            )
            own.append(copies.start(grad.at[0:half], accs.at[i].reshape(half, size, TILE)))
        for name in FIRST:
            tasks[name].advance()
        for i in range(tiles):
            for kind, g, first, slot in (("c", gc, 6, 6 + i), ("s", gs, 9, SELF_SLOTS[i])):
                name = kind + str(i)
                tasks[name] = Share(
                    link, g.at[i, half * size :], g.at[i], recvs.at[slot], res.at[first + i],
                    size, PATHS[name], DP_BITS,
                )
        tasks["dm"] = Rows(link, copies, dblk, rows_recv, (0, 2 * T), dm_out, T, PATH_ROWS)
        tasks["dx"] = Rows(link, copies, dblk, rows_recv, (0, 3 * T), dx_out, T, PATH_ROWS)
        tasks["vec"] = Small(link, vec, vec_recv, PATH_ALL)
        orders_c = [xor_order(PATHS["c" + str(i)], chunks) for i in range(tiles)]
        orders_s = [xor_order(PATHS["s" + str(i)], chunks) for i in range(tiles)]
    else:
        orders_c = orders_s = [list(range(chunks))] * tiles
    for name, home in homes.items():
        loads_c[name] = copies.start(sources_c[name], home)
    if linked:
        for item in own:
            item.wait()
    load_dz.wait()

    steps = iter(PLAN)

    def tick():
        if linked:
            for name in next(steps):
                tasks[name].advance()

    loads_s = {}

    def free_cross(name):
        if name in homes:
            loads_s[name] = copies.start(sources_s[name], homes[name])

    def free_self(name):
        if linked and name == "dblk":
            while tasks["dm"].stage <= tasks["dm"].last:
                tasks["dm"].advance()
            tasks["dm"].store.wait()

    backward_phase(
        dims, True, chunks, info, loads_c, (dres, z1, gain, shift, lse2l, lse2s),
        (q, o, w, wo, k, v, dq, do, da, blk_t, o_t, src_t, dblk, gc), vec.at[0], orders_c, tick,
        free_cross,
    )
    if not linked:
        stores = [copies.start(gc, gc_out)]
        copies.start(dblk, dm_out).wait()
    backward_phase(
        dims, False, chunks, info, loads_s, (dres, None, None, None, lse1l, lse1s),
        (q, o, w, wo, k, v, dq, do, da, blk_t, o_t, src_t, dblk, gs), vec.at[0], orders_s, tick,
        free_self,
    )
    if linked:
        for name in FINAL:
            tasks[name].advance()
        for task in tasks.values():
            while task.stage <= task.last:
                task.advance()
        copies.start(res, shares_out).wait()
        tasks["dx"].store.wait()
        vec_out[...] = vec[len(PATH_ALL)]
    else:
        vec_out[...] = vec[0]
        stores += [copies.start(gs, gs_out), copies.start(dblk, dx_out)]
        for item in stores:
            item.wait()


def backward_call(dims, chunks, linked, info, dz2, cross_hbm, self_hbm, gup, gdown, small):
    T, LL, LS, NS, D, n = dims
    full, own = (n * T, D), (T, D)
    tiles = D // TILE
    size = 4 * (D // chunks)
    grads = (tiles, chunks * size, TILE)
    vec = jax.ShapeDtypeStruct((VEC_ROWS, D), F32)
    steps = len(PATH_ALL)
    if linked:
        out_shape = [
            jax.ShapeDtypeStruct((4 * tiles, size, TILE), BF16),
            jax.ShapeDtypeStruct(own, BF16),
            jax.ShapeDtypeStruct(own, BF16),
            vec,
        ]
        out_specs = [HBM, HBM, HBM, VMEM]
        landing = 7 * size + 3 * size // 4
        count = 4 * tiles * 7 + 4 + steps
        extra = [
            pltpu.VMEM((2 * tiles, chunks // 2 * size, TILE), BF16),
            pltpu.VMEM((3 * tiles, landing, TILE), BF16),
            pltpu.VMEM((4 * T, D), BF16),
            pltpu.VMEM((4 * tiles, size, TILE), BF16),
            pltpu.VMEM((steps, VEC_ROWS, D), F32),
            pltpu.SemaphoreType.DMA((count,)),
            pltpu.SemaphoreType.DMA((count,)),
        ]
    else:
        out_shape = [
            jax.ShapeDtypeStruct(grads, BF16),
            jax.ShapeDtypeStruct(grads, BF16),
            jax.ShapeDtypeStruct(full, BF16),
            jax.ShapeDtypeStruct(full, BF16),
            vec,
        ]
        out_specs = [HBM, HBM, HBM, HBM, VMEM]
        extra = []
    params = {"collective_id": 0} if linked else {}
    return pl.pallas_call(
        functools.partial(backward_kernel, dims, chunks, linked),
        out_shape=out_shape,
        in_specs=[SMEM] + [HBM] * 17 + [VMEM] * 8,
        out_specs=out_specs,
        scratch_shapes=[
            pltpu.VMEM(own, BF16),
            pltpu.VMEM(own, BF16),
            pltpu.VMEM((3, D, D), BF16),
            pltpu.VMEM((D, D), BF16),
            pltpu.VMEM(full, BF16),
            pltpu.VMEM(full, BF16),
            pltpu.VMEM(own, BF16),
            pltpu.VMEM(own, BF16),
            pltpu.VMEM(own, BF16),
            pltpu.VMEM((D, n * T), BF16),
            pltpu.VMEM((D, T), BF16),
            pltpu.VMEM((D, T), BF16),
            pltpu.VMEM(full, BF16),
            pltpu.VMEM(own, F32),
            pltpu.VMEM(grads, BF16),
            pltpu.VMEM(grads, BF16),
            pltpu.VMEM((steps + 1, VEC_ROWS, D), F32),
            pltpu.SemaphoreType.DMA((32,)),
        ]
        + extra,
        compiler_params=pltpu.CompilerParams(
            vmem_limit_bytes=60 * MIB, has_side_effects=True, **params
        ),
        cost_estimate=pl.CostEstimate(
            flops=80 * 10**9, bytes_accessed=50 * 10**6, transcendentals=8 * 10**6
        ),
        name="backward",
    )(info, dz2, *cross_hbm, *self_hbm, gup, gdown, *small)


def finish_kernel(dims, mesh_sizes, shares, dm, dx, vec, *outs):
    T, LL, LS, NS, D, n = dims
    (
        dx_l, dx_s, dm_l, dm_s, g_self, g_selfout, b_self, g_cross, g_crossout, b_cross,
        g_gain, g_shift, g_up, b_up, g_down, b_down,
    ) = outs
    shards = mesh_sizes[1] * mesh_sizes[2]
    mine = lax.axis_index("seq") * mesh_sizes[2] + lax.axis_index("rep")
    dx_l[...], dx_s[...] = dx[0:LL], dx[LL:T]
    dm_l[...], dm_s[...] = dm[0:LL], dm[LL:T]
    rows = D // shards
    for t in range(D // TILE):
        c = slice(t * TILE, (t + 1) * TILE)
        for i in range(4):
            part = slice(i * rows, (i + 1) * rows)
            g_up[:, i * D + t * TILE : i * D + (t + 1) * TILE] = shares[t, part, :].astype(F32)
            for first, whole, alone in ((6, g_cross, g_crossout), (9, g_self, g_selfout)):
                value = shares[first + t, part, :].astype(F32)
                if i == 0:
                    alone[:, c] = value
                else:
                    whole[i - 1, :, c] = value
        g_down[:, c] = shares[3 + t].astype(F32)
    turned = pltpu.roll(vec[...], D - mine * rows, 1)
    for i, out in enumerate((b_self, b_cross, g_gain, g_shift)):
        out[...] = turned[3 * i : 3 * i + 3, 0:rows]
    b_down[...] = turned[12:13, 0:rows]
    ups = vec[13:14, :]
    per_row = D // (4 * rows)
    for i in range(1, 4):
        ups = jnp.where(mine // per_row == i, vec[13 + i : 14 + i, :], ups)
    out = ups[:, 0 : 4 * rows]
    for i in range(1, per_row):
        out = jnp.where(mine % per_row == i, ups[:, i * 4 * rows : (i + 1) * 4 * rows], out)
    b_up[...] = out


def finish_call(dims, sizes, shares, dm, dx, vec):
    T, LL, LS, NS, D, n = dims
    rows = D // (sizes[1] * sizes[2])

    def shape(*dims):
        return jax.ShapeDtypeStruct(dims, F32)

    tokens = [jax.ShapeDtypeStruct((LL, D), BF16), jax.ShapeDtypeStruct((T - LL, D), BF16)]
    out_shape = tokens + tokens + [
        shape(3, rows, D), shape(rows, D), shape(3, rows), shape(3, rows, D), shape(rows, D),
        shape(3, rows), shape(3, rows), shape(3, rows), shape(rows, 4 * D), shape(1, 4 * rows),
        shape(4 * rows, D), shape(1, rows),
    ]
    return pl.pallas_call(
        functools.partial(finish_kernel, dims, sizes),
        out_shape=out_shape,
        in_specs=[VMEM] * 4,
        out_specs=[VMEM] * len(out_shape),
        compiler_params=pltpu.CompilerParams(vmem_limit_bytes=40 * MIB),
        name="finish",
    )(shares, dm, dx, vec)


def swap(a, axis, bit, size):
    return lax.ppermute(a, axis, [(i, i ^ bit) for i in range(size)])


def bits_of(size):
    return [1 << i for i in range(size.bit_length() - 1)]


def add_low(a, b):
    return (a.astype(F32) + b.astype(F32)).astype(BF16)


def halve(a, steps):
    for axis, bit, size in steps:
        half = a.shape[0] // 2
        a = add_low(a[:half], swap(a[half:], axis, bit, size))
    return a[0]


def all_sum(a, axis, size):
    rows, cols = a.shape
    me = lax.axis_index(axis)
    steps = bits_of(size)
    sent = []
    for bit in steps:
        mine = (me // bit) % 2
        a = a.reshape(2, a.shape[0] // 2, cols)
        keep = lax.dynamic_index_in_dim(a, mine, 0, keepdims=False)
        give = lax.dynamic_index_in_dim(a, 1 - mine, 0, keepdims=False)
        a = add_low(keep, swap(give, axis, bit, size))
        sent.append(mine)
    for bit, mine in zip(reversed(steps), reversed(sent)):
        other = swap(a, axis, bit, size)
        first = jnp.where(mine == 0, a, other)
        second = jnp.where(mine == 0, other, a)
        a = jnp.concatenate([first, second], axis=0)
    return a.reshape(rows, cols)


def on_device(
    sizes,
    long_rows,
    short_rows,
    long_memory,
    short_memory,
    long_cotangent,
    short_cotangent,
    long_lengths,
    short_lengths,
    self_qkv,
    self_out,
    self_bias,
    cross_qkv,
    cross_out,
    cross_bias,
    norm_gain,
    norm_bias,
    up_proj,
    up_bias,
    down_proj,
    down_bias,
):
    n_dp, n, n_rep = sizes
    count_l, LL, D = long_rows.shape
    NS, LS, _ = short_rows.shape
    FF = up_proj.shape[1]
    T = LL + NS * LS
    dims = (T, LL, LS, NS, D, n)
    shards = n * n_rep

    def flat(a):
        return a.reshape(-1, D)

    me = lax.axis_index("seq")
    mine = me * n_rep + lax.axis_index("rep")
    info = jnp.concatenate([long_lengths, short_lengths, me[None]]).astype(jnp.int32)

    index = jnp.arange(shards, dtype=jnp.int32) ^ mine
    rel_seq, rel_rep = index // n_rep, index % n_rep
    core, rest = rel_seq % 2, rel_seq // 2
    pos_a = core * (shards // 2) + rest * n_rep + rel_rep
    pos_b = core * (shards // 2) + rel_rep * (n // 2) + rest
    chunks = 8
    linked = (n_dp, n, n_rep) == (4, 4, 2)
    if linked:
        table = jnp.stack([pos_a if name in X_FIRST else pos_b for name in FEED_TASKS])
    else:
        table = jnp.tile(jnp.arange(chunks, dtype=jnp.int32), (len(FEED_TASKS), 1))

    norm = (norm_gain, norm_bias)
    outs = forward_call(
        dims, info, flat(long_rows), flat(short_rows), flat(long_memory), flat(short_memory),
        self_qkv, self_out, cross_qkv, cross_out, self_bias, cross_bias, *norm,
    )
    q1, k1, v1, o1, lse1l, lse1s, z1, xt = outs[:8]
    q2, k2, v2, o2, lse2l, lse2s, z2, mt = outs[8:]
    y_l, y_s, dz2, g_up, g_down, vec_f = feed_call(
        chunks, table, z2, flat(long_cotangent), flat(short_cotangent), up_proj, down_proj,
        up_bias[None], down_bias[None], *norm,
    )
    results = backward_call(
        dims,
        chunks,
        linked,
        info,
        dz2,
        (cross_qkv, cross_out, k2, v2, q2, o2, mt),
        (self_qkv, self_out, k1, v1, q1, o1, xt),
        g_up,
        g_down,
        (z1, *norm, lse2l, lse2s, lse1l, lse1s, vec_f),
    )
    rows = D // shards
    if linked:
        shares, dm, dx, small = results
        dx_l, dx_s, dm_l, dm_s, *rest = finish_call(dims, sizes, shares, dm, dx, small)
        rest[9], rest[11] = rest[9][0], rest[11][0]
        tokens = (y_l, y_s, dx_l, dx_s, dm_l, dm_s)
        shapes = (long_rows.shape, short_rows.shape) * 3
        return tuple(a.reshape(b) for a, b in zip(tokens, shapes)) + tuple(rest)
    gc, gs, dm, dx, small = results
    steps_core = [("seq", 1, n)]
    steps_x = [("seq", bit, n) for bit in reversed(bits_of(n)[1:])]
    steps_y = [("rep", bit, n_rep) for bit in reversed(bits_of(n_rep))]

    def reduce_all(a, pos, steps):
        parts = a.reshape(shards, a.shape[0] // shards, a.shape[1])
        parts = jnp.zeros_like(parts).at[pos].set(parts)
        return all_sum(halve(parts, steps), "dp", n_dp)

    order_a = (pos_a, steps_core + steps_x + steps_y)
    order_b = (pos_b, steps_core + steps_y + steps_x)
    split = (D // TILE, chunks, 4, D // chunks, TILE)
    g_up = g_up.reshape(split).transpose(1, 3, 2, 0, 4).reshape(D, FF)
    up_share = reduce_all(g_up, *order_a)
    down_share = reduce_all(g_down.transpose(1, 2, 0, 3).reshape(FF, D), *order_b)

    def four(g):
        mats = g.reshape(split).transpose(2, 1, 3, 0, 4).reshape(4, D, D)
        return jnp.stack([reduce_all(mats[i], *order_a) for i in range(4)])

    cross_share, self_share = four(gc), four(gs)
    seq_steps = [("seq", bit, n) for bit in bits_of(n)]
    dm = dm.reshape(n, T, D)
    dx = dx.reshape(n, T, D)
    dm = halve(dm, seq_steps)
    dx = halve(dx, seq_steps)
    small = lax.psum(small, ("dp", "seq", "rep"))

    def part(a, width):
        return lax.dynamic_slice_in_dim(a, mine * width, width, axis=-1)

    vecs = part(small[0:13], D // shards)
    upb_grad = part(small[13:17].reshape(-1), FF // shards)

    def unflat(a):
        return (
            a[:LL].reshape(count_l, LL, D),
            a[LL:].reshape(NS, LS, D),
        )

    y_l, y_s = y_l.reshape(long_rows.shape), y_s.reshape(short_rows.shape)
    dx_l, dx_s = unflat(dx)
    dm_l, dm_s = unflat(dm)
    cross_grad = cross_share.astype(F32)
    self_grad = self_share.astype(F32)
    return (
        y_l,
        y_s,
        dx_l,
        dx_s,
        dm_l,
        dm_s,
        self_grad[1:4],
        self_grad[0],
        vecs[0:3],
        cross_grad[1:4],
        cross_grad[0],
        vecs[3:6],
        vecs[6:9],
        vecs[9:12],
        up_share.astype(F32),
        upb_grad,
        down_share.astype(F32),
        vecs[12],
    )


def solution(mesh):
    rows = P(("dp", "rep"), "seq", None)
    lengths = P(("dp", "rep"))
    share = ("seq", "rep")
    in_specs = (rows,) * 6 + (lengths,) * 2 + (P(),) * 12
    out_specs = (rows,) * 6 + (
        P(None, share, None),
        P(share, None),
        P(None, share),
        P(None, share, None),
        P(share, None),
        P(None, share),
        P(None, share),
        P(None, share),
        P(share, None),
        P(share),
        P(share, None),
        P(share),
    )
    sizes = (mesh.shape["dp"], mesh.shape["seq"], mesh.shape["rep"])
    return jax.shard_map(
        functools.partial(on_device, sizes),
        mesh=mesh,
        in_specs=in_specs,
        out_specs=out_specs,
        check_vma=False,
    )
```

```python
import functools

import jax
import jax.numpy as jnp
from jax import lax
from jax.experimental import pallas as pl
from jax.experimental.pallas import tpu as pltpu
from jax.sharding import PartitionSpec as P

HD = 64
PAIR = 2 * HD
F32 = jnp.float32
BF16 = jnp.bfloat16
NEG = -1000000000.0
MIB = 1024 * 1024
VEC_ROWS = 24

HBM = pl.BlockSpec(memory_space=pltpu.HBM)
VMEM = pl.BlockSpec(memory_space=pltpu.VMEM)
SMEM = pl.BlockSpec(memory_space=pltpu.SMEM)


def dot(a, b):
    return jnp.dot(a, b, preferred_element_type=F32)


def dot_t(a, b):
    return lax.dot_general(a, b, (((1,), (1,)), ((), ())), preferred_element_type=F32)


def loop(count, body, first=0):
    if count <= 3 and first == 0:
        for i in range(count):
            body(i)
        return
    lax.fori_loop(first, count, lambda i, c: (body(i), c)[1], 0)


def tile(j, width):
    if isinstance(j, int):
        return pl.ds(j * width, width)
    return pl.ds(pl.multiple_of(j * width, width), width)


def norm_parts(z):
    center = z - jnp.mean(z, axis=-1, keepdims=True)
    rstd = lax.rsqrt(jnp.mean(center * center, axis=-1, keepdims=True) + 1e-05)
    return center * rstd, rstd


def norm_back(dy, gain, xhat, rstd):
    dyg = dy * gain
    mean_a = jnp.mean(dyg, axis=-1, keepdims=True)
    mean_b = jnp.mean(dyg * xhat, axis=-1, keepdims=True)
    return rstd * (dyg - mean_a - xhat * mean_b)


def col_sum(a):
    return jnp.sum(a.astype(F32), axis=0, keepdims=True)


def transpose_into(dst_ref, src_ref, rows, cols, row_off=0):
    def body(j):
        dst_ref[tile(j, 128), row_off : row_off + rows] = src_ref[
            row_off : row_off + rows, tile(j, 128)
        ].T

    loop(cols // 128, body)


class Copies:
    def __init__(self, sems):
        self.sems, self.used = sems, 0

    def start(self, src, dst):
        copy = pltpu.make_async_copy(src, dst, self.sems.at[self.used])
        self.used += 1
        copy.start()
        return copy


def row_info(long_len, short_len, count):
    return [long_len[0], *(short_len[i] for i in range(count)), lax.axis_index("seq")]


def head_masks(dtype):
    lane = lax.broadcasted_iota(jnp.int32, (1, PAIR), 1)
    low = (lane < HD).astype(F32)
    return low.astype(dtype), (1.0 - low).astype(dtype)


def stack_heads(a, masks):
    return jnp.concatenate([a * masks[0], a * masks[1]], axis=0)


def unstack_heads(out_t, width):
    sub = lax.broadcasted_iota(jnp.int32, (PAIR, width), 0)
    return jnp.where(sub < HD, out_t[:, :width], out_t[:, width:]).T


def key_positions(block, keys, queries, size, me):
    row = lax.broadcasted_iota(jnp.int32, (keys, queries), 0)
    if keys == size:
        return row + (block ^ me) * size
    return ((row // size) ^ me) * size + row % size


def limits(queries, size, me, length, causal):
    if not causal:
        return length - 1
    lane = lax.broadcasted_iota(jnp.int32, (1, queries), 1) % size
    return jnp.minimum(lane + me * size, length - 1)


def attend_forward(dims, causal, info, q_ref, k_ref, v_ref, o_ref, lse_l, lse_s, s_scr):
    T, LL, LS, NS, D, n = dims
    me = info[NS + 1]
    masks = head_masks(BF16)

    def pair(p):
        c = tile(p, PAIR)
        q2 = stack_heads(q_ref[0:LL, c], masks)
        lim = limits(2 * LL, LL, me, info[0], causal)
        top = None
        for r in range(n):
            s = dot_t(k_ref[r * T : r * T + LL, c], q2)
            s = jnp.where(key_positions(r, LL, 2 * LL, LL, me) <= lim, s, NEG)
            s_scr[r * LL : (r + 1) * LL, :] = s
            m = jnp.max(s, axis=0, keepdims=True)
            top = m if top is None else jnp.maximum(top, m)
        total, acc = None, None
        for r in range(n):
            w = jnp.exp(s_scr[r * LL : (r + 1) * LL, :] - top)
            t = jnp.sum(w, axis=0, keepdims=True)
            a = dot(v_ref[r * T : r * T + LL, c].T, w.astype(BF16))
            total = t if total is None else total + t
            acc = a if acc is None else acc + a
        acc = acc * (1.0 / total)
        o_ref[0:LL, c] = unstack_heads(acc, LL).astype(BF16)
        lse_l[p] = jnp.broadcast_to(top + jnp.log(total), (8, 2 * LL))
        for i in range(NS):
            off = LL + i * LS
            q2 = stack_heads(q_ref[off : off + LS, c], masks)
            kb = jnp.concatenate([k_ref[r * T + off : r * T + off + LS, c] for r in range(n)], 0)
            vb = jnp.concatenate([v_ref[r * T + off : r * T + off + LS, c] for r in range(n)], 0)
            s = dot_t(kb, q2)
            lim = limits(2 * LS, LS, me, info[1 + i], causal)
            s = jnp.where(key_positions(0, n * LS, 2 * LS, LS, me) <= lim, s, NEG)
            top = jnp.max(s, axis=0, keepdims=True)
            w = jnp.exp(s - top)
            total = jnp.sum(w, axis=0, keepdims=True)
            acc = dot(vb.T, w.astype(BF16)) * (1.0 / total)
            o_ref[off : off + LS, c] = unstack_heads(acc, LS).astype(BF16)
            lse_s[p * NS + i] = jnp.broadcast_to(top + jnp.log(total), (8, 2 * LS))

    loop(D // PAIR, pair)


def attend_backward(
    dims,
    causal,
    info,
    q_ref,
    k_ref,
    v_ref,
    o_ref,
    do_ref,
    lse_l,
    lse_s,
    dq_ref,
    dk_ref,
    dv_ref,
    first,
    last,
):
    T, LL, LS, NS, D, n = dims
    me = info[NS + 1]
    masks = head_masks(BF16)
    ones = jnp.ones((8, PAIR), F32)

    def row_dots(do2, o):
        prod = do2.astype(F32) * jnp.concatenate([o, o], 0).astype(F32)
        full = lax.dot_general(
            ones,
            prod,
            (((1,), (1,)), ((), ())),
            precision=lax.Precision.HIGHEST,
            preferred_element_type=F32,
        )
        return full[0:1]

    def pair(p):
        c = tile(p, PAIR)
        q2 = stack_heads(q_ref[0:LL, c], masks)
        do2 = stack_heads(do_ref[0:LL, c], masks)
        delta = row_dots(do2, o_ref[0:LL, c])
        lse = lse_l[p][0:1]
        lim = limits(2 * LL, LL, me, info[0], causal)
        dq_t = None
        for r in range(n):
            rows = slice(r * T, r * T + LL)
            kb, vb = k_ref[rows, c], v_ref[rows, c]
            s = dot_t(kb, q2)
            s = jnp.where(key_positions(r, LL, 2 * LL, LL, me) <= lim, s, NEG)
            probs = jnp.exp(s - lse)
            ds = (probs * (dot_t(vb, do2) - delta)).astype(BF16)
            dv_ref[rows, c] = dot(probs.astype(BF16), do2).astype(BF16)
            dk_ref[rows, c] = dot(ds, q2).astype(BF16)
            part = dot(kb.T, ds)
            dq_t = part if dq_t is None else dq_t + part
        dq_ref[0:LL, c] = (unstack_heads(dq_t, LL) * HD**-0.5).astype(BF16)
        for i in range(NS):
            off = LL + i * LS
            q2 = stack_heads(q_ref[off : off + LS, c], masks)
            do2 = stack_heads(do_ref[off : off + LS, c], masks)
            delta = row_dots(do2, o_ref[off : off + LS, c])
            lse = lse_s[p * NS + i][0:1]
            kb = jnp.concatenate([k_ref[r * T + off : r * T + off + LS, c] for r in range(n)], 0)
            vb = jnp.concatenate([v_ref[r * T + off : r * T + off + LS, c] for r in range(n)], 0)
            s = dot_t(kb, q2)
            lim = limits(2 * LS, LS, me, info[1 + i], causal)
            s = jnp.where(key_positions(0, n * LS, 2 * LS, LS, me) <= lim, s, NEG)
            probs = jnp.exp(s - lse)
            ds = (probs * (dot_t(vb, do2) - delta)).astype(BF16)
            dv = dot(probs.astype(BF16), do2).astype(BF16)
            dk = dot(ds, q2).astype(BF16)
            for r in range(n):
                dv_ref[r * T + off : r * T + off + LS, c] = dv[r * LS : (r + 1) * LS]
                dk_ref[r * T + off : r * T + off + LS, c] = dk[r * LS : (r + 1) * LS]
            dq_ref[off : off + LS, c] = (unstack_heads(dot(kb.T, ds), LS) * HD**-0.5).astype(BF16)

    lax.fori_loop(first, last, lambda i, c: (pair(i), c)[1], 0)


def flip(index, bit):
    return index + bit - 2 * bit * ((index // bit) % 2)


class Link:
    def __init__(self, send_sems, recv_sems):
        self.send_sems, self.recv_sems, self.used = send_sems, recv_sems, 0

    def start(self, src, dst, axis, bit):
        copy = pltpu.make_async_remote_copy(
            src_ref=src,
            dst_ref=dst,
            send_sem=self.send_sems.at[self.used],
            recv_sem=self.recv_sems.at[self.used],
            device_id={axis: flip(lax.axis_index(axis), bit)},
            device_id_type=pl.DeviceIdType.MESH,
        )
        self.used += 1
        copy.start()
        return copy


PATH_A = (("seq", 1), ("seq", 2), ("rep", 1))
PATH_B = (("seq", 1), ("rep", 1), ("seq", 2))
PATH_ROWS = (("seq", 1), ("seq", 2))
DP_BITS = (1, 2)
PATH_ALL = PATH_A + (("dp", 1), ("dp", 2))
TILE = 256
FFN_ROWS = 384
FEED_TASKS = ("u0", "u1", "u2", "w0", "w1", "w2")
FEED_ORDER = ("w0", "g0", "g1", "w1", "g2", "w2", "g3")
X_FIRST = ("u1", "u2", "w1", "w2", "s2")
PATHS = {
    kind + str(i): PATH_A if kind + str(i) in X_FIRST else PATH_B for kind in "uwcs" for i in range(3)
}
SELF_SLOTS = (1, 0, 2)
PLAN = (
    ("w0",),
    (),
    ("u0", "w0"),
    ("w1",),
    ("u1", "u0"),
    ("w2", "w1"),
    ("u2", "u1", "w2"),
    ("w0", "u2"),
    ("w1", "u0"),
    ("c0",),
    ("c0", "u1", "w1"),
    ("c1",),
    ("w1", "c1", "w2"),
    ("c2",),
    ("c0", "w0", "w1"),
    ("dm", "c2"),
    ("u1", "w0", "w1"),
    ("dm",),
    ("u2", "u1", "w0", "w1"),
    ("c1", "u0", "u1", "w2", "c0", "w0"),
    ("s0",),
    ("u0", "u1", "s0", "w2", "c2", "c0"),
    ("s1", "w0"),
    ("u0", "u2", "dm", "u1", "w2", "s1", "c0", "c1"),
    ("s2", "vec", "u0", "s0", "u2", "c2"),
    ("w2", "c1", "s2", "vec"),
    ("dx", "c0", "u0"),
    ("u2", "c2", "s0"),
    ("c1", "s1", "w2", "dx"),
)
FINAL = (
    "c0", "u2", "s0", "c2", "s2", "u2", "c1", "vec", "s0", "c2",
    "c1", "s1", "s2", "s0", "vec", "c2", "s1", "s2", "s1", "s0",
    "vec", "s2", "dx", "s1", "vec", "s1", "s2", "s2",
)


class Gather:
    def __init__(self, link, ref, rows):
        self.link, self.ref, self.rows = link, ref, rows

    def block(self, r, part=None):
        first, count = r * self.rows, self.rows
        if part is not None:
            count = self.rows // 2
            first = first + part * count
        return self.ref.at[first : first + count]

    def send_core(self):
        self.core = self.link.start(self.block(0), self.block(1), "seq", 1)

    def send_far(self):
        self.far = [
            self.link.start(self.block(0, p), self.block(2, p), "seq", 2) for p in range(2)
        ]

    def relay(self):
        self.relayed = []
        for p in range(2):
            self.far[p].wait()
            self.relayed.append(self.link.start(self.block(2, p), self.block(3, p), "seq", 1))

    def end(self):
        for copy in self.relayed:
            copy.wait()


def greet(pairs):
    barrier = pltpu.get_barrier_semaphore()
    for axis, bit in pairs:
        pl.semaphore_signal(
            barrier,
            inc=1,
            device_id={axis: flip(lax.axis_index(axis), bit)},
            device_id_type=pl.DeviceIdType.MESH,
        )
    pl.semaphore_wait(barrier, len(pairs))


def forward_kernel(dims, *refs):
    T, LL, LS, NS, D, n = dims
    refs = list(refs)

    def take(count):
        out = refs[:count]
        del refs[:count]
        return out

    long_len, short_len, xl, xs, ml, ms = take(6)
    info = row_info(long_len, short_len, NS)
    ws_hbm, wos_hbm, wc_hbm, woc_hbm, bias_s, bias_c, gain, shift = take(8)
    q1, k1_out, v1_out, o1, lse1l, lse1s, z1, t1_out = take(8)
    q2, k2_out, v2_out, o2, lse2l, lse2s, z2, t2_out = take(8)
    x, m, ws, wos, wc, woc, k1, v1, k2, v2, blk_t, s_scr, sems, send_sems, recv_sems = refs
    copies = Copies(sems)
    load_x = [copies.start(xl, x.at[0:LL]), copies.start(xs, x.at[LL:T])]
    load_ws = copies.start(ws_hbm, ws)
    load_m = [copies.start(ml, m.at[0:LL]), copies.start(ms, m.at[LL:T])]
    load_wc = copies.start(wc_hbm, wc)
    load_wos, load_woc = copies.start(wos_hbm, wos), copies.start(woc_hbm, woc)
    greet(PATH_ROWS)
    link = Link(send_sems, recv_sems)
    rows_x, rows_m = Gather(link, x, T), Gather(link, m, T)
    for item in load_x:
        item.wait()
    rows_x.send_far()
    rows_x.send_core()
    for item in load_m:
        item.wait()
    rows_m.send_core()

    def queries(source, w, bias, q):
        def body(j):
            c = tile(j, TILE)
            out = dot(source[0:T, :].astype(BF16), w[0, :, c]) + bias[0:1, c]
            q[:, c] = (out.astype(BF16).astype(F32) * HD**-0.5).astype(BF16)

        loop(D // TILE, body)

    def keys_values(source, w, bias, k, v, r):
        rows = slice(r * T, (r + 1) * T)

        def body(j):
            c = tile(j, TILE)
            k[rows, c] = dot(source[rows, :], w[1, :, c]).astype(BF16)
            v[rows, c] = (dot(source[rows, :], w[2, :, c]) + bias[1:2, c]).astype(BF16)

        loop(D // TILE, body)

    def residual(source, o, wo, bias, z):
        def body(j):
            c = tile(j, TILE)
            z[:, c] = source[0:T, c].astype(F32) + dot(o[...], wo[:, c]) + bias[2:3, c]

        loop(D // TILE, body)

    load_ws.wait()
    queries(x, ws, bias_s, q1)
    keys_values(x, ws, bias_s, k1, v1, 0)
    transpose_into(blk_t, x, T, D, 0)
    load_wc.wait()
    keys_values(m, wc, bias_c, k2, v2, 0)
    rows_x.core.wait()
    keys_values(x, ws, bias_s, k1, v1, 1)
    transpose_into(blk_t, x, T, D, T)
    rows_m.core.wait()
    keys_values(m, wc, bias_c, k2, v2, 1)
    rows_x.relay()
    rows_m.send_far()
    keys_values(x, ws, bias_s, k1, v1, 2)
    transpose_into(blk_t, x, T, D, 2 * T)
    rows_x.end()
    keys_values(x, ws, bias_s, k1, v1, 3)
    transpose_into(blk_t, x, T, D, 3 * T)
    stores = [copies.start(k1, k1_out), copies.start(v1, v1_out)]
    store_t = copies.start(blk_t, t1_out)
    attend_forward(dims, True, info, q1, k1, v1, o1, lse1l, lse1s, s_scr)
    load_wos.wait()
    residual(x, o1, wos, bias_s, z1)
    rows_m.relay()
    xhat, _ = norm_parts(z1[...])
    z2[...] = xhat * gain[0:1] + shift[0:1]
    queries(z2, wc, bias_c, q2)
    keys_values(m, wc, bias_c, k2, v2, 2)
    store_t.wait()
    for r in range(3):
        transpose_into(blk_t, m, T, D, r * T)
    rows_m.end()
    keys_values(m, wc, bias_c, k2, v2, 3)
    transpose_into(blk_t, m, T, D, 3 * T)
    stores += [copies.start(k2, k2_out), copies.start(v2, v2_out), copies.start(blk_t, t2_out)]
    attend_forward(dims, False, info, q2, k2, v2, o2, lse2l, lse2s, s_scr)
    load_woc.wait()
    residual(z2, o2, woc, bias_c, z2)
    for item in stores:
        item.wait()


def forward_call(dims, *operands):
    T, LL, LS, NS, D, n = dims
    pairs = D // PAIR
    full, own = (n * T, D), (T, D)
    outs = [
        jax.ShapeDtypeStruct(own, BF16),
        jax.ShapeDtypeStruct(full, BF16),
        jax.ShapeDtypeStruct(full, BF16),
        jax.ShapeDtypeStruct(own, BF16),
        jax.ShapeDtypeStruct((pairs, 8, 2 * LL), F32),
        jax.ShapeDtypeStruct((pairs * NS, 8, 2 * LS), F32),
        jax.ShapeDtypeStruct(own, F32),
        jax.ShapeDtypeStruct((D, n * T), BF16),
    ]
    return pl.pallas_call(
        functools.partial(forward_kernel, dims),
        out_shape=outs + outs,
        in_specs=[SMEM] * 2 + [HBM] * 8 + [VMEM] * 4,
        out_specs=[VMEM, HBM, HBM, VMEM, VMEM, VMEM, VMEM, HBM] * 2,
        scratch_shapes=[pltpu.VMEM(full, BF16)] * 2
        + [pltpu.VMEM((3, D, D), BF16), pltpu.VMEM((D, D), BF16)] * 2
        + [pltpu.VMEM(full, BF16)] * 4
        + [
            pltpu.VMEM((D, n * T), BF16),
            pltpu.VMEM((n * LL, 2 * LL), F32),
            pltpu.SemaphoreType.DMA((16,)),
            pltpu.SemaphoreType.DMA((10,)),
            pltpu.SemaphoreType.DMA((10,)),
        ],
        compiler_params=pltpu.CompilerParams(
            collective_id=1, has_side_effects=True, vmem_limit_bytes=58 * MIB
        ),
        cost_estimate=pl.CostEstimate(
            flops=20 * 10**9, bytes_accessed=40 * 10**6, transcendentals=8 * 10**6
        ),
        name="forward",
    )(*operands)


def feed_phase(dims, loads, copies, data, scratch, vec, store_task, outs, tick):
    T, LL, LS, NS, D, n = dims
    upb, downb, gain, shift = data
    zb, acc, wu, wd, low, h2t, block, gp, act_t, dy_ref, y_ref = scratch
    tiles = D // TILE
    groups = len(wu)
    rows = D // 8
    loads["z2"].wait()
    xhat2, _ = norm_parts(zb[...])
    h2 = xhat2 * gain[1:2] + shift[1:2]
    low[...] = h2.astype(BF16)
    acc[...] = h2 + downb[...]
    transpose_into(h2t, low, T, D)

    def up_tile(q, t):
        c = tile(t, TILE)
        u = dot(low[...], wu[q][:, c]) + upb[:, q * D + t * TILE : q * D + (t + 1) * TILE]
        sq = u * u
        th = jnp.tanh(0.7978845608028654 * u * (1.0 + 0.044715 * sq))
        half = 0.5 * (1.0 + th)
        act = (u * half).astype(BF16)
        block[:, c] = act
        act_t[tile(t, TILE), q * T : (q + 1) * T] = act.T
        slope = half + (0.5 * 0.7978845608028654) * u * (1.0 - th * th) * (
            1.0 + (3.0 * 0.044715) * sq
        )
        gp[q * tiles + t] = slope.astype(BF16)

    def down_tile(q, j):
        c = tile(j, TILE)
        acc[:, c] += dot(block[...], wd[q][:, c])

    for q in range(groups):
        loads["up", q].wait()
        loop(tiles, functools.partial(up_tile, q))
        loads["down", q].wait()
        loop(tiles, functools.partial(down_tile, q))
    xhat3, rstd3 = norm_parts(acc[...])
    y_ref[...] = (xhat3 * gain[2:3] + shift[2:3]).astype(BF16)
    stores = [copies.start(y_ref.at[0:LL], outs[0]), copies.start(y_ref.at[LL:T], outs[1])]
    for item in loads["dy"]:
        item.wait()
    dy = dy_ref[...].astype(F32)
    vec[8:9] = col_sum(dy * xhat3)
    vec[11:12] = col_sum(dy)
    dz3 = norm_back(dy, gain[2:3], xhat3, rstd3)
    low[...] = dz3.astype(BF16)
    acc[...] = dz3
    vec[12:13] = col_sum(low[...])

    def down_grad(t):
        size = 4 * rows
        parts = []
        for q in range(groups):
            value = dot(act_t[:, q * T : (q + 1) * T], low[:, t * TILE : (t + 1) * TILE])
            value = value.astype(BF16)
            parts += [(None, 0, value[i : i + size]) for i in range(0, D, size)]
        store_task(tiles + t, parts)

    def back_tile(j, q):
        c = tile(j, TILE)
        acc[:, c] += dot_t(block[...], wu[q][c, :])

    def up_grad(q):
        for t in range(tiles):
            c = slice(t * TILE, (t + 1) * TILE)
            j = q * tiles + t
            du = (gp[j].astype(F32) * dot_t(low[...], wd[q][c, :])).astype(BF16)
            vec[13 + q : 14 + q, c] = col_sum(du)
            block[:, c] = du
            value = dot(h2t[...], du).astype(BF16)
            store_task(
                j // 4, [(i, (j % 4) * rows, value[i * rows : (i + 1) * rows]) for i in range(8)]
            )
        for t in range(tiles):
            back_tile(t, q)

    for step in FEED_ORDER:
        if step[0] == "w":
            down_grad(int(step[1]))
        else:
            up_grad(int(step[1]))
        tick()
    dh2 = acc[...]
    xhat2, rstd2 = norm_parts(zb[...])
    vec[7:8] = col_sum(dh2 * xhat2)
    vec[10:11] = col_sum(dh2)
    acc[...] = norm_back(dh2, gain[1:2], xhat2, rstd2)
    for item in stores:
        item.wait()


def backward_phase(dims, cross, chunks, info, loads, data, scratch, vec, orders, tick, free):
    T, LL, LS, NS, D, n = dims
    dz, z_in, gain, shift, lse_l, lse_s = data
    q, o, w, wo, k, v, dq, do, da, blk_t, o_t, src_t, dblk, grads = scratch
    rows = D // chunks
    base = 3 if cross else 0

    def weight_grad(i, slot, lhs_t, rhs):
        grad = dot(lhs_t, rhs).astype(BF16)
        out = grads.at[i].reshape(chunks, 4 * rows, TILE)
        for s in range(chunks):
            out[orders[i][s], slot * rows : (slot + 1) * rows, :] = grad[s * rows : (s + 1) * rows]

    da[...] = dz[...].astype(BF16)
    vec[base + 2 : base + 3] = col_sum(da[...])
    loads["o"].wait()
    transpose_into(o_t, o, T, D)
    loads["wo"].wait()
    for i in range(D // TILE):
        c = slice(i * TILE, (i + 1) * TILE)
        do[:, c] = dot_t(da[...], wo[c, :]).astype(BF16)
        weight_grad(i, 0, o_t[...], da[:, c])
    free("wo")
    if cross:
        xhat, _ = norm_parts(z_in[...])
        da[...] = (xhat * gain[0:1] + shift[0:1]).astype(BF16)
        transpose_into(src_t, da, T, D)
    tick()
    for name in ("q", "k", "v", "t"):
        loads[name].wait()
    if not cross:
        src_t[...] = blk_t[:, 0:T]
    pairs = TILE // PAIR
    for i in range(D // TILE):
        c = slice(i * TILE, (i + 1) * TILE)
        attend_backward(
            dims, not cross, info, q, k, v, o, do, lse_l, lse_s, dq, k, v, pairs * i, pairs * (i + 1)
        )
        tick()
        vec[base : base + 1, c] = col_sum(dq[:, c])
        vec[base + 1 : base + 2, c] = col_sum(v[:, c])
        weight_grad(i, 1, src_t[...], dq[:, c])
        weight_grad(i, 2, blk_t[...], k[:, c])
        weight_grad(i, 3, blk_t[...], v[:, c])
        tick()
    for name in ("q", "o", "t"):
        free(name)
    loads["w"].wait()
    free("dblk")

    def dblk_tile(i, at, j):
        c = tile(j, TILE)
        rows_in = slice(i * T, (i + 1) * T)
        part = dot_t(k[rows_in, :], w[1, c, :]) + dot_t(v[rows_in, :], w[2, c, :])
        if i == 0:
            part_q = dz[:, c] + dot_t(dq[...], w[0, c, :])
            if cross:
                dz[:, c] = part_q
            else:
                part = part + part_q
        dblk[at * T : (at + 1) * T, c] = part.astype(BF16)

    kept_first = sorted(range(n), key=lambda r: (r % 2, r // 2))
    for at in reversed(range(n)):
        loop(D // TILE, functools.partial(dblk_tile, kept_first[at], at))
        if at > 0:
            tick()
    for name in ("k", "v", "w"):
        free(name)
    tick()
    if cross:
        dh = dz[...]
        xhat, rstd = norm_parts(z_in[...])
        vec[6:7] = col_sum(dh * xhat)
        vec[9:10] = col_sum(dh)
        dz[...] = norm_back(dh, gain[0:1], xhat, rstd)


def add_rows(dst, dst_at, a, a_at, b, b_at, count, step=96):
    def body(i):
        def at(start):
            return pl.ds(pl.multiple_of(start + i * step, 16), step)

        total = a[at(a_at), :].astype(F32) + b[at(b_at), :].astype(F32)
        dst[at(dst_at), :] = total.astype(dst.dtype)

    loop(count // step, body)


class Share:
    def __init__(self, link, theirs, acc, recv, res, size, path, dp_bits):
        self.link, self.theirs, self.acc, self.recv, self.res = link, theirs, acc, recv, res
        self.size, self.path, self.dp_bits = size, path, dp_bits
        self.stage, self.copy, self.at = 0, None, 0
        self.off, self.count = 0, size
        self.kept, self.last = [], len(path) + 2 * len(dp_bits)

    def advance(self):
        stage, path, dp_bits = self.stage, self.path, self.dp_bits
        if stage > self.last:
            return
        self.stage += 1
        halves = len(path)
        if stage == 0:
            rows = self.size << (halves - 1)
            self.land, self.rows = self.at, rows
            self.at += rows
            land = self.recv.at[0:rows]
            if len(self.theirs.shape) == 3:
                land = land.reshape(*self.theirs.shape)
            self.copy = self.link.start(self.theirs, land, *path[0])
            return
        self.copy.wait()
        if stage <= halves + len(dp_bits):
            last = stage == halves + len(dp_bits)
            dst = self.res if last else self.acc
            add_rows(dst, self.off, self.acc, self.off, self.recv, self.land, self.rows, 48)
        if stage < halves:
            rows = self.size << (halves - 1 - stage)
            self.land, self.rows = self.at, rows
            self.at += rows
            src = self.acc.at[rows : 2 * rows]
            dst = self.recv.at[self.land : self.land + rows]
            self.copy = self.link.start(src, dst, *path[stage])
        elif stage < halves + len(dp_bits):
            bit = dp_bits[stage - halves]
            mine = (lax.axis_index("dp") // bit) % 2
            self.count //= 2
            give = self.off + (1 - mine) * self.count
            self.off = self.off + mine * self.count
            self.kept.append((self.off, self.count, bit))
            self.land, self.rows = self.at, self.count
            self.at += self.count
            src = self.acc.at[pl.ds(pl.multiple_of(give, 16), self.count)]
            dst = self.recv.at[self.land : self.land + self.count]
            self.copy = self.link.start(src, dst, "dp", bit)
        elif self.kept:
            off, count, bit = self.kept.pop()
            part = self.res.at[pl.ds(pl.multiple_of(off, 16), count)]
            self.copy = self.link.start(part, part, "dp", bit)


class Rows:
    def __init__(self, link, copies, blocks, recv, lands, out, size, path):
        self.link, self.copies, self.blocks, self.recv, self.out = link, copies, blocks, recv, out
        self.size, self.path, self.stage, self.lands, self.last = size, path, 0, lands, len(path)

    def advance(self):
        stage, path = self.stage, self.path
        if stage > self.last:
            return
        self.stage += 1
        if stage > 0:
            self.copy.wait()
            add_rows(self.blocks, 0, self.blocks, 0, self.recv, self.land, self.rows)
        if stage == len(path):
            self.store = self.copies.start(self.blocks.at[0 : self.rows], self.out)
        if stage < len(path):
            rows = self.size << (len(path) - 1 - stage)
            self.land, self.rows = self.lands[stage], rows
            src = self.blocks.at[rows : 2 * rows]
            dst = self.recv.at[self.land : self.land + rows]
            self.copy = self.link.start(src, dst, *path[stage])


class Small:
    def __init__(self, link, vec, recv, path):
        self.link, self.vec, self.recv, self.path, self.stage = link, vec, recv, path, 0
        self.last = len(path)

    def advance(self):
        stage, path = self.stage, self.path
        if stage > self.last:
            return
        self.stage += 1
        if stage > 0:
            self.copy.wait()
            self.vec[stage] = self.vec[stage - 1] + self.recv[stage - 1]
        if stage < len(path):
            self.copy = self.link.start(self.vec.at[stage], self.recv.at[stage], *path[stage])


def inner_place(path, s):
    x = (s // 4 + lax.axis_index("seq") // 2) % 2
    y = (s + lax.axis_index("rep")) % 2
    return x * 2 + y if path is PATH_A else y * 2 + x


def xor_order(path, chunks):
    core = lax.axis_index("seq")
    return [(s // 2 + core) % 2 * (chunks // 2) + inner_place(path, s) for s in range(chunks)]


def backward_kernel(dims, linked, *refs):
    T, LL, LS, NS, D, n = dims
    chunks = 8
    half = chunks // 2
    size = FFN_ROWS
    tiles = D // TILE
    refs = list(refs)

    def take(count):
        out = refs[:count]
        del refs[:count]
        return out

    long_len, short_len = take(2)
    info = row_info(long_len, short_len, NS)
    z2_hbm, z1_hbm, cot_l, cot_s, wup_hbm, wdown_hbm = take(6)
    cross_hbm, self_hbm = take(7), take(7)
    upb, downb, gain, shift, lse2l, lse2s, lse1l, lse1s = take(8)
    yl_out, ys_out = take(2)
    if linked:
        shares_out, dm_out, dx_out, vec_out = take(4)
    else:
        gf_out, gc_out, gs_out, dm_out, dx_out, vec_out = take(6)
    q, o, w, wo, k, v, dq, do, da, blk_t, o_t, src_t, dblk, dres, zb = take(15)
    gc, gs, accs, vec, sems = take(5)
    if linked:
        recvs, rows_recv, res, vec_recv, send_sems, recv_sems = take(6)

    copies = Copies(sems)
    homes = {"wo": wo, "o": o, "q": q, "k": k, "v": v, "t": blk_t, "w": w}
    sources_c = dict(zip(("w", "wo", "k", "v", "q", "o", "t"), cross_hbm))
    sources_s = dict(zip(("w", "wo", "k", "v", "q", "o", "t"), self_hbm))
    wu = [(k, v)[i // 2].at[(i % 2) * D : (i % 2 + 1) * D] for i in range(4)]
    wd = [w.at[0], w.at[1], w.at[2], dblk.at[0:D]]
    loads_f = {"z2": copies.start(z2_hbm, zb)}
    for i in range(4):
        loads_f["up", i] = copies.start(wup_hbm.at[:, i * D : (i + 1) * D], wu[i])
        loads_f["down", i] = copies.start(wdown_hbm.at[i * D : (i + 1) * D], wd[i])
    loads_f["dy"] = [copies.start(cot_l, do.at[0:LL]), copies.start(cot_s, do.at[LL:T])]
    loads_c = {name: copies.start(sources_c[name], homes[name]) for name in ("o", "wo")}
    vec[0] = jnp.zeros((VEC_ROWS, D), F32)

    def theirs(i):
        return gs.at[i // 2, (i % 2) * half * size : (i % 2 + 1) * half * size]

    tasks = {}
    steps = iter(PLAN)

    def tick():
        if linked:
            for name in next(steps):
                tasks[name].advance()

    if linked:
        greet(PATH_ALL)
        link = Link(send_sems, recv_sems)
        for i, name in enumerate(FEED_TASKS):
            tasks[name] = Share(
                link, theirs(i), accs.at[i], recvs.at[i], res.at[i], size, PATHS[name], DP_BITS
            )
        for i in range(tiles):
            for kind, g, first, slot in (("c", gc, 6, 6 + i), ("s", gs, 9, SELF_SLOTS[i])):
                name = kind + str(i)
                tasks[name] = Share(
                    link, g.at[i, half * size :], g.at[i], recvs.at[slot], res.at[first + i],
                    size, PATHS[name], DP_BITS,
                )
        tasks["dm"] = Rows(link, copies, dblk, rows_recv, (0, 2 * T), dm_out, T, PATH_ROWS)
        tasks["dx"] = Rows(link, copies, dblk, rows_recv, (0, 3 * T), dx_out, T, PATH_ROWS)
        tasks["vec"] = Small(link, vec, vec_recv, PATH_ALL)
        orders_c = [xor_order(PATHS["c" + str(i)], chunks) for i in range(tiles)]
        orders_s = [xor_order(PATHS["s" + str(i)], chunks) for i in range(tiles)]
    else:
        orders_c = orders_s = [list(range(chunks))] * tiles

    side = lax.axis_index("seq") % 2

    def store_task(i, parts):
        for s in range(chunks):
            if s // 2 % 2:
                continue
            (_, off, low_part), (_, _, high_part) = parts[s], parts[s + 2]
            if linked:
                place = inner_place(PATHS[FEED_TASKS[i]], s)
                at = pl.multiple_of(place * size + off, 16)
                rows = pl.ds(at, low_part.shape[0])
                accs[i, rows, :] = jnp.where(side == 0, low_part, high_part)
                theirs(i)[rows, :] = jnp.where(side == 0, high_part, low_part)
            else:
                for c, part in ((s, low_part), (s + 2, high_part)):
                    out = accs.at[i] if c < half else theirs(i)
                    at = c % half * size + off
                    out[at : at + part.shape[0], :] = part

    feed_phase(
        dims, loads_f, copies, (upb, downb, gain, shift),
        (zb, dres, wu, wd, da, src_t, q, gc.reshape(chunks * tiles, T, TILE), blk_t, do, dq),
        vec.at[0], store_task, (yl_out, ys_out), tick,
    )
    load_z1 = copies.start(z1_hbm, zb)
    for name in ("q", "k", "v", "t", "w"):
        loads_c[name] = copies.start(sources_c[name], homes[name])
    load_z1.wait()
    if not linked:
        for i in range(2 * tiles):
            copies.start(accs.at[i], gf_out.at[i, 0]).wait()
            copies.start(theirs(i), gf_out.at[i, 1]).wait()
    loads_s = {}

    def free_cross(name):
        if name in homes:
            loads_s[name] = copies.start(sources_s[name], homes[name])

    def free_self(name):
        if linked and name == "dblk":
            while tasks["dm"].stage <= tasks["dm"].last:
                tasks["dm"].advance()
            tasks["dm"].store.wait()

    backward_phase(
        dims, True, chunks, info, loads_c, (dres, zb, gain, shift, lse2l, lse2s),
        (q, o, w, wo, k, v, dq, do, da, blk_t, o_t, src_t, dblk, gc), vec.at[0], orders_c, tick,
        free_cross,
    )
    if not linked:
        stores = [copies.start(gc, gc_out)]
        copies.start(dblk, dm_out).wait()
    backward_phase(
        dims, False, chunks, info, loads_s, (dres, None, None, None, lse1l, lse1s),
        (q, o, w, wo, k, v, dq, do, da, blk_t, o_t, src_t, dblk, gs), vec.at[0], orders_s, tick,
        free_self,
    )
    if linked:
        for name in FINAL:
            tasks[name].advance()
        for task in tasks.values():
            while task.stage <= task.last:
                task.advance()
        copies.start(res, shares_out).wait()
        tasks["dx"].store.wait()
        vec_out[...] = vec[len(PATH_ALL)]
    else:
        vec_out[...] = vec[0]
        stores += [copies.start(gs, gs_out), copies.start(dblk, dx_out)]
        for item in stores:
            item.wait()


def backward_call(dims, linked, info, feed_hbm, cross_hbm, self_hbm, small):
    T, LL, LS, NS, D, n = dims
    full, own = (n * T, D), (T, D)
    tiles = D // TILE
    size = FFN_ROWS
    grads = (tiles, 8 * size, TILE)
    vec = jax.ShapeDtypeStruct((VEC_ROWS, D), F32)
    steps = len(PATH_ALL)
    out_shape = [jax.ShapeDtypeStruct((LL, D), BF16), jax.ShapeDtypeStruct((T - LL, D), BF16)]
    if linked:
        out_shape += [
            jax.ShapeDtypeStruct((4 * tiles, size, TILE), BF16),
            jax.ShapeDtypeStruct(own, BF16),
            jax.ShapeDtypeStruct(own, BF16),
            vec,
        ]
        landing = 7 * size + 3 * size // 4
        count = 4 * tiles * 7 + 4 + steps
        extra = [
            pltpu.VMEM((3 * tiles, landing, TILE), BF16),
            pltpu.VMEM((4 * T, D), BF16),
            pltpu.VMEM((4 * tiles, size, TILE), BF16),
            pltpu.VMEM((steps, VEC_ROWS, D), F32),
            pltpu.SemaphoreType.DMA((count,)),
            pltpu.SemaphoreType.DMA((count,)),
        ]
    else:
        out_shape += [
            jax.ShapeDtypeStruct((2 * tiles, 2, 4 * size, TILE), BF16),
            jax.ShapeDtypeStruct(grads, BF16),
            jax.ShapeDtypeStruct(grads, BF16),
            jax.ShapeDtypeStruct(full, BF16),
            jax.ShapeDtypeStruct(full, BF16),
            vec,
        ]
        extra = []
    params = {"collective_id": 0} if linked else {}
    return pl.pallas_call(
        functools.partial(backward_kernel, dims, linked),
        out_shape=out_shape,
        in_specs=[SMEM] * 2 + [HBM] * 20 + [VMEM] * 8,
        out_specs=[HBM] * (len(out_shape) - 1) + [VMEM],
        scratch_shapes=[
            pltpu.VMEM(own, BF16),
            pltpu.VMEM(own, BF16),
            pltpu.VMEM((3, D, D), BF16),
            pltpu.VMEM((D, D), BF16),
            pltpu.VMEM(full, BF16),
            pltpu.VMEM(full, BF16),
            pltpu.VMEM(own, BF16),
            pltpu.VMEM(own, BF16),
            pltpu.VMEM(own, BF16),
            pltpu.VMEM((D, n * T), BF16),
            pltpu.VMEM((D, T), BF16),
            pltpu.VMEM((D, T), BF16),
            pltpu.VMEM(full, BF16),
            pltpu.VMEM(own, F32),
            pltpu.VMEM(own, F32),
            pltpu.VMEM(grads, BF16),
            pltpu.VMEM(grads, BF16),
            pltpu.VMEM((2 * tiles, 4 * size, TILE), BF16),
            pltpu.VMEM((steps + 1, VEC_ROWS, D), F32),
            pltpu.SemaphoreType.DMA((48,)),
        ]
        + extra,
        compiler_params=pltpu.CompilerParams(
            vmem_limit_bytes=60 * MIB, has_side_effects=True, **params
        ),
        cost_estimate=pl.CostEstimate(
            flops=100 * 10**9, bytes_accessed=60 * 10**6, transcendentals=8 * 10**6
        ),
        name="backward",
    )(*info, *feed_hbm, *cross_hbm, *self_hbm, *small)


def finish_kernel(dims, mesh_sizes, yl, ys, shares_hbm, dm, dx, vec_hbm, *refs):
    T, LL, LS, NS, D, n = dims
    *outs, shares, vec, sems = refs
    (
        y_l, y_s, dx_l, dx_s, dm_l, dm_s, g_self, g_selfout, b_self, g_cross, g_crossout, b_cross,
        g_gain, g_shift, g_up, b_up, g_down, b_down,
    ) = outs
    shards = mesh_sizes[1] * mesh_sizes[2]
    mine = lax.axis_index("seq") * mesh_sizes[2] + lax.axis_index("rep")
    copies = Copies(sems)
    load_vec, load_shares = copies.start(vec_hbm, vec), copies.start(shares_hbm, shares)
    pairs = ((yl, y_l), (ys, y_s), (dx.at[0:LL], dx_l), (dx.at[LL:T], dx_s), (dm.at[0:LL], dm_l), (dm.at[LL:T], dm_s))
    moves = [copies.start(src, dst) for src, dst in pairs]
    load_shares.wait()
    rows = D // shards
    for t in range(D // TILE):
        c = slice(t * TILE, (t + 1) * TILE)
        for i in range(4):
            part = slice(i * rows, (i + 1) * rows)
            j = 4 * t + i
            g_up[:, j * TILE : (j + 1) * TILE] = shares[t, part, :].astype(F32)
            for first, whole, alone in ((6, g_cross, g_crossout), (9, g_self, g_selfout)):
                value = shares[first + t, part, :].astype(F32)
                if i == 0:
                    alone[:, c] = value
                else:
                    whole[i - 1, :, c] = value
        g_down[:, c] = shares[3 + t].astype(F32)
    load_vec.wait()
    turned = pltpu.roll(vec[...], D - mine * rows, 1)
    for i, out in enumerate((b_self, b_cross, g_gain, g_shift)):
        out[...] = turned[3 * i : 3 * i + 3, 0:rows]
    b_down[...] = turned[12:13, 0:rows]
    ups = vec[13:14, :]
    per_row = D // (4 * rows)
    for i in range(1, 4):
        ups = jnp.where(mine // per_row == i, vec[13 + i : 14 + i, :], ups)
    out = ups[:, 0 : 4 * rows]
    for i in range(1, per_row):
        out = jnp.where(mine % per_row == i, ups[:, i * 4 * rows : (i + 1) * 4 * rows], out)
    b_up[...] = out
    for item in moves:
        item.wait()


def finish_call(dims, sizes, yl, ys, shares, dm, dx, vec):
    T, LL, LS, NS, D, n = dims
    rows = D // (sizes[1] * sizes[2])

    def shape(*dims):
        return jax.ShapeDtypeStruct(dims, F32)

    tokens = [jax.ShapeDtypeStruct((LL, D), BF16), jax.ShapeDtypeStruct((T - LL, D), BF16)]
    out_shape = tokens + tokens + tokens + [
        shape(3, rows, D), shape(rows, D), shape(3, rows), shape(3, rows, D), shape(rows, D),
        shape(3, rows), shape(3, rows), shape(3, rows), shape(rows, 4 * D), shape(1, 4 * rows),
        shape(4 * rows, D), shape(1, rows),
    ]
    return pl.pallas_call(
        functools.partial(finish_kernel, dims, sizes),
        out_shape=out_shape,
        in_specs=[HBM] * 6,
        out_specs=[VMEM] * len(out_shape),
        scratch_shapes=[
            pltpu.VMEM(shares.shape, BF16),
            pltpu.VMEM(vec.shape, F32),
            pltpu.SemaphoreType.DMA((8,)),
        ],
        compiler_params=pltpu.CompilerParams(vmem_limit_bytes=58 * MIB),
        name="finish",
    )(yl, ys, shares, dm, dx, vec)


def swap(a, axis, bit, size):
    return lax.ppermute(a, axis, [(i, i ^ bit) for i in range(size)])


def bits_of(size):
    return [1 << i for i in range(size.bit_length() - 1)]


def add_low(a, b):
    return (a.astype(F32) + b.astype(F32)).astype(BF16)


def halve(a, steps):
    for axis, bit, size in steps:
        half = a.shape[0] // 2
        a = add_low(a[:half], swap(a[half:], axis, bit, size))
    return a[0]


def all_sum(a, axis, size):
    rows, cols = a.shape
    me = lax.axis_index(axis)
    steps = bits_of(size)
    sent = []
    for bit in steps:
        mine = (me // bit) % 2
        a = a.reshape(2, a.shape[0] // 2, cols)
        keep = lax.dynamic_index_in_dim(a, mine, 0, keepdims=False)
        give = lax.dynamic_index_in_dim(a, 1 - mine, 0, keepdims=False)
        a = add_low(keep, swap(give, axis, bit, size))
        sent.append(mine)
    for bit, mine in zip(reversed(steps), reversed(sent)):
        other = swap(a, axis, bit, size)
        first = jnp.where(mine == 0, a, other)
        second = jnp.where(mine == 0, other, a)
        a = jnp.concatenate([first, second], axis=0)
    return a.reshape(rows, cols)


def on_device(
    sizes,
    long_rows,
    short_rows,
    long_memory,
    short_memory,
    long_cotangent,
    short_cotangent,
    long_lengths,
    short_lengths,
    self_qkv,
    self_out,
    self_bias,
    cross_qkv,
    cross_out,
    cross_bias,
    norm_gain,
    norm_bias,
    up_proj,
    up_bias,
    down_proj,
    down_bias,
):
    n_dp, n, n_rep = sizes
    count_l, LL, D = long_rows.shape
    NS, LS, _ = short_rows.shape
    FF = up_proj.shape[1]
    T = LL + NS * LS
    dims = (T, LL, LS, NS, D, n)
    shards = n * n_rep

    def flat(a):
        return a.reshape(-1, D)

    me = lax.axis_index("seq")
    mine = me * n_rep + lax.axis_index("rep")
    info = (long_lengths, short_lengths)

    linked = (n_dp, n, n_rep) == (4, 4, 2)

    norm = (norm_gain, norm_bias)
    outs = forward_call(
        dims, *info, flat(long_rows), flat(short_rows), flat(long_memory), flat(short_memory),
        self_qkv, self_out, cross_qkv, cross_out, self_bias, cross_bias, *norm,
    )
    q1, k1, v1, o1, lse1l, lse1s, z1, xt = outs[:8]
    q2, k2, v2, o2, lse2l, lse2s, z2, mt = outs[8:]
    y_l, y_s, *results = backward_call(
        dims,
        linked,
        info,
        (z2, z1, flat(long_cotangent), flat(short_cotangent), up_proj, down_proj),
        (cross_qkv, cross_out, k2, v2, q2, o2, mt),
        (self_qkv, self_out, k1, v1, q1, o1, xt),
        (up_bias[None], down_bias[None], *norm, lse2l, lse2s, lse1l, lse1s),
    )
    rows = D // shards
    if linked:
        shares, dm, dx, small = results
        rest = finish_call(dims, sizes, y_l, y_s, shares, dm, dx, small)
        tokens, rest = rest[:6], list(rest[6:])
        rest[9], rest[11] = rest[9][0], rest[11][0]
        shapes = (long_rows.shape, short_rows.shape) * 3
        return tuple(a.reshape(b) for a, b in zip(tokens, shapes)) + tuple(rest)
    gf, gc, gs, dm, dx, small = results
    chunks = 8
    index = jnp.arange(shards, dtype=jnp.int32) ^ mine
    rel_seq, rel_rep = index // n_rep, index % n_rep
    core, rest = rel_seq % 2, rel_seq // 2
    pos_a = core * (shards // 2) + rest * n_rep + rel_rep
    pos_b = core * (shards // 2) + rel_rep * (n // 2) + rest
    steps_core = [("seq", 1, n)]
    steps_x = [("seq", bit, n) for bit in reversed(bits_of(n)[1:])]
    steps_y = [("rep", bit, n_rep) for bit in reversed(bits_of(n_rep))]

    def reduce_all(a, pos, steps):
        parts = a.reshape(shards, a.shape[0] // shards, a.shape[1])
        parts = jnp.zeros_like(parts).at[pos].set(parts)
        return all_sum(halve(parts, steps), "dp", n_dp)

    order_a = (pos_a, steps_core + steps_x + steps_y)
    order_b = (pos_b, steps_core + steps_y + steps_x)
    split = (D // TILE, chunks, 4, D // chunks, TILE)
    g_up = gf[: D // TILE].reshape(split).transpose(1, 3, 0, 2, 4).reshape(D, FF)
    g_down = gf[D // TILE :].reshape(D // TILE, chunks, FF // chunks, TILE)
    up_share = reduce_all(g_up, *order_a)
    down_share = reduce_all(g_down.transpose(1, 2, 0, 3).reshape(FF, D), *order_b)

    def four(g):
        mats = g.reshape(split).transpose(2, 1, 3, 0, 4).reshape(4, D, D)
        return jnp.stack([reduce_all(mats[i], *order_a) for i in range(4)])

    cross_share, self_share = four(gc), four(gs)
    seq_steps = [("seq", bit, n) for bit in bits_of(n)]
    dm = dm.reshape(n, T, D)
    dx = dx.reshape(n, T, D)
    dm = halve(dm, seq_steps)
    dx = halve(dx, seq_steps)
    small = lax.psum(small, ("dp", "seq", "rep"))

    def part(a, width):
        return lax.dynamic_slice_in_dim(a, mine * width, width, axis=-1)

    vecs = part(small[0:13], D // shards)
    upb_grad = part(small[13:17].reshape(-1), FF // shards)

    def unflat(a):
        return (
            a[:LL].reshape(count_l, LL, D),
            a[LL:].reshape(NS, LS, D),
        )

    y_l, y_s = y_l.reshape(long_rows.shape), y_s.reshape(short_rows.shape)
    dx_l, dx_s = unflat(dx)
    dm_l, dm_s = unflat(dm)
    cross_grad = cross_share.astype(F32)
    self_grad = self_share.astype(F32)
    return (
        y_l,
        y_s,
        dx_l,
        dx_s,
        dm_l,
        dm_s,
        self_grad[1:4],
        self_grad[0],
        vecs[0:3],
        cross_grad[1:4],
        cross_grad[0],
        vecs[3:6],
        vecs[6:9],
        vecs[9:12],
        up_share.astype(F32),
        upb_grad,
        down_share.astype(F32),
        vecs[12],
    )


def solution(mesh):
    rows = P(("dp", "rep"), "seq", None)
    lengths = P(("dp", "rep"))
    share = ("seq", "rep")
    in_specs = (rows,) * 6 + (lengths,) * 2 + (P(),) * 12
    out_specs = (rows,) * 6 + (
        P(None, share, None),
        P(share, None),
        P(None, share),
        P(None, share, None),
        P(share, None),
        P(None, share),
        P(None, share),
        P(None, share),
        P(share, None),
        P(share),
        P(share, None),
        P(share),
    )
    sizes = (mesh.shape["dp"], mesh.shape["seq"], mesh.shape["rep"])
    return jax.shard_map(
        functools.partial(on_device, sizes),
        mesh=mesh,
        in_specs=in_specs,
        out_specs=out_specs,
        check_vma=False,
    )
```

```python
import functools

import jax
import jax.numpy as jnp
from jax import lax
from jax.experimental import pallas as pl
from jax.experimental.pallas import tpu as pltpu
from jax.sharding import PartitionSpec as P

HD = 64
PAIR = 2 * HD
F32 = jnp.float32
BF16 = jnp.bfloat16
NEG = -1000000000.0
MIB = 1024 * 1024
VEC_ROWS = 24

HBM = pl.BlockSpec(memory_space=pltpu.HBM)
VMEM = pl.BlockSpec(memory_space=pltpu.VMEM)
SMEM = pl.BlockSpec(memory_space=pltpu.SMEM)


def dot(a, b):
    return jnp.dot(a, b, preferred_element_type=F32)


def dot_t(a, b):
    return lax.dot_general(a, b, (((1,), (1,)), ((), ())), preferred_element_type=F32)


def loop(count, body, first=0):
    if count <= 3 and first == 0:
        for i in range(count):
            body(i)
        return
    lax.fori_loop(first, count, lambda i, c: (body(i), c)[1], 0)


def tile(j, width):
    if isinstance(j, int):
        return pl.ds(j * width, width)
    return pl.ds(pl.multiple_of(j * width, width), width)


def norm_parts(z):
    center = z - jnp.mean(z, axis=-1, keepdims=True)
    rstd = lax.rsqrt(jnp.mean(center * center, axis=-1, keepdims=True) + 1e-05)
    return center * rstd, rstd


def norm_back(dy, gain, xhat, rstd):
    dyg = dy * gain
    mean_a = jnp.mean(dyg, axis=-1, keepdims=True)
    mean_b = jnp.mean(dyg * xhat, axis=-1, keepdims=True)
    return rstd * (dyg - mean_a - xhat * mean_b)


def col_sum(a):
    return jnp.sum(a.astype(F32), axis=0, keepdims=True)


def transpose_into(dst_ref, src_ref, rows, cols, row_off=0):
    def body(j):
        dst_ref[tile(j, 128), row_off : row_off + rows] = src_ref[
            row_off : row_off + rows, tile(j, 128)
        ].T

    loop(cols // 128, body)


class Copies:
    def __init__(self, sems):
        self.sems, self.used = sems, 0

    def start(self, src, dst):
        copy = pltpu.make_async_copy(src, dst, self.sems.at[self.used])
        self.used += 1
        copy.start()
        return copy


def row_info(long_len, short_len, count):
    return [long_len[0], *(short_len[i] for i in range(count)), lax.axis_index("seq")]


def head_masks(dtype):
    lane = lax.broadcasted_iota(jnp.int32, (1, PAIR), 1)
    low = (lane < HD).astype(F32)
    return low.astype(dtype), (1.0 - low).astype(dtype)


def stack_heads(a, masks):
    return jnp.concatenate([a * masks[0], a * masks[1]], axis=0)


def unstack_heads(out_t, width):
    sub = lax.broadcasted_iota(jnp.int32, (PAIR, width), 0)
    return jnp.where(sub < HD, out_t[:, :width], out_t[:, width:]).T


def key_positions(block, keys, queries, size, me):
    row = lax.broadcasted_iota(jnp.int32, (keys, queries), 0)
    if keys == size:
        return row + (block ^ me) * size
    return ((row // size) ^ me) * size + row % size


def limits(queries, size, me, length, causal):
    if not causal:
        return length - 1
    lane = lax.broadcasted_iota(jnp.int32, (1, queries), 1) % size
    return jnp.minimum(lane + me * size, length - 1)


def attend_forward(dims, causal, info, q_ref, k_ref, v_ref, o_ref, lse_l, lse_s, s_scr):
    T, LL, LS, NS, D, n = dims
    me = info[NS + 1]
    masks = head_masks(BF16)

    def pair(p):
        c = tile(p, PAIR)
        q2 = stack_heads(q_ref[0:LL, c], masks)
        lim = limits(2 * LL, LL, me, info[0], causal)
        top = None
        for r in range(n):
            s = dot_t(k_ref[r * T : r * T + LL, c], q2)
            s = jnp.where(key_positions(r, LL, 2 * LL, LL, me) <= lim, s, NEG)
            s_scr[r * LL : (r + 1) * LL, :] = s
            m = jnp.max(s, axis=0, keepdims=True)
            top = m if top is None else jnp.maximum(top, m)
        total, acc = None, None
        for r in range(n):
            w = jnp.exp(s_scr[r * LL : (r + 1) * LL, :] - top)
            t = jnp.sum(w, axis=0, keepdims=True)
            a = dot(v_ref[r * T : r * T + LL, c].T, w.astype(BF16))
            total = t if total is None else total + t
            acc = a if acc is None else acc + a
        acc = acc * (1.0 / total)
        o_ref[0:LL, c] = unstack_heads(acc, LL).astype(BF16)
        lse_l[p] = jnp.broadcast_to(top + jnp.log(total), (8, 2 * LL))
        for i in range(NS):
            off = LL + i * LS
            q2 = stack_heads(q_ref[off : off + LS, c], masks)
            kb = jnp.concatenate([k_ref[r * T + off : r * T + off + LS, c] for r in range(n)], 0)
            vb = jnp.concatenate([v_ref[r * T + off : r * T + off + LS, c] for r in range(n)], 0)
            s = dot_t(kb, q2)
            lim = limits(2 * LS, LS, me, info[1 + i], causal)
            s = jnp.where(key_positions(0, n * LS, 2 * LS, LS, me) <= lim, s, NEG)
            top = jnp.max(s, axis=0, keepdims=True)
            w = jnp.exp(s - top)
            total = jnp.sum(w, axis=0, keepdims=True)
            acc = dot(vb.T, w.astype(BF16)) * (1.0 / total)
            o_ref[off : off + LS, c] = unstack_heads(acc, LS).astype(BF16)
            lse_s[p * NS + i] = jnp.broadcast_to(top + jnp.log(total), (8, 2 * LS))

    loop(D // PAIR, pair)


def attend_backward(
    dims,
    causal,
    info,
    q_ref,
    k_ref,
    v_ref,
    o_ref,
    do_ref,
    lse_l,
    lse_s,
    dq_ref,
    dk_ref,
    dv_ref,
    first,
    last,
):
    T, LL, LS, NS, D, n = dims
    me = info[NS + 1]
    masks = head_masks(BF16)
    ones = jnp.ones((8, PAIR), F32)

    def row_dots(do2, o):
        prod = do2.astype(F32) * jnp.concatenate([o, o], 0).astype(F32)
        full = lax.dot_general(
            ones,
            prod,
            (((1,), (1,)), ((), ())),
            precision=lax.Precision.HIGHEST,
            preferred_element_type=F32,
        )
        return full[0:1]

    def pair(p):
        c = tile(p, PAIR)
        q2 = stack_heads(q_ref[0:LL, c], masks)
        do2 = stack_heads(do_ref[0:LL, c], masks)
        delta = row_dots(do2, o_ref[0:LL, c])
        lse = lse_l[p][0:1]
        lim = limits(2 * LL, LL, me, info[0], causal)
        dq_t = None
        for r in range(n):
            rows = slice(r * T, r * T + LL)
            kb, vb = k_ref[rows, c], v_ref[rows, c]
            s = dot_t(kb, q2)
            s = jnp.where(key_positions(r, LL, 2 * LL, LL, me) <= lim, s, NEG)
            probs = jnp.exp(s - lse)
            ds = (probs * (dot_t(vb, do2) - delta)).astype(BF16)
            dv_ref[rows, c] = dot(probs.astype(BF16), do2).astype(BF16)
            dk_ref[rows, c] = dot(ds, q2).astype(BF16)
            part = dot(kb.T, ds)
            dq_t = part if dq_t is None else dq_t + part
        dq_ref[0:LL, c] = (unstack_heads(dq_t, LL) * HD**-0.5).astype(BF16)
        for i in range(NS):
            off = LL + i * LS
            q2 = stack_heads(q_ref[off : off + LS, c], masks)
            do2 = stack_heads(do_ref[off : off + LS, c], masks)
            delta = row_dots(do2, o_ref[off : off + LS, c])
            lse = lse_s[p * NS + i][0:1]
            kb = jnp.concatenate([k_ref[r * T + off : r * T + off + LS, c] for r in range(n)], 0)
            vb = jnp.concatenate([v_ref[r * T + off : r * T + off + LS, c] for r in range(n)], 0)
            s = dot_t(kb, q2)
            lim = limits(2 * LS, LS, me, info[1 + i], causal)
            s = jnp.where(key_positions(0, n * LS, 2 * LS, LS, me) <= lim, s, NEG)
            probs = jnp.exp(s - lse)
            ds = (probs * (dot_t(vb, do2) - delta)).astype(BF16)
            dv = dot(probs.astype(BF16), do2).astype(BF16)
            dk = dot(ds, q2).astype(BF16)
            for r in range(n):
                dv_ref[r * T + off : r * T + off + LS, c] = dv[r * LS : (r + 1) * LS]
                dk_ref[r * T + off : r * T + off + LS, c] = dk[r * LS : (r + 1) * LS]
            dq_ref[off : off + LS, c] = (unstack_heads(dot(kb.T, ds), LS) * HD**-0.5).astype(BF16)

    lax.fori_loop(first, last, lambda i, c: (pair(i), c)[1], 0)


def flip(index, bit):
    return index + bit - 2 * bit * ((index // bit) % 2)


class Link:
    def __init__(self, send_sems, recv_sems):
        self.send_sems, self.recv_sems, self.used = send_sems, recv_sems, 0

    def start(self, src, dst, axis, bit):
        copy = pltpu.make_async_remote_copy(
            src_ref=src,
            dst_ref=dst,
            send_sem=self.send_sems.at[self.used],
            recv_sem=self.recv_sems.at[self.used],
            device_id={axis: flip(lax.axis_index(axis), bit)},
            device_id_type=pl.DeviceIdType.MESH,
        )
        self.used += 1
        copy.start()
        return copy


PATH_A = (("seq", 1), ("seq", 2), ("rep", 1))
PATH_B = (("seq", 1), ("rep", 1), ("seq", 2))
PATH_ROWS = (("seq", 1), ("seq", 2))
DP_BITS = (1, 2)
PATH_ALL = PATH_A + (("dp", 1), ("dp", 2))
TILE = 256
FFN_ROWS = 384
FEED_TASKS = ("u0", "u1", "u2", "w0", "w1", "w2")
FEED_ORDER = ("w0", "g0", "g1", "w1", "g2", "w2", "g3")
X_FIRST = ("u0", "u2", "c1", "c2", "s1", "s2a")
PATHS = {
    name: PATH_A if name in X_FIRST else PATH_B
    for name in FEED_TASKS + ("c0", "c1", "c2", "s0", "s1", "s2a", "s2b")
}
SELF_SLOTS = (0, 1, 2)
PLAN = (
    ("w0",),
    (),
    ("u0", "w0"),
    ("w1",),
    ("u1", "u0"),
    ("w2", "w1"),
    ("u2", "u1", "w2"),
    ("w0", "u2"),
    ("u0", "w1", "w0"),
    ("c0",),
    ("w0", "c0"),
    ("c1", "u1", "u2"),
    ("w0", "c1", "w1"),
    ("c2", "w2", "u1"),
    ("w0",),
    ("dm", "w1", "u0", "c2", "u1"),
    (),
    ("w0", "dm", "w1", "c1", "u0"),
    ("u1", "c0", "w1", "w2"),
    ("u0", "u2", "u1", "w1", "w2", "c1"),
    ("s0", "c2"),
    ("u0", "u2", "w2", "s0", "u1", "c1", "c2"),
    ("s1",),
    ("u0", "u2", "c2", "w2", "s1", "dm", "c1"),
    ("s2a", "s2b", "vec", "c0", "s0", "u2", "w2"),
    ("s2a", "c2", "s2b", "vec", "c0", "c1"),
    ("dx", "u2"),
    ("c2", "s1"),
    ("c1", "c0", "s2b", "dx"),
)
FINAL = (
    "c2", "s0", "c0", "s1", "s2a", "s0", "vec", "c0", "s2b", "s1",
    "s2a", "s0", "vec", "s2b", "s2a", "s1", "vec", "s0", "s2b", "s2a",
    "s0", "s1", "dx", "vec", "s1", "s2b", "s2a", "s2b", "s2a",
)


class Gather:
    def __init__(self, link, ref, rows):
        self.link, self.ref, self.rows = link, ref, rows

    def block(self, r, part=None):
        first, count = r * self.rows, self.rows
        if part is not None:
            count = self.rows // 2
            first = first + part * count
        return self.ref.at[first : first + count]

    def send_core(self):
        self.core = self.link.start(self.block(0), self.block(1), "seq", 1)

    def send_far(self):
        self.far = [
            self.link.start(self.block(0, p), self.block(2, p), "seq", 2) for p in range(2)
        ]

    def relay(self):
        self.relayed = []
        for p in range(2):
            self.far[p].wait()
            self.relayed.append(self.link.start(self.block(2, p), self.block(3, p), "seq", 1))

    def end(self):
        for copy in self.relayed:
            copy.wait()


def greet(pairs):
    barrier = pltpu.get_barrier_semaphore()
    for axis, bit in pairs:
        pl.semaphore_signal(
            barrier,
            inc=1,
            device_id={axis: flip(lax.axis_index(axis), bit)},
            device_id_type=pl.DeviceIdType.MESH,
        )
    pl.semaphore_wait(barrier, len(pairs))


def forward_kernel(dims, *refs):
    T, LL, LS, NS, D, n = dims
    refs = list(refs)

    def take(count):
        out = refs[:count]
        del refs[:count]
        return out

    long_len, short_len, xl, xs, ml, ms = take(6)
    info = row_info(long_len, short_len, NS)
    ws_hbm, wos_hbm, wc_hbm, woc_hbm, bias_s, bias_c, gain, shift = take(8)
    q1, k1_out, v1_out, o1, lse1l, lse1s, z1, t1_out = take(8)
    q2, k2_out, v2_out, o2, lse2l, lse2s, z2, t2_out = take(8)
    x, m, ws, wos, wc, woc, k1, v1, k2, v2, blk_t, mem_t, s_scr, sems, send_sems, recv_sems = refs
    copies = Copies(sems)
    load_x = [copies.start(xl, x.at[0:LL]), copies.start(xs, x.at[LL:T])]
    load_ws = copies.start(ws_hbm, ws)
    load_m = [copies.start(ml, m.at[0:LL]), copies.start(ms, m.at[LL:T])]
    load_wc = copies.start(wc_hbm, wc)
    load_wos, load_woc = copies.start(wos_hbm, wos), copies.start(woc_hbm, woc)
    greet(PATH_ROWS)
    link = Link(send_sems, recv_sems)
    rows_x, rows_m = Gather(link, x, T), Gather(link, m, T)
    for item in load_x:
        item.wait()
    rows_x.send_far()
    rows_x.send_core()
    for item in load_m:
        item.wait()
    rows_m.send_core()

    def queries(source, w, bias, q):
        def body(j):
            c = tile(j, TILE)
            out = dot(source[0:T, :].astype(BF16), w[0, :, c]) + bias[0:1, c]
            q[:, c] = (out.astype(BF16).astype(F32) * HD**-0.5).astype(BF16)

        loop(D // TILE, body)

    def keys_values(source, w, bias, k, v, r):
        rows = slice(r * T, (r + 1) * T)

        def body(j):
            c = tile(j, TILE)
            k[rows, c] = dot(source[rows, :], w[1, :, c]).astype(BF16)
            v[rows, c] = (dot(source[rows, :], w[2, :, c]) + bias[1:2, c]).astype(BF16)

        loop(D // TILE, body)

    def residual(source, o, wo, bias, z):
        def body(j):
            c = tile(j, TILE)
            z[:, c] = source[0:T, c].astype(F32) + dot(o[...], wo[:, c]) + bias[2:3, c]

        loop(D // TILE, body)

    load_ws.wait()
    queries(x, ws, bias_s, q1)
    keys_values(x, ws, bias_s, k1, v1, 0)
    transpose_into(blk_t, x, T, D, 0)
    load_wc.wait()
    keys_values(m, wc, bias_c, k2, v2, 0)
    transpose_into(mem_t, m, T, D, 0)
    rows_x.core.wait()
    keys_values(x, ws, bias_s, k1, v1, 1)
    transpose_into(blk_t, x, T, D, T)
    rows_m.core.wait()
    keys_values(m, wc, bias_c, k2, v2, 1)
    transpose_into(mem_t, m, T, D, T)
    rows_x.relay()
    rows_m.send_far()
    keys_values(x, ws, bias_s, k1, v1, 2)
    transpose_into(blk_t, x, T, D, 2 * T)
    rows_x.end()
    keys_values(x, ws, bias_s, k1, v1, 3)
    transpose_into(blk_t, x, T, D, 3 * T)
    stores = [copies.start(k1, k1_out), copies.start(v1, v1_out)]
    stores.append(copies.start(blk_t, t1_out))
    attend_forward(dims, True, info, q1, k1, v1, o1, lse1l, lse1s, s_scr)
    load_wos.wait()
    residual(x, o1, wos, bias_s, z1)
    rows_m.relay()
    xhat, _ = norm_parts(z1[...])
    z2[...] = xhat * gain[0:1] + shift[0:1]
    queries(z2, wc, bias_c, q2)
    keys_values(m, wc, bias_c, k2, v2, 2)
    transpose_into(mem_t, m, T, D, 2 * T)
    rows_m.end()
    keys_values(m, wc, bias_c, k2, v2, 3)
    transpose_into(mem_t, m, T, D, 3 * T)
    stores += [copies.start(k2, k2_out), copies.start(v2, v2_out), copies.start(mem_t, t2_out)]
    attend_forward(dims, False, info, q2, k2, v2, o2, lse2l, lse2s, s_scr)
    load_woc.wait()
    residual(z2, o2, woc, bias_c, z2)
    for item in stores:
        item.wait()


def forward_call(dims, *operands):
    T, LL, LS, NS, D, n = dims
    pairs = D // PAIR
    full, own = (n * T, D), (T, D)
    outs = [
        jax.ShapeDtypeStruct(own, BF16),
        jax.ShapeDtypeStruct(full, BF16),
        jax.ShapeDtypeStruct(full, BF16),
        jax.ShapeDtypeStruct(own, BF16),
        jax.ShapeDtypeStruct((pairs, 8, 2 * LL), F32),
        jax.ShapeDtypeStruct((pairs * NS, 8, 2 * LS), F32),
        jax.ShapeDtypeStruct(own, F32),
        jax.ShapeDtypeStruct((D, n * T), BF16),
    ]
    return pl.pallas_call(
        functools.partial(forward_kernel, dims),
        out_shape=outs + outs,
        in_specs=[SMEM] * 2 + [HBM] * 8 + [VMEM] * 4,
        out_specs=[VMEM, HBM, HBM, VMEM, VMEM, VMEM, VMEM, HBM] * 2,
        scratch_shapes=[pltpu.VMEM(full, BF16)] * 2
        + [pltpu.VMEM((3, D, D), BF16), pltpu.VMEM((D, D), BF16)] * 2
        + [pltpu.VMEM(full, BF16)] * 4
        + [
            pltpu.VMEM((D, n * T), BF16),
            pltpu.VMEM((D, n * T), BF16),
            pltpu.VMEM((n * LL, 2 * LL), F32),
            pltpu.SemaphoreType.DMA((16,)),
            pltpu.SemaphoreType.DMA((10,)),
            pltpu.SemaphoreType.DMA((10,)),
        ],
        compiler_params=pltpu.CompilerParams(
            collective_id=1, has_side_effects=True, vmem_limit_bytes=58 * MIB
        ),
        cost_estimate=pl.CostEstimate(
            flops=20 * 10**9, bytes_accessed=40 * 10**6, transcendentals=8 * 10**6
        ),
        name="forward",
    )(*operands)


def feed_phase(dims, loads, copies, data, scratch, vec, store_task, outs, tick):
    T, LL, LS, NS, D, n = dims
    upb, downb, gain, shift = data
    zb, acc, wu, wd, low, h2t, block, gp, act_t, dy_ref, y_ref = scratch
    tiles = D // TILE
    groups = len(wu)
    rows = D // 8
    loads["z2"].wait()
    xhat2, _ = norm_parts(zb[...])
    h2 = xhat2 * gain[1:2] + shift[1:2]
    low[...] = h2.astype(BF16)
    acc[...] = h2 + downb[...][None, :]
    transpose_into(h2t, low, T, D)

    def up_tile(q, t):
        c = tile(t, TILE)
        u = dot(low[...], wu[q][:, c]) + upb[q * D + t * TILE : q * D + (t + 1) * TILE][None, :]
        sq = u * u
        th = jnp.tanh(0.7978845608028654 * u * (1.0 + 0.044715 * sq))
        half = 0.5 * (1.0 + th)
        act = (u * half).astype(BF16)
        block[:, c] = act
        act_t[tile(t, TILE), q * T : (q + 1) * T] = act.T
        slope = half + (0.5 * 0.7978845608028654) * u * (1.0 - th * th) * (
            1.0 + (3.0 * 0.044715) * sq
        )
        gp[q * tiles + t] = slope.astype(BF16)

    def down_tile(q, j):
        c = tile(j, TILE)
        acc[:, c] += dot(block[...], wd[q][:, c])

    for q in range(groups):
        loads["up", q].wait()
        loop(tiles, functools.partial(up_tile, q))
        loads["down", q].wait()
        loop(tiles, functools.partial(down_tile, q))
    xhat3, rstd3 = norm_parts(acc[...])
    y_ref[...] = (xhat3 * gain[2:3] + shift[2:3]).astype(BF16)
    stores = [copies.start(y_ref.at[0:LL], outs[0]), copies.start(y_ref.at[LL:T], outs[1])]
    for item in loads["dy"]:
        item.wait()
    dy = dy_ref[...].astype(F32)
    vec[8:9] = col_sum(dy * xhat3)
    vec[11:12] = col_sum(dy)
    dz3 = norm_back(dy, gain[2:3], xhat3, rstd3)
    low[...] = dz3.astype(BF16)
    acc[...] = dz3
    vec[12:13] = col_sum(low[...])

    def down_grad(t):
        size = 4 * rows
        parts = []
        for q in range(groups):
            value = dot(act_t[:, q * T : (q + 1) * T], low[:, t * TILE : (t + 1) * TILE])
            value = value.astype(BF16)
            parts += [(None, 0, value[i : i + size]) for i in range(0, D, size)]
        store_task(tiles + t, parts)

    def back_tile(j, q):
        c = tile(j, TILE)
        acc[:, c] += dot_t(block[...], wu[q][c, :])

    def up_grad(q):
        for t in range(tiles):
            c = slice(t * TILE, (t + 1) * TILE)
            j = q * tiles + t
            du = (gp[j].astype(F32) * dot_t(low[...], wd[q][c, :])).astype(BF16)
            vec[13 + q : 14 + q, c] = col_sum(du)
            block[:, c] = du
            value = dot(h2t[...], du).astype(BF16)
            store_task(
                j // 4, [(i, (j % 4) * rows, value[i * rows : (i + 1) * rows]) for i in range(8)]
            )
        for t in range(tiles):
            back_tile(t, q)

    for step in FEED_ORDER:
        if step[0] == "w":
            down_grad(int(step[1]))
        else:
            up_grad(int(step[1]))
        tick()
    dh2 = acc[...]
    xhat2, rstd2 = norm_parts(zb[...])
    vec[7:8] = col_sum(dh2 * xhat2)
    vec[10:11] = col_sum(dh2)
    acc[...] = norm_back(dh2, gain[1:2], xhat2, rstd2)
    for item in stores:
        item.wait()


def backward_phase(dims, cross, chunks, info, loads, data, scratch, vec, row_of, tick, free):
    T, LL, LS, NS, D, n = dims
    dz, z_in, gain, shift, lse_l, lse_s = data
    q, o, w, wo, k, v, dq, do, da, blk_t, o_t, src_t, dblk, grads = scratch
    rows = D // chunks
    base = 3 if cross else 0

    def weight_grad(i, slot, lhs_t, rhs):
        grad = dot(lhs_t, rhs).astype(BF16)
        for s in range(chunks):
            at = pl.ds(row_of(i, slot, s), rows)
            grads[i, at, :] = grad[s * rows : (s + 1) * rows]

    da[...] = dz[...].astype(BF16)
    vec[base + 2 : base + 3] = col_sum(da[...])
    loads["o"].wait()
    transpose_into(o_t, o, T, D)
    loads["wo"].wait()
    for i in range(D // TILE):
        c = slice(i * TILE, (i + 1) * TILE)
        do[:, c] = dot_t(da[...], wo[c, :]).astype(BF16)
        weight_grad(i, 0, o_t[...], da[:, c])
    free("wo")
    if cross:
        xhat, _ = norm_parts(z_in[...])
        da[...] = (xhat * gain[0:1] + shift[0:1]).astype(BF16)
        transpose_into(src_t, da, T, D)
    tick()
    for name in ("q", "k", "v", "t"):
        loads[name].wait()
    if not cross:
        src_t[...] = blk_t[:, 0:T]
    pairs = TILE // PAIR
    for i in range(D // TILE):
        c = slice(i * TILE, (i + 1) * TILE)
        attend_backward(
            dims, not cross, info, q, k, v, o, do, lse_l, lse_s, dq, k, v, pairs * i, pairs * (i + 1)
        )
        tick()
        vec[base : base + 1, c] = col_sum(dq[:, c])
        vec[base + 1 : base + 2, c] = col_sum(v[:, c])
        weight_grad(i, 1, src_t[...], dq[:, c])
        weight_grad(i, 2, blk_t[...], k[:, c])
        weight_grad(i, 3, blk_t[...], v[:, c])
        tick()
    for name in ("q", "o", "t"):
        free(name)
    loads["w"].wait()
    free("dblk")

    def dblk_tile(i, at, j):
        c = tile(j, TILE)
        rows_in = slice(i * T, (i + 1) * T)
        part = dot_t(k[rows_in, :], w[1, c, :]) + dot_t(v[rows_in, :], w[2, c, :])
        if i == 0:
            part_q = dz[:, c] + dot_t(dq[...], w[0, c, :])
            if cross:
                dz[:, c] = part_q
            else:
                part = part + part_q
        dblk[at * T : (at + 1) * T, c] = part.astype(BF16)

    kept_first = sorted(range(n), key=lambda r: (r % 2, r // 2))
    for at in reversed(range(n)):
        loop(D // TILE, functools.partial(dblk_tile, kept_first[at], at))
        if at > 0:
            tick()
    for name in ("k", "v", "w"):
        free(name)
    tick()
    if cross:
        dh = dz[...]
        xhat, rstd = norm_parts(z_in[...])
        vec[6:7] = col_sum(dh * xhat)
        vec[9:10] = col_sum(dh)
        dz[...] = norm_back(dh, gain[0:1], xhat, rstd)


def add_rows(dst, dst_at, a, a_at, b, b_at, count, step=96):
    def body(i):
        def at(start):
            return pl.ds(pl.multiple_of(start + i * step, 16), step)

        total = a[at(a_at), :].astype(F32) + b[at(b_at), :].astype(F32)
        dst[at(dst_at), :] = total.astype(dst.dtype)

    loop(count // step, body)


class Share:
    def __init__(self, link, theirs, acc, recv, res, size, path, dp_bits):
        self.link, self.theirs, self.acc, self.recv, self.res = link, theirs, acc, recv, res
        self.size, self.path, self.dp_bits = size, path, dp_bits
        self.stage, self.copy, self.at = 0, None, 0
        self.off, self.count = 0, size
        self.kept, self.last = [], len(path) + 2 * len(dp_bits)

    def advance(self):
        stage, path, dp_bits = self.stage, self.path, self.dp_bits
        if stage > self.last:
            return
        self.stage += 1
        halves = len(path)
        if stage == 0:
            rows = self.size << (halves - 1)
            self.land, self.rows = self.at, rows
            self.at += rows
            land = self.recv.at[0:rows]
            if len(self.theirs.shape) == 3:
                land = land.reshape(*self.theirs.shape)
            self.copy = self.link.start(self.theirs, land, *path[0])
            return
        self.copy.wait()
        if stage <= halves + len(dp_bits):
            last = stage == halves + len(dp_bits)
            dst = self.res if last else self.acc
            add_rows(dst, self.off, self.acc, self.off, self.recv, self.land, self.rows, 48)
        if stage < halves:
            rows = self.size << (halves - 1 - stage)
            self.land, self.rows = self.at, rows
            self.at += rows
            src = self.acc.at[rows : 2 * rows]
            dst = self.recv.at[self.land : self.land + rows]
            self.copy = self.link.start(src, dst, *path[stage])
        elif stage < halves + len(dp_bits):
            bit = dp_bits[stage - halves]
            mine = (lax.axis_index("dp") // bit) % 2
            self.count //= 2
            give = self.off + (1 - mine) * self.count
            self.off = self.off + mine * self.count
            self.kept.append((self.off, self.count, bit))
            self.land, self.rows = self.at, self.count
            self.at += self.count
            src = self.acc.at[pl.ds(pl.multiple_of(give, 16), self.count)]
            dst = self.recv.at[self.land : self.land + self.count]
            self.copy = self.link.start(src, dst, "dp", bit)
        elif self.kept:
            off, count, bit = self.kept.pop()
            part = self.res.at[pl.ds(pl.multiple_of(off, 16), count)]
            self.copy = self.link.start(part, part, "dp", bit)


class Rows:
    def __init__(self, link, copies, blocks, recv, lands, out, size, path):
        self.link, self.copies, self.blocks, self.recv, self.out = link, copies, blocks, recv, out
        self.size, self.path, self.stage, self.lands, self.last = size, path, 0, lands, len(path)

    def advance(self):
        stage, path = self.stage, self.path
        if stage > self.last:
            return
        self.stage += 1
        if stage > 0:
            self.copy.wait()
            add_rows(self.blocks, 0, self.blocks, 0, self.recv, self.land, self.rows)
        if stage == len(path):
            self.store = self.copies.start(self.blocks.at[0 : self.rows], self.out)
        if stage < len(path):
            rows = self.size << (len(path) - 1 - stage)
            self.land, self.rows = self.lands[stage], rows
            src = self.blocks.at[rows : 2 * rows]
            dst = self.recv.at[self.land : self.land + rows]
            self.copy = self.link.start(src, dst, *path[stage])


class Small:
    def __init__(self, link, vec, recv, path):
        self.link, self.vec, self.recv, self.path, self.stage = link, vec, recv, path, 0
        self.last = len(path)

    def advance(self):
        stage, path = self.stage, self.path
        if stage > self.last:
            return
        self.stage += 1
        if stage > 0:
            self.copy.wait()
            self.vec[stage] = self.vec[stage - 1] + self.recv[stage - 1]
        if stage < len(path):
            self.copy = self.link.start(self.vec.at[stage], self.recv.at[stage], *path[stage])


def inner_place(path, s):
    x = (s // 4 + lax.axis_index("seq") // 2) % 2
    y = (s + lax.axis_index("rep")) % 2
    return x * 2 + y if path is PATH_A else y * 2 + x


def xor_place(path, s):
    return (s // 2 + lax.axis_index("seq")) % 2 * 4 + inner_place(path, s)


def backward_kernel(dims, linked, *refs):
    T, LL, LS, NS, D, n = dims
    chunks = 8
    half = chunks // 2
    size = FFN_ROWS
    tiles = D // TILE
    refs = list(refs)

    def take(count):
        out = refs[:count]
        del refs[:count]
        return out

    long_len, short_len = take(2)
    info = row_info(long_len, short_len, NS)
    z2_hbm, z1_hbm, cot_l, cot_s, wup_hbm, wdown_hbm = take(6)
    cross_hbm, self_hbm = take(7), take(7)
    upb, downb, gain, shift, lse2l, lse2s, lse1l, lse1s = take(8)
    yl_out, ys_out = take(2)
    if linked:
        shares_out, dm_out, dx_out, vec_out = take(4)
    else:
        gf_out, gc_out, gs_out, dm_out, dx_out, vec_out = take(6)
    q, o, w, wo, k, v, dq, do, da, blk_t, o_t, src_t, dblk, dres, zb = take(15)
    gc, gs, accs, vec, sems = take(5)
    if linked:
        recvs, rows_recv, res, vec_recv, send_sems, recv_sems = take(6)

    copies = Copies(sems)
    homes = {"wo": wo, "o": o, "q": q, "k": k, "v": v, "t": blk_t, "w": w}
    sources_c = dict(zip(("w", "wo", "k", "v", "q", "o", "t"), cross_hbm))
    sources_s = dict(zip(("w", "wo", "k", "v", "q", "o", "t"), self_hbm))
    wu = [(k, v)[i // 2].at[(i % 2) * D : (i % 2 + 1) * D] for i in range(4)]
    wd = [w.at[0], w.at[1], w.at[2], dblk.at[0:D]]
    loads_f = {"z2": copies.start(z2_hbm, zb)}
    for i in range(4):
        loads_f["up", i] = copies.start(wup_hbm.at[:, i * D : (i + 1) * D], wu[i])
        loads_f["down", i] = copies.start(wdown_hbm.at[i * D : (i + 1) * D], wd[i])
    loads_f["dy"] = [copies.start(cot_l, do.at[0:LL]), copies.start(cot_s, do.at[LL:T])]
    loads_c = {name: copies.start(sources_c[name], homes[name]) for name in ("o", "wo")}
    vec[0] = jnp.zeros((VEC_ROWS, D), F32)

    def theirs(i):
        return gs.at[i // 2, (i % 2) * half * size : (i % 2 + 1) * half * size]

    tasks = {}
    steps = iter(PLAN)

    def tick():
        if linked:
            for name in next(steps):
                tasks[name].advance()

    if linked:
        greet(PATH_ALL)
        link = Link(send_sems, recv_sems)
        for i, name in enumerate(FEED_TASKS):
            tasks[name] = Share(
                link, theirs(i), accs.at[i], recvs.at[i], res.at[i], size, PATHS[name], DP_BITS
            )
        whole = (0, chunks * size)
        for name, g, i, slot, (first, last) in (
            ("c0", gc, 0, 6, whole),
            ("c1", gc, 1, 7, whole),
            ("c2", gc, 2, 8, whole),
            ("s0", gs, 0, SELF_SLOTS[0], whole),
            ("s1", gs, 1, SELF_SLOTS[1], whole),
            ("s2a", gs, 2, SELF_SLOTS[2], (0, whole[1] // 2)),
            ("s2b", gs, 2, SELF_SLOTS[2], (whole[1] // 2, whole[1])),
        ):
            rows = last - first
            out = res.at[(6 if g is gc else 9) + i]
            landing = recvs.shape[1] * rows // whole[1]
            land = first * recvs.shape[1] // whole[1]
            tasks[name] = Share(
                link,
                g.at[i, first + rows // 2 : last],
                g.at[i, first:last],
                recvs.at[slot, land : land + landing],
                out.at[first // chunks : last // chunks],
                rows // chunks,
                PATHS[name],
                DP_BITS,
            )
        tasks["dm"] = Rows(link, copies, dblk, rows_recv, (0, 2 * T), dm_out, T, PATH_ROWS)
        tasks["dx"] = Rows(link, copies, dblk, rows_recv, (0, 3 * T), dx_out, T, PATH_ROWS)
        tasks["vec"] = Small(link, vec, vec_recv, PATH_ALL)

    def row_of(kind, i, slot, s):
        rows = size // 4
        if not linked:
            return s * size + slot * rows
        name = kind + str(i)
        if name != "s2":
            return pl.multiple_of(xor_place(PATHS[name], s) * size + slot * rows, 16)
        at = xor_place(PATHS[name + "ab"[slot // 2]], s) * 2 * rows + slot % 2 * rows
        return pl.multiple_of(slot // 2 * chunks * 2 * rows + at, 16)


    side = lax.axis_index("seq") % 2

    def store_task(i, parts):
        for s in range(chunks):
            if s // 2 % 2:
                continue
            (_, off, low_part), (_, _, high_part) = parts[s], parts[s + 2]
            if linked:
                place = inner_place(PATHS[FEED_TASKS[i]], s)
                at = pl.multiple_of(place * size + off, 16)
                rows = pl.ds(at, low_part.shape[0])
                accs[i, rows, :] = jnp.where(side == 0, low_part, high_part)
                theirs(i)[rows, :] = jnp.where(side == 0, high_part, low_part)
            else:
                for c, part in ((s, low_part), (s + 2, high_part)):
                    out = accs.at[i] if c < half else theirs(i)
                    at = c % half * size + off
                    out[at : at + part.shape[0], :] = part

    feed_phase(
        dims, loads_f, copies, (upb, downb, gain, shift),
        (zb, dres, wu, wd, da, src_t, q, gc.reshape(chunks * tiles, T, TILE), blk_t, do, dq),
        vec.at[0], store_task, (yl_out, ys_out), tick,
    )
    load_z1 = copies.start(z1_hbm, zb)
    for name in ("q", "k", "v", "t", "w"):
        loads_c[name] = copies.start(sources_c[name], homes[name])
    load_z1.wait()
    if not linked:
        for i in range(2 * tiles):
            copies.start(accs.at[i], gf_out.at[i, 0]).wait()
            copies.start(theirs(i), gf_out.at[i, 1]).wait()
    loads_s = {}

    def free_cross(name):
        if name in homes:
            loads_s[name] = copies.start(sources_s[name], homes[name])

    def free_self(name):
        if linked and name == "dblk":
            while tasks["dm"].stage <= tasks["dm"].last:
                tasks["dm"].advance()
            tasks["dm"].store.wait()

    backward_phase(
        dims, True, chunks, info, loads_c, (dres, zb, gain, shift, lse2l, lse2s),
        (q, o, w, wo, k, v, dq, do, da, blk_t, o_t, src_t, dblk, gc), vec.at[0], functools.partial(row_of, "c"), tick,
        free_cross,
    )
    if not linked:
        stores = [copies.start(gc, gc_out)]
        copies.start(dblk, dm_out).wait()
    backward_phase(
        dims, False, chunks, info, loads_s, (dres, None, None, None, lse1l, lse1s),
        (q, o, w, wo, k, v, dq, do, da, blk_t, o_t, src_t, dblk, gs), vec.at[0], functools.partial(row_of, "s"), tick,
        free_self,
    )
    if linked:
        for name in FINAL:
            tasks[name].advance()
        for task in tasks.values():
            while task.stage <= task.last:
                task.advance()
        copies.start(res, shares_out).wait()
        tasks["dx"].store.wait()
        vec_out[...] = vec[len(PATH_ALL)]
    else:
        vec_out[...] = vec[0]
        stores += [copies.start(gs, gs_out), copies.start(dblk, dx_out)]
        for item in stores:
            item.wait()


def backward_call(dims, linked, info, feed_hbm, cross_hbm, self_hbm, small):
    T, LL, LS, NS, D, n = dims
    full, own = (n * T, D), (T, D)
    tiles = D // TILE
    size = FFN_ROWS
    grads = (tiles, 8 * size, TILE)
    vec = jax.ShapeDtypeStruct((VEC_ROWS, D), F32)
    steps = len(PATH_ALL)
    out_shape = [jax.ShapeDtypeStruct((LL, D), BF16), jax.ShapeDtypeStruct((T - LL, D), BF16)]
    if linked:
        out_shape += [
            jax.ShapeDtypeStruct((4 * tiles, size, TILE), BF16),
            jax.ShapeDtypeStruct(own, BF16),
            jax.ShapeDtypeStruct(own, BF16),
            vec,
        ]
        landing = 7 * size + 3 * size // 4
        count = (4 * tiles + 1) * 7 + 4 + steps
        extra = [
            pltpu.VMEM((3 * tiles, landing, TILE), BF16),
            pltpu.VMEM((4 * T, D), BF16),
            pltpu.VMEM((4 * tiles, size, TILE), BF16),
            pltpu.VMEM((steps, VEC_ROWS, D), F32),
            pltpu.SemaphoreType.DMA((count,)),
            pltpu.SemaphoreType.DMA((count,)),
        ]
    else:
        out_shape += [
            jax.ShapeDtypeStruct((2 * tiles, 2, 4 * size, TILE), BF16),
            jax.ShapeDtypeStruct(grads, BF16),
            jax.ShapeDtypeStruct(grads, BF16),
            jax.ShapeDtypeStruct(full, BF16),
            jax.ShapeDtypeStruct(full, BF16),
            vec,
        ]
        extra = []
    params = {"collective_id": 0} if linked else {}
    return pl.pallas_call(
        functools.partial(backward_kernel, dims, linked),
        out_shape=out_shape,
        in_specs=[SMEM] * 2 + [HBM] * 20 + [VMEM] * 8,
        out_specs=[HBM] * (len(out_shape) - 1) + [VMEM],
        scratch_shapes=[
            pltpu.VMEM(own, BF16),
            pltpu.VMEM(own, BF16),
            pltpu.VMEM((3, D, D), BF16),
            pltpu.VMEM((D, D), BF16),
            pltpu.VMEM(full, BF16),
            pltpu.VMEM(full, BF16),
            pltpu.VMEM(own, BF16),
            pltpu.VMEM(own, BF16),
            pltpu.VMEM(own, BF16),
            pltpu.VMEM((D, n * T), BF16),
            pltpu.VMEM((D, T), BF16),
            pltpu.VMEM((D, T), BF16),
            pltpu.VMEM(full, BF16),
            pltpu.VMEM(own, F32),
            pltpu.VMEM(own, F32),
            pltpu.VMEM(grads, BF16),
            pltpu.VMEM(grads, BF16),
            pltpu.VMEM((2 * tiles, 4 * size, TILE), BF16),
            pltpu.VMEM((steps + 1, VEC_ROWS, D), F32),
            pltpu.SemaphoreType.DMA((48,)),
        ]
        + extra,
        compiler_params=pltpu.CompilerParams(
            vmem_limit_bytes=60 * MIB, has_side_effects=True, **params
        ),
        cost_estimate=pl.CostEstimate(
            flops=100 * 10**9, bytes_accessed=60 * 10**6, transcendentals=8 * 10**6
        ),
        name="backward",
    )(*info, *feed_hbm, *cross_hbm, *self_hbm, *small)


def finish_kernel(dims, mesh_sizes, yl, ys, shares_hbm, dm, dx, vec_hbm, *refs):
    T, LL, LS, NS, D, n = dims
    *outs, shares, vec, sems = refs
    (
        y_l, y_s, dx_l, dx_s, dm_l, dm_s, g_self, g_selfout, b_self, g_cross, g_crossout, b_cross,
        g_gain, g_shift, g_up, b_up, g_down, b_down,
    ) = outs
    shards = mesh_sizes[1] * mesh_sizes[2]
    mine = lax.axis_index("seq") * mesh_sizes[2] + lax.axis_index("rep")
    copies = Copies(sems)
    load_vec, load_shares = copies.start(vec_hbm, vec), copies.start(shares_hbm, shares)
    pairs = ((yl, y_l), (ys, y_s), (dx.at[0:LL], dx_l), (dx.at[LL:T], dx_s), (dm.at[0:LL], dm_l), (dm.at[LL:T], dm_s))
    moves = [copies.start(src, dst) for src, dst in pairs]
    load_shares.wait()
    rows = D // shards
    for t in range(D // TILE):
        c = slice(t * TILE, (t + 1) * TILE)
        for i in range(4):
            part = slice(i * rows, (i + 1) * rows)
            j = 4 * t + i
            g_up[:, j * TILE : (j + 1) * TILE] = shares[t, part, :].astype(F32)
            for first, whole, alone in ((6, g_cross, g_crossout), (9, g_self, g_selfout)):
                value = shares[first + t, part, :].astype(F32)
                if i == 0:
                    alone[:, c] = value
                else:
                    whole[i - 1, :, c] = value
        g_down[:, c] = shares[3 + t].astype(F32)
    load_vec.wait()
    turned = pltpu.roll(vec[...], D - mine * rows, 1)
    for i, out in enumerate((b_self, b_cross, g_gain, g_shift)):
        out[...] = turned[3 * i : 3 * i + 3, 0:rows]
    b_down[...] = turned[12:13, 0:rows]
    ups = vec[13:14, :]
    per_row = D // (4 * rows)
    for i in range(1, 4):
        ups = jnp.where(mine // per_row == i, vec[13 + i : 14 + i, :], ups)
    out = ups[:, 0 : 4 * rows]
    for i in range(1, per_row):
        out = jnp.where(mine % per_row == i, ups[:, i * 4 * rows : (i + 1) * 4 * rows], out)
    b_up[...] = out
    for item in moves:
        item.wait()


def finish_call(dims, sizes, yl, ys, shares, dm, dx, vec):
    T, LL, LS, NS, D, n = dims
    rows = D // (sizes[1] * sizes[2])

    def shape(*dims):
        return jax.ShapeDtypeStruct(dims, F32)

    tokens = [jax.ShapeDtypeStruct((LL, D), BF16), jax.ShapeDtypeStruct((T - LL, D), BF16)]
    out_shape = tokens + tokens + tokens + [
        shape(3, rows, D), shape(rows, D), shape(3, rows), shape(3, rows, D), shape(rows, D),
        shape(3, rows), shape(3, rows), shape(3, rows), shape(rows, 4 * D), shape(1, 4 * rows),
        shape(4 * rows, D), shape(1, rows),
    ]
    return pl.pallas_call(
        functools.partial(finish_kernel, dims, sizes),
        out_shape=out_shape,
        in_specs=[HBM] * 6,
        out_specs=[VMEM] * len(out_shape),
        scratch_shapes=[
            pltpu.VMEM(shares.shape, BF16),
            pltpu.VMEM(vec.shape, F32),
            pltpu.SemaphoreType.DMA((8,)),
        ],
        compiler_params=pltpu.CompilerParams(vmem_limit_bytes=58 * MIB),
        name="finish",
    )(yl, ys, shares, dm, dx, vec)


def swap(a, axis, bit, size):
    return lax.ppermute(a, axis, [(i, i ^ bit) for i in range(size)])


def bits_of(size):
    return [1 << i for i in range(size.bit_length() - 1)]


def add_low(a, b):
    return (a.astype(F32) + b.astype(F32)).astype(BF16)


def halve(a, steps):
    for axis, bit, size in steps:
        half = a.shape[0] // 2
        a = add_low(a[:half], swap(a[half:], axis, bit, size))
    return a[0]


def all_sum(a, axis, size):
    rows, cols = a.shape
    me = lax.axis_index(axis)
    steps = bits_of(size)
    sent = []
    for bit in steps:
        mine = (me // bit) % 2
        a = a.reshape(2, a.shape[0] // 2, cols)
        keep = lax.dynamic_index_in_dim(a, mine, 0, keepdims=False)
        give = lax.dynamic_index_in_dim(a, 1 - mine, 0, keepdims=False)
        a = add_low(keep, swap(give, axis, bit, size))
        sent.append(mine)
    for bit, mine in zip(reversed(steps), reversed(sent)):
        other = swap(a, axis, bit, size)
        first = jnp.where(mine == 0, a, other)
        second = jnp.where(mine == 0, other, a)
        a = jnp.concatenate([first, second], axis=0)
    return a.reshape(rows, cols)


def on_device(
    sizes,
    long_rows,
    short_rows,
    long_memory,
    short_memory,
    long_cotangent,
    short_cotangent,
    long_lengths,
    short_lengths,
    self_qkv,
    self_out,
    self_bias,
    cross_qkv,
    cross_out,
    cross_bias,
    norm_gain,
    norm_bias,
    up_proj,
    up_bias,
    down_proj,
    down_bias,
):
    n_dp, n, n_rep = sizes
    count_l, LL, D = long_rows.shape
    NS, LS, _ = short_rows.shape
    FF = up_proj.shape[1]
    T = LL + NS * LS
    dims = (T, LL, LS, NS, D, n)
    shards = n * n_rep

    def flat(a):
        return a.reshape(-1, D)

    me = lax.axis_index("seq")
    mine = me * n_rep + lax.axis_index("rep")
    info = (long_lengths, short_lengths)

    linked = (n_dp, n, n_rep) == (4, 4, 2)

    norm = (norm_gain, norm_bias)
    outs = forward_call(
        dims, *info, flat(long_rows), flat(short_rows), flat(long_memory), flat(short_memory),
        self_qkv, self_out, cross_qkv, cross_out, self_bias, cross_bias, *norm,
    )
    q1, k1, v1, o1, lse1l, lse1s, z1, xt = outs[:8]
    q2, k2, v2, o2, lse2l, lse2s, z2, mt = outs[8:]
    y_l, y_s, *results = backward_call(
        dims,
        linked,
        info,
        (z2, z1, flat(long_cotangent), flat(short_cotangent), up_proj, down_proj),
        (cross_qkv, cross_out, k2, v2, q2, o2, mt),
        (self_qkv, self_out, k1, v1, q1, o1, xt),
        (up_bias, down_bias, *norm, lse2l, lse2s, lse1l, lse1s),
    )
    rows = D // shards
    if linked:
        shares, dm, dx, small = results
        rest = finish_call(dims, sizes, y_l, y_s, shares, dm, dx, small)
        tokens, rest = rest[:6], list(rest[6:])
        rest[9], rest[11] = rest[9][0], rest[11][0]
        shapes = (long_rows.shape, short_rows.shape) * 3
        return tuple(a.reshape(b) for a, b in zip(tokens, shapes)) + tuple(rest)
    gf, gc, gs, dm, dx, small = results
    chunks = 8
    index = jnp.arange(shards, dtype=jnp.int32) ^ mine
    rel_seq, rel_rep = index // n_rep, index % n_rep
    core, rest = rel_seq % 2, rel_seq // 2
    pos_a = core * (shards // 2) + rest * n_rep + rel_rep
    pos_b = core * (shards // 2) + rel_rep * (n // 2) + rest
    steps_core = [("seq", 1, n)]
    steps_x = [("seq", bit, n) for bit in reversed(bits_of(n)[1:])]
    steps_y = [("rep", bit, n_rep) for bit in reversed(bits_of(n_rep))]

    def reduce_all(a, pos, steps):
        parts = a.reshape(shards, a.shape[0] // shards, a.shape[1])
        parts = jnp.zeros_like(parts).at[pos].set(parts)
        return all_sum(halve(parts, steps), "dp", n_dp)

    order_a = (pos_a, steps_core + steps_x + steps_y)
    order_b = (pos_b, steps_core + steps_y + steps_x)
    split = (D // TILE, chunks, 4, D // chunks, TILE)
    g_up = gf[: D // TILE].reshape(split).transpose(1, 3, 0, 2, 4).reshape(D, FF)
    g_down = gf[D // TILE :].reshape(D // TILE, chunks, FF // chunks, TILE)
    up_share = reduce_all(g_up, *order_a)
    down_share = reduce_all(g_down.transpose(1, 2, 0, 3).reshape(FF, D), *order_b)

    def four(g):
        mats = g.reshape(split).transpose(2, 1, 3, 0, 4).reshape(4, D, D)
        return jnp.stack([reduce_all(mats[i], *order_a) for i in range(4)])

    cross_share, self_share = four(gc), four(gs)
    seq_steps = [("seq", bit, n) for bit in bits_of(n)]
    dm = dm.reshape(n, T, D)
    dx = dx.reshape(n, T, D)
    dm = halve(dm, seq_steps)
    dx = halve(dx, seq_steps)
    small = lax.psum(small, ("dp", "seq", "rep"))

    def part(a, width):
        return lax.dynamic_slice_in_dim(a, mine * width, width, axis=-1)

    vecs = part(small[0:13], D // shards)
    upb_grad = part(small[13:17].reshape(-1), FF // shards)

    def unflat(a):
        return (
            a[:LL].reshape(count_l, LL, D),
            a[LL:].reshape(NS, LS, D),
        )

    y_l, y_s = y_l.reshape(long_rows.shape), y_s.reshape(short_rows.shape)
    dx_l, dx_s = unflat(dx)
    dm_l, dm_s = unflat(dm)
    cross_grad = cross_share.astype(F32)
    self_grad = self_share.astype(F32)
    return (
        y_l,
        y_s,
        dx_l,
        dx_s,
        dm_l,
        dm_s,
        self_grad[1:4],
        self_grad[0],
        vecs[0:3],
        cross_grad[1:4],
        cross_grad[0],
        vecs[3:6],
        vecs[6:9],
        vecs[9:12],
        up_share.astype(F32),
        upb_grad,
        down_share.astype(F32),
        vecs[12],
    )


def solution(mesh):
    rows = P(("dp", "rep"), "seq", None)
    lengths = P(("dp", "rep"))
    share = ("seq", "rep")
    in_specs = (rows,) * 6 + (lengths,) * 2 + (P(),) * 12
    out_specs = (rows,) * 6 + (
        P(None, share, None),
        P(share, None),
        P(None, share),
        P(None, share, None),
        P(share, None),
        P(None, share),
        P(None, share),
        P(None, share),
        P(share, None),
        P(share),
        P(share, None),
        P(share),
    )
    sizes = (mesh.shape["dp"], mesh.shape["seq"], mesh.shape["rep"])
    return jax.shard_map(
        functools.partial(on_device, sizes),
        mesh=mesh,
        in_specs=in_specs,
        out_specs=out_specs,
        check_vma=False,
    )
```

```python
import functools

import jax
import jax.numpy as jnp
from jax import lax
from jax.experimental import pallas as pl
from jax.experimental.pallas import tpu as pltpu
from jax.sharding import PartitionSpec as P

HD = 64
PAIR = 2 * HD
F32 = jnp.float32
BF16 = jnp.bfloat16
NEG = -1000000000.0
MIB = 1024 * 1024
VEC_ROWS = 24

HBM = pl.BlockSpec(memory_space=pltpu.HBM)
VMEM = pl.BlockSpec(memory_space=pltpu.VMEM)
SMEM = pl.BlockSpec(memory_space=pltpu.SMEM)


def dot(a, b):
    return jnp.dot(a, b, preferred_element_type=F32)


def dot_t(a, b):
    return lax.dot_general(a, b, (((1,), (1,)), ((), ())), preferred_element_type=F32)


def loop(count, body, first=0):
    if count - first <= 6:
        for i in range(first, count):
            body(i)
        return
    lax.fori_loop(first, count, lambda i, c: (body(i), c)[1], 0)


def tile(j, width):
    if isinstance(j, int):
        return pl.ds(j * width, width)
    return pl.ds(pl.multiple_of(j * width, width), width)


def norm_parts(z):
    center = z - jnp.mean(z, axis=-1, keepdims=True)
    rstd = lax.rsqrt(jnp.mean(center * center, axis=-1, keepdims=True) + 1e-05)
    return center * rstd, rstd


def norm_back(dy, gain, xhat, rstd):
    dyg = dy * gain
    mean_a = jnp.mean(dyg, axis=-1, keepdims=True)
    mean_b = jnp.mean(dyg * xhat, axis=-1, keepdims=True)
    return rstd * (dyg - mean_a - xhat * mean_b)


def col_sum(a):
    return jnp.sum(a.astype(F32), axis=0, keepdims=True)


def transpose_into(dst_ref, src_ref, rows, cols, row_off=0):
    def body(j):
        dst_ref[tile(j, 128), row_off : row_off + rows] = src_ref[
            row_off : row_off + rows, tile(j, 128)
        ].T

    loop(cols // 128, body)


class Copies:
    def __init__(self, sems):
        self.sems, self.used = sems, 0

    def start(self, src, dst):
        copy = pltpu.make_async_copy(src, dst, self.sems.at[self.used])
        self.used += 1
        copy.start()
        return copy


def row_info(long_len, short_len, count):
    return [long_len[0], *(short_len[i] for i in range(count)), lax.axis_index("seq")]


def head_masks(dtype):
    lane = lax.broadcasted_iota(jnp.int32, (1, PAIR), 1)
    low = (lane < HD).astype(F32)
    return low.astype(dtype), (1.0 - low).astype(dtype)


def stack_heads(a, masks):
    return jnp.concatenate([a * masks[0], a * masks[1]], axis=0)


def unstack_heads(out_t, width):
    sub = lax.broadcasted_iota(jnp.int32, (PAIR, width), 0)
    return jnp.where(sub < HD, out_t[:, :width], out_t[:, width:]).T


def key_positions(block, keys, queries, size, me):
    row = lax.broadcasted_iota(jnp.int32, (keys, queries), 0)
    if keys == size:
        return row + (block ^ me) * size
    return ((row // size) ^ me) * size + row % size


def limits(queries, size, me, length, causal):
    if not causal:
        return length - 1
    lane = lax.broadcasted_iota(jnp.int32, (1, queries), 1) % size
    return jnp.minimum(lane + me * size, length - 1)


def attend_forward(dims, causal, info, q_ref, k_ref, v_ref, o_ref, lse_l, lse_s, s_scr):
    T, LL, LS, NS, D, n = dims
    me = info[NS + 1]
    masks = head_masks(BF16)

    def pair(p):
        c = tile(p, PAIR)
        q2 = stack_heads(q_ref[0:LL, c], masks)
        lim = limits(2 * LL, LL, me, info[0], causal)
        top = None
        for r in range(n):
            s = dot_t(k_ref[r * T : r * T + LL, c], q2)
            s = jnp.where(key_positions(r, LL, 2 * LL, LL, me) <= lim, s, NEG)
            s_scr[r * LL : (r + 1) * LL, :] = s
            m = jnp.max(s, axis=0, keepdims=True)
            top = m if top is None else jnp.maximum(top, m)
        total, acc = None, None
        for r in range(n):
            w = jnp.exp(s_scr[r * LL : (r + 1) * LL, :] - top)
            t = jnp.sum(w, axis=0, keepdims=True)
            a = dot(v_ref[r * T : r * T + LL, c].T, w.astype(BF16))
            total = t if total is None else total + t
            acc = a if acc is None else acc + a
        acc = acc * (1.0 / total)
        o_ref[0:LL, c] = unstack_heads(acc, LL).astype(BF16)
        lse_l[p] = jnp.broadcast_to(top + jnp.log(total), (8, 2 * LL))
        for i in range(NS):
            off = LL + i * LS
            q2 = stack_heads(q_ref[off : off + LS, c], masks)
            kb = jnp.concatenate([k_ref[r * T + off : r * T + off + LS, c] for r in range(n)], 0)
            vb = jnp.concatenate([v_ref[r * T + off : r * T + off + LS, c] for r in range(n)], 0)
            s = dot_t(kb, q2)
            lim = limits(2 * LS, LS, me, info[1 + i], causal)
            s = jnp.where(key_positions(0, n * LS, 2 * LS, LS, me) <= lim, s, NEG)
            top = jnp.max(s, axis=0, keepdims=True)
            w = jnp.exp(s - top)
            total = jnp.sum(w, axis=0, keepdims=True)
            acc = dot(vb.T, w.astype(BF16)) * (1.0 / total)
            o_ref[off : off + LS, c] = unstack_heads(acc, LS).astype(BF16)
            lse_s[p * NS + i] = jnp.broadcast_to(top + jnp.log(total), (8, 2 * LS))

    loop(D // PAIR, pair)


def attend_backward(
    dims,
    causal,
    info,
    q_ref,
    k_ref,
    v_ref,
    o_ref,
    do_ref,
    lse_l,
    lse_s,
    dq_ref,
    dk_ref,
    dv_ref,
    first,
    last,
):
    T, LL, LS, NS, D, n = dims
    me = info[NS + 1]
    masks = head_masks(BF16)
    ones = jnp.ones((8, PAIR), F32)

    def row_dots(do2, o):
        prod = do2.astype(F32) * jnp.concatenate([o, o], 0).astype(F32)
        full = lax.dot_general(
            ones,
            prod,
            (((1,), (1,)), ((), ())),
            precision=lax.Precision.HIGHEST,
            preferred_element_type=F32,
        )
        return full[0:1]

    def pair(p):
        c = tile(p, PAIR)
        q2 = stack_heads(q_ref[0:LL, c], masks)
        do2 = stack_heads(do_ref[0:LL, c], masks)
        delta = row_dots(do2, o_ref[0:LL, c])
        lse = lse_l[p][0:1]
        lim = limits(2 * LL, LL, me, info[0], causal)
        dq_t = None
        for r in range(n):
            rows = slice(r * T, r * T + LL)
            kb, vb = k_ref[rows, c], v_ref[rows, c]
            s = dot_t(kb, q2)
            s = jnp.where(key_positions(r, LL, 2 * LL, LL, me) <= lim, s, NEG)
            probs = jnp.exp(s - lse)
            ds = (probs * (dot_t(vb, do2) - delta)).astype(BF16)
            dv_ref[rows, c] = dot(probs.astype(BF16), do2).astype(BF16)
            dk_ref[rows, c] = dot(ds, q2).astype(BF16)
            part = dot(kb.T, ds)
            dq_t = part if dq_t is None else dq_t + part
        dq_ref[0:LL, c] = (unstack_heads(dq_t, LL) * HD**-0.5).astype(BF16)
        for i in range(NS):
            off = LL + i * LS
            q2 = stack_heads(q_ref[off : off + LS, c], masks)
            do2 = stack_heads(do_ref[off : off + LS, c], masks)
            delta = row_dots(do2, o_ref[off : off + LS, c])
            lse = lse_s[p * NS + i][0:1]
            kb = jnp.concatenate([k_ref[r * T + off : r * T + off + LS, c] for r in range(n)], 0)
            vb = jnp.concatenate([v_ref[r * T + off : r * T + off + LS, c] for r in range(n)], 0)
            s = dot_t(kb, q2)
            lim = limits(2 * LS, LS, me, info[1 + i], causal)
            s = jnp.where(key_positions(0, n * LS, 2 * LS, LS, me) <= lim, s, NEG)
            probs = jnp.exp(s - lse)
            ds = (probs * (dot_t(vb, do2) - delta)).astype(BF16)
            dv = dot(probs.astype(BF16), do2).astype(BF16)
            dk = dot(ds, q2).astype(BF16)
            for r in range(n):
                dv_ref[r * T + off : r * T + off + LS, c] = dv[r * LS : (r + 1) * LS]
                dk_ref[r * T + off : r * T + off + LS, c] = dk[r * LS : (r + 1) * LS]
            dq_ref[off : off + LS, c] = (unstack_heads(dot(kb.T, ds), LS) * HD**-0.5).astype(BF16)

    loop(last, pair, first)


def flip(index, bit):
    return index + bit - 2 * bit * ((index // bit) % 2)


class Link:
    def __init__(self, send_sems, recv_sems):
        self.send_sems, self.recv_sems, self.used = send_sems, recv_sems, 0

    def start(self, src, dst, axis, bit):
        copy = pltpu.make_async_remote_copy(
            src_ref=src,
            dst_ref=dst,
            send_sem=self.send_sems.at[self.used],
            recv_sem=self.recv_sems.at[self.used],
            device_id={axis: flip(lax.axis_index(axis), bit)},
            device_id_type=pl.DeviceIdType.MESH,
        )
        self.used += 1
        copy.start()
        return copy


PATH_A = (("seq", 1), ("seq", 2), ("rep", 1))
PATH_B = (("seq", 1), ("rep", 1), ("seq", 2))
PATH_ROWS = (("seq", 1), ("seq", 2))
DP_BITS = (1, 2)
PATH_ALL = PATH_A + (("dp", 1), ("dp", 2))
TILE = 256
FFN_ROWS = 384
FEED_TASKS = ("u0", "u1", "u2", "w0", "w1", "w2")
FEED_ORDER = ("w0", "g0", "g1", "w1", "g2", "w2", "g3")
X_FIRST = ("u0", "u2", "c1", "c2", "s1", "s2a")
PATHS = {
    name: PATH_A if name in X_FIRST else PATH_B
    for name in FEED_TASKS + ("c0", "c1", "c2", "s0", "s1", "s2a", "s2b")
}
SELF_SLOTS = (0, 1, 2)
PLAN = (
    ("w0",),
    (),
    ("u0", "w0"),
    ("w1",),
    ("u1", "u0"),
    ("w2", "w1"),
    ("u2", "u1", "w2"),
    ("w0", "u2"),
    ("u0", "w1", "w0"),
    ("c0",),
    ("w0", "c0"),
    ("c1", "u1", "u2"),
    ("w0", "c1", "w1"),
    ("c2", "w2", "u1"),
    ("w0",),
    ("dm", "w1", "u0", "c2", "u1"),
    (),
    ("w0", "dm", "w1", "c1", "u0"),
    ("u1", "c0", "w1", "w2"),
    ("u0", "u2", "u1", "w1", "w2", "c1"),
    ("s0", "c2"),
    ("u0", "u2", "w2", "s0", "u1", "c1", "c2"),
    ("s1",),
    ("u0", "u2", "c2", "w2", "s1", "dm", "c1"),
    ("s2a", "s2b", "vec", "c0", "s0", "u2", "w2"),
    ("s2a", "c2", "s2b", "vec", "c0", "c1"),
    ("dx", "u2"),
    ("c2", "s1"),
    ("c1", "c0", "s2b", "dx"),
)
FINAL = (
    "c2", "s0", "c0", "s1", "s2a", "s0", "vec", "c0", "s2b", "s1",
    "s2a", "s0", "vec", "s2b", "s2a", "s1", "vec", "s0", "s2b", "s2a",
    "s0", "s1", "dx", "vec", "s1", "s2b", "s2a", "s2b", "s2a",
)


class Gather:
    def __init__(self, link, ref, rows):
        self.link, self.ref, self.rows = link, ref, rows

    def block(self, r, part=None):
        first, count = r * self.rows, self.rows
        if part is not None:
            count = self.rows // 2
            first = first + part * count
        return self.ref.at[first : first + count]

    def send_core(self):
        self.core = self.link.start(self.block(0), self.block(1), "seq", 1)

    def send_far(self):
        self.far = [
            self.link.start(self.block(0, p), self.block(2, p), "seq", 2) for p in range(2)
        ]

    def relay(self):
        self.relayed = []
        for p in range(2):
            self.far[p].wait()
            self.relayed.append(self.link.start(self.block(2, p), self.block(3, p), "seq", 1))

    def end(self):
        for copy in self.relayed:
            copy.wait()


def greet(pairs):
    barrier = pltpu.get_barrier_semaphore()
    for axis, bit in pairs:
        pl.semaphore_signal(
            barrier,
            inc=1,
            device_id={axis: flip(lax.axis_index(axis), bit)},
            device_id_type=pl.DeviceIdType.MESH,
        )
    pl.semaphore_wait(barrier, len(pairs))


def forward_kernel(dims, *refs):
    T, LL, LS, NS, D, n = dims
    refs = list(refs)

    def take(count):
        out = refs[:count]
        del refs[:count]
        return out

    long_len, short_len, xl, xs, ml, ms = take(6)
    info = row_info(long_len, short_len, NS)
    ws_hbm, wos_hbm, wc_hbm, woc_hbm, bias_s, bias_c, gain, shift = take(8)
    q1, k1_out, v1_out, o1, lse1l, lse1s, z1, t1_out = take(8)
    q2, k2_out, v2_out, o2, lse2l, lse2s, z2, t2_out = take(8)
    x, m, ws, wos, wc, woc, k1, v1, k2, v2, blk_t, mem_t, s_scr, sems, send_sems, recv_sems = refs
    copies = Copies(sems)
    load_x = [copies.start(xl, x.at[0:LL]), copies.start(xs, x.at[LL:T])]
    load_ws = copies.start(ws_hbm, ws)
    load_m = [copies.start(ml, m.at[0:LL]), copies.start(ms, m.at[LL:T])]
    load_wc = copies.start(wc_hbm, wc)
    load_wos, load_woc = copies.start(wos_hbm, wos), copies.start(woc_hbm, woc)
    greet(PATH_ROWS)
    link = Link(send_sems, recv_sems)
    rows_x, rows_m = Gather(link, x, T), Gather(link, m, T)
    for item in load_x:
        item.wait()
    rows_x.send_far()
    rows_x.send_core()
    for item in load_m:
        item.wait()
    rows_m.send_core()

    def queries(source, w, bias, q):
        def body(j):
            c = tile(j, TILE)
            out = dot(source[0:T, :].astype(BF16), w[0, :, c]) + bias[0:1, c]
            q[:, c] = (out.astype(BF16).astype(F32) * HD**-0.5).astype(BF16)

        loop(D // TILE, body)

    def keys_values(source, w, bias, k, v, r):
        rows = slice(r * T, (r + 1) * T)

        def body(j):
            c = tile(j, TILE)
            k[rows, c] = dot(source[rows, :], w[1, :, c]).astype(BF16)
            v[rows, c] = (dot(source[rows, :], w[2, :, c]) + bias[1:2, c]).astype(BF16)

        loop(D // TILE, body)

    def residual(source, o, wo, bias, z):
        def body(j):
            c = tile(j, TILE)
            z[:, c] = source[0:T, c].astype(F32) + dot(o[...], wo[:, c]) + bias[2:3, c]

        loop(D // TILE, body)

    load_ws.wait()
    queries(x, ws, bias_s, q1)
    keys_values(x, ws, bias_s, k1, v1, 0)
    transpose_into(blk_t, x, T, D, 0)
    load_wc.wait()
    keys_values(m, wc, bias_c, k2, v2, 0)
    transpose_into(mem_t, m, T, D, 0)
    rows_x.core.wait()
    keys_values(x, ws, bias_s, k1, v1, 1)
    transpose_into(blk_t, x, T, D, T)
    rows_m.core.wait()
    keys_values(m, wc, bias_c, k2, v2, 1)
    transpose_into(mem_t, m, T, D, T)
    rows_x.relay()
    rows_m.send_far()
    keys_values(x, ws, bias_s, k1, v1, 2)
    transpose_into(blk_t, x, T, D, 2 * T)
    rows_x.end()
    keys_values(x, ws, bias_s, k1, v1, 3)
    transpose_into(blk_t, x, T, D, 3 * T)
    stores = [copies.start(k1, k1_out), copies.start(v1, v1_out)]
    stores.append(copies.start(blk_t, t1_out))
    attend_forward(dims, True, info, q1, k1, v1, o1, lse1l, lse1s, s_scr)
    load_wos.wait()
    residual(x, o1, wos, bias_s, z1)
    rows_m.relay()
    xhat, _ = norm_parts(z1[...])
    z2[...] = xhat * gain[0:1] + shift[0:1]
    queries(z2, wc, bias_c, q2)
    keys_values(m, wc, bias_c, k2, v2, 2)
    transpose_into(mem_t, m, T, D, 2 * T)
    rows_m.end()
    keys_values(m, wc, bias_c, k2, v2, 3)
    transpose_into(mem_t, m, T, D, 3 * T)
    stores += [copies.start(k2, k2_out), copies.start(v2, v2_out), copies.start(mem_t, t2_out)]
    attend_forward(dims, False, info, q2, k2, v2, o2, lse2l, lse2s, s_scr)
    load_woc.wait()
    residual(z2, o2, woc, bias_c, z2)
    for item in stores:
        item.wait()


def forward_call(dims, *operands):
    T, LL, LS, NS, D, n = dims
    pairs = D // PAIR
    full, own = (n * T, D), (T, D)
    outs = [
        jax.ShapeDtypeStruct(own, BF16),
        jax.ShapeDtypeStruct(full, BF16),
        jax.ShapeDtypeStruct(full, BF16),
        jax.ShapeDtypeStruct(own, BF16),
        jax.ShapeDtypeStruct((pairs, 8, 2 * LL), F32),
        jax.ShapeDtypeStruct((pairs * NS, 8, 2 * LS), F32),
        jax.ShapeDtypeStruct(own, F32),
        jax.ShapeDtypeStruct((D, n * T), BF16),
    ]
    return pl.pallas_call(
        functools.partial(forward_kernel, dims),
        out_shape=outs + outs,
        in_specs=[SMEM] * 2 + [HBM] * 8 + [VMEM] * 4,
        out_specs=[VMEM, HBM, HBM, VMEM, VMEM, VMEM, VMEM, HBM] * 2,
        scratch_shapes=[pltpu.VMEM(full, BF16)] * 2
        + [pltpu.VMEM((3, D, D), BF16), pltpu.VMEM((D, D), BF16)] * 2
        + [pltpu.VMEM(full, BF16)] * 4
        + [
            pltpu.VMEM((D, n * T), BF16),
            pltpu.VMEM((D, n * T), BF16),
            pltpu.VMEM((n * LL, 2 * LL), F32),
            pltpu.SemaphoreType.DMA((16,)),
            pltpu.SemaphoreType.DMA((10,)),
            pltpu.SemaphoreType.DMA((10,)),
        ],
        compiler_params=pltpu.CompilerParams(
            collective_id=1, has_side_effects=True, vmem_limit_bytes=58 * MIB
        ),
        cost_estimate=pl.CostEstimate(
            flops=20 * 10**9, bytes_accessed=40 * 10**6, transcendentals=8 * 10**6
        ),
        name="forward",
    )(*operands)


def feed_phase(dims, loads, copies, data, scratch, vec, store_task, outs, tick):
    T, LL, LS, NS, D, n = dims
    upb, downb, gain, shift = data
    zb, acc, wu, wd, low, h2t, block, gp, act_t, dy_ref, y_ref = scratch
    tiles = D // TILE
    groups = len(wu)
    rows = D // 8
    loads["z2"].wait()
    xhat2, _ = norm_parts(zb[...])
    h2 = xhat2 * gain[1:2] + shift[1:2]
    low[...] = h2.astype(BF16)
    acc[...] = h2 + downb[...][None, :]
    transpose_into(h2t, low, T, D)

    def up_tile(q, t):
        c = tile(t, TILE)
        u = dot(low[...], wu[q][:, c]) + upb[q * D + t * TILE : q * D + (t + 1) * TILE][None, :]
        sq = u * u
        th = jnp.tanh(0.7978845608028654 * u * (1.0 + 0.044715 * sq))
        half = 0.5 * (1.0 + th)
        act = (u * half).astype(BF16)
        block[:, c] = act
        act_t[tile(t, TILE), q * T : (q + 1) * T] = act.T
        slope = half + (0.5 * 0.7978845608028654) * u * (1.0 - th * th) * (
            1.0 + (3.0 * 0.044715) * sq
        )
        gp[q * tiles + t] = slope.astype(BF16)

    def down_tile(q, j):
        c = tile(j, TILE)
        acc[:, c] += dot(block[...], wd[q][:, c])

    for q in range(groups):
        loads["up", q].wait()
        loop(tiles, functools.partial(up_tile, q))
        loads["down", q].wait()
        loop(tiles, functools.partial(down_tile, q))
    xhat3, rstd3 = norm_parts(acc[...])
    y_ref[...] = (xhat3 * gain[2:3] + shift[2:3]).astype(BF16)
    stores = [copies.start(y_ref.at[0:LL], outs[0]), copies.start(y_ref.at[LL:T], outs[1])]
    for item in loads["dy"]:
        item.wait()
    dy = dy_ref[...].astype(F32)
    vec[8:9] = col_sum(dy * xhat3)
    vec[11:12] = col_sum(dy)
    dz3 = norm_back(dy, gain[2:3], xhat3, rstd3)
    low[...] = dz3.astype(BF16)
    acc[...] = dz3
    vec[12:13] = col_sum(low[...])

    def down_grad(t):
        size = 4 * rows
        parts = []
        for q in range(groups):
            value = dot(act_t[:, q * T : (q + 1) * T], low[:, t * TILE : (t + 1) * TILE])
            value = value.astype(BF16)
            parts += [(None, 0, value[i : i + size]) for i in range(0, D, size)]
        store_task(tiles + t, parts)

    def back_tile(j, q):
        c = tile(j, TILE)
        acc[:, c] += dot_t(block[...], wu[q][c, :])

    def up_grad(q):
        for t in range(tiles):
            c = slice(t * TILE, (t + 1) * TILE)
            j = q * tiles + t
            du = (gp[j].astype(F32) * dot_t(low[...], wd[q][c, :])).astype(BF16)
            vec[13 + q : 14 + q, c] = col_sum(du)
            block[:, c] = du
            value = dot(h2t[...], du).astype(BF16)
            store_task(
                j // 4, [(i, (j % 4) * rows, value[i * rows : (i + 1) * rows]) for i in range(8)]
            )
        for t in range(tiles):
            back_tile(t, q)

    for step in FEED_ORDER:
        if step[0] == "w":
            down_grad(int(step[1]))
        else:
            up_grad(int(step[1]))
        tick()
    dh2 = acc[...]
    xhat2, rstd2 = norm_parts(zb[...])
    vec[7:8] = col_sum(dh2 * xhat2)
    vec[10:11] = col_sum(dh2)
    acc[...] = norm_back(dh2, gain[1:2], xhat2, rstd2)
    for item in stores:
        item.wait()


def backward_phase(dims, cross, chunks, info, loads, data, scratch, vec, row_of, tick, free):
    T, LL, LS, NS, D, n = dims
    dz, z_in, gain, shift, lse_l, lse_s = data
    q, o, w, wo, k, v, dq, do, da, blk_t, o_t, src_t, dblk, grads = scratch
    rows = D // chunks
    base = 3 if cross else 0

    def weight_grad(i, slot, lhs_t, rhs):
        grad = dot(lhs_t, rhs).astype(BF16)
        for s in range(chunks):
            at = pl.ds(row_of(i, slot, s), rows)
            grads[i, at, :] = grad[s * rows : (s + 1) * rows]

    da[...] = dz[...].astype(BF16)
    vec[base + 2 : base + 3] = col_sum(da[...])
    loads["o"].wait()
    transpose_into(o_t, o, T, D)
    loads["wo"].wait()
    for i in range(D // TILE):
        c = slice(i * TILE, (i + 1) * TILE)
        do[:, c] = dot_t(da[...], wo[c, :]).astype(BF16)
        weight_grad(i, 0, o_t[...], da[:, c])
    free("wo")
    if cross:
        xhat, _ = norm_parts(z_in[...])
        da[...] = (xhat * gain[0:1] + shift[0:1]).astype(BF16)
        transpose_into(src_t, da, T, D)
    tick()
    for name in ("q", "k", "v", "t"):
        loads[name].wait()
    if not cross:
        src_t[...] = blk_t[:, 0:T]
    pairs = TILE // PAIR
    for i in range(D // TILE):
        c = slice(i * TILE, (i + 1) * TILE)
        attend_backward(
            dims, not cross, info, q, k, v, o, do, lse_l, lse_s, dq, k, v, pairs * i, pairs * (i + 1)
        )
        tick()
        vec[base : base + 1, c] = col_sum(dq[:, c])
        vec[base + 1 : base + 2, c] = col_sum(v[:, c])
        weight_grad(i, 1, src_t[...], dq[:, c])
        weight_grad(i, 2, blk_t[...], k[:, c])
        weight_grad(i, 3, blk_t[...], v[:, c])
        tick()
    for name in ("q", "o", "t"):
        free(name)
    loads["w"].wait()
    free("dblk")

    def dblk_tile(i, at, j):
        c = tile(j, TILE)
        rows_in = slice(i * T, (i + 1) * T)
        part = dot_t(k[rows_in, :], w[1, c, :]) + dot_t(v[rows_in, :], w[2, c, :])
        if i == 0:
            part_q = dz[:, c] + dot_t(dq[...], w[0, c, :])
            if cross:
                dz[:, c] = part_q
            else:
                part = part + part_q
        dblk[at * T : (at + 1) * T, c] = part.astype(BF16)

    kept_first = sorted(range(n), key=lambda r: (r % 2, r // 2))
    for at in reversed(range(n)):
        loop(D // TILE, functools.partial(dblk_tile, kept_first[at], at))
        if at > 0:
            tick()
    for name in ("k", "v", "w"):
        free(name)
    tick()
    if cross:
        dh = dz[...]
        xhat, rstd = norm_parts(z_in[...])
        vec[6:7] = col_sum(dh * xhat)
        vec[9:10] = col_sum(dh)
        dz[...] = norm_back(dh, gain[0:1], xhat, rstd)


def add_rows(dst, dst_at, a, a_at, b, b_at, count, step=96):
    def body(i):
        def at(start):
            return pl.ds(pl.multiple_of(start + i * step, 16), step)

        total = a[at(a_at), :].astype(F32) + b[at(b_at), :].astype(F32)
        dst[at(dst_at), :] = total.astype(dst.dtype)

    loop(count // step, body)


class Share:
    def __init__(self, link, theirs, acc, recv, res, size, path, dp_bits):
        self.link, self.theirs, self.acc, self.recv, self.res = link, theirs, acc, recv, res
        self.size, self.path, self.dp_bits = size, path, dp_bits
        self.stage, self.copy, self.at = 0, None, 0
        self.off, self.count = 0, size
        self.kept, self.last = [], len(path) + 2 * len(dp_bits)

    def advance(self):
        stage, path, dp_bits = self.stage, self.path, self.dp_bits
        if stage > self.last:
            return
        self.stage += 1
        halves = len(path)
        if stage == 0:
            rows = self.size << (halves - 1)
            self.land, self.rows = self.at, rows
            self.at += rows
            land = self.recv.at[0:rows]
            if len(self.theirs.shape) == 3:
                land = land.reshape(*self.theirs.shape)
            self.copy = self.link.start(self.theirs, land, *path[0])
            return
        self.copy.wait()
        if stage <= halves + len(dp_bits):
            last = stage == halves + len(dp_bits)
            dst = self.res if last else self.acc
            add_rows(dst, self.off, self.acc, self.off, self.recv, self.land, self.rows, 48)
        if stage < halves:
            rows = self.size << (halves - 1 - stage)
            self.land, self.rows = self.at, rows
            self.at += rows
            src = self.acc.at[rows : 2 * rows]
            dst = self.recv.at[self.land : self.land + rows]
            self.copy = self.link.start(src, dst, *path[stage])
        elif stage < halves + len(dp_bits):
            bit = dp_bits[stage - halves]
            mine = (lax.axis_index("dp") // bit) % 2
            self.count //= 2
            give = self.off + (1 - mine) * self.count
            self.off = self.off + mine * self.count
            self.kept.append((self.off, self.count, bit))
            self.land, self.rows = self.at, self.count
            self.at += self.count
            src = self.acc.at[pl.ds(pl.multiple_of(give, 16), self.count)]
            dst = self.recv.at[self.land : self.land + self.count]
            self.copy = self.link.start(src, dst, "dp", bit)
        elif self.kept:
            off, count, bit = self.kept.pop()
            part = self.res.at[pl.ds(pl.multiple_of(off, 16), count)]
            self.copy = self.link.start(part, part, "dp", bit)


class Rows:
    def __init__(self, link, copies, blocks, recv, lands, out, size, path):
        self.link, self.copies, self.blocks, self.recv, self.out = link, copies, blocks, recv, out
        self.size, self.path, self.stage, self.lands, self.last = size, path, 0, lands, len(path)

    def advance(self):
        stage, path = self.stage, self.path
        if stage > self.last:
            return
        self.stage += 1
        if stage > 0:
            self.copy.wait()
            add_rows(self.blocks, 0, self.blocks, 0, self.recv, self.land, self.rows)
        if stage == len(path):
            self.store = self.copies.start(self.blocks.at[0 : self.rows], self.out)
        if stage < len(path):
            rows = self.size << (len(path) - 1 - stage)
            self.land, self.rows = self.lands[stage], rows
            src = self.blocks.at[rows : 2 * rows]
            dst = self.recv.at[self.land : self.land + rows]
            self.copy = self.link.start(src, dst, *path[stage])


class Small:
    def __init__(self, link, vec, recv, path):
        self.link, self.vec, self.recv, self.path, self.stage = link, vec, recv, path, 0
        self.last = len(path)

    def advance(self):
        stage, path = self.stage, self.path
        if stage > self.last:
            return
        self.stage += 1
        if stage > 0:
            self.copy.wait()
            self.vec[stage] = self.vec[stage - 1] + self.recv[stage - 1]
        if stage < len(path):
            self.copy = self.link.start(self.vec.at[stage], self.recv.at[stage], *path[stage])


def inner_place(path, s):
    x = (s // 4 + lax.axis_index("seq") // 2) % 2
    y = (s + lax.axis_index("rep")) % 2
    return x * 2 + y if path is PATH_A else y * 2 + x


def xor_place(path, s):
    return (s // 2 + lax.axis_index("seq")) % 2 * 4 + inner_place(path, s)


def backward_kernel(dims, linked, *refs):
    T, LL, LS, NS, D, n = dims
    chunks = 8
    half = chunks // 2
    size = FFN_ROWS
    tiles = D // TILE
    refs = list(refs)

    def take(count):
        out = refs[:count]
        del refs[:count]
        return out

    long_len, short_len = take(2)
    info = row_info(long_len, short_len, NS)
    z2_hbm, z1_hbm, cot_l, cot_s, wup_hbm, wdown_hbm = take(6)
    cross_hbm, self_hbm = take(7), take(7)
    upb, downb, gain, shift, lse2l, lse2s, lse1l, lse1s = take(8)
    yl_out, ys_out = take(2)
    if linked:
        shares_out, dm_out, dx_out, vec_out = take(4)
    else:
        gf_out, gc_out, gs_out, dm_out, dx_out, vec_out = take(6)
    q, o, w, wo, k, v, dq, do, da, blk_t, o_t, src_t, dblk, dres, zb = take(15)
    gc, gs, accs, vec, sems = take(5)
    if linked:
        recvs, rows_recv, res, vec_recv, send_sems, recv_sems = take(6)

    copies = Copies(sems)
    homes = {"wo": wo, "o": o, "q": q, "k": k, "v": v, "t": blk_t, "w": w}
    sources_c = dict(zip(("w", "wo", "k", "v", "q", "o", "t"), cross_hbm))
    sources_s = dict(zip(("w", "wo", "k", "v", "q", "o", "t"), self_hbm))
    wu = [(k, v)[i // 2].at[(i % 2) * D : (i % 2 + 1) * D] for i in range(4)]
    wd = [w.at[0], w.at[1], w.at[2], dblk.at[0:D]]
    loads_f = {"z2": copies.start(z2_hbm, zb)}
    for i in range(4):
        loads_f["up", i] = copies.start(wup_hbm.at[:, i * D : (i + 1) * D], wu[i])
        loads_f["down", i] = copies.start(wdown_hbm.at[i * D : (i + 1) * D], wd[i])
    loads_f["dy"] = [copies.start(cot_l, do.at[0:LL]), copies.start(cot_s, do.at[LL:T])]
    loads_c = {name: copies.start(sources_c[name], homes[name]) for name in ("o", "wo")}
    vec[0] = jnp.zeros((VEC_ROWS, D), F32)

    def theirs(i):
        return gs.at[i // 2, (i % 2) * half * size : (i % 2 + 1) * half * size]

    tasks = {}
    steps = iter(PLAN)

    def tick():
        if linked:
            for name in next(steps):
                tasks[name].advance()

    if linked:
        greet(PATH_ALL)
        link = Link(send_sems, recv_sems)
        for i, name in enumerate(FEED_TASKS):
            tasks[name] = Share(
                link, theirs(i), accs.at[i], recvs.at[i], res.at[i], size, PATHS[name], DP_BITS
            )
        whole = (0, chunks * size)
        for name, g, i, slot, (first, last) in (
            ("c0", gc, 0, 6, whole),
            ("c1", gc, 1, 7, whole),
            ("c2", gc, 2, 8, whole),
            ("s0", gs, 0, SELF_SLOTS[0], whole),
            ("s1", gs, 1, SELF_SLOTS[1], whole),
            ("s2a", gs, 2, SELF_SLOTS[2], (0, whole[1] // 2)),
            ("s2b", gs, 2, SELF_SLOTS[2], (whole[1] // 2, whole[1])),
        ):
            rows = last - first
            out = res.at[(6 if g is gc else 9) + i]
            landing = recvs.shape[1] * rows // whole[1]
            land = first * recvs.shape[1] // whole[1]
            tasks[name] = Share(
                link,
                g.at[i, first + rows // 2 : last],
                g.at[i, first:last],
                recvs.at[slot, land : land + landing],
                out.at[first // chunks : last // chunks],
                rows // chunks,
                PATHS[name],
                DP_BITS,
            )
        tasks["dm"] = Rows(link, copies, dblk, rows_recv, (0, 2 * T), dm_out, T, PATH_ROWS)
        tasks["dx"] = Rows(link, copies, dblk, rows_recv, (0, 3 * T), dx_out, T, PATH_ROWS)
        tasks["vec"] = Small(link, vec, vec_recv, PATH_ALL)

    def row_of(kind, i, slot, s):
        rows = size // 4
        if not linked:
            return s * size + slot * rows
        name = kind + str(i)
        if name != "s2":
            return pl.multiple_of(xor_place(PATHS[name], s) * size + slot * rows, 16)
        at = xor_place(PATHS[name + "ab"[slot // 2]], s) * 2 * rows + slot % 2 * rows
        return pl.multiple_of(slot // 2 * chunks * 2 * rows + at, 16)


    side = lax.axis_index("seq") % 2

    def store_task(i, parts):
        for s in range(chunks):
            if s // 2 % 2:
                continue
            (_, off, low_part), (_, _, high_part) = parts[s], parts[s + 2]
            if linked:
                place = inner_place(PATHS[FEED_TASKS[i]], s)
                at = pl.multiple_of(place * size + off, 16)
                rows = pl.ds(at, low_part.shape[0])
                accs[i, rows, :] = jnp.where(side == 0, low_part, high_part)
                theirs(i)[rows, :] = jnp.where(side == 0, high_part, low_part)
            else:
                for c, part in ((s, low_part), (s + 2, high_part)):
                    out = accs.at[i] if c < half else theirs(i)
                    at = c % half * size + off
                    out[at : at + part.shape[0], :] = part

    feed_phase(
        dims, loads_f, copies, (upb, downb, gain, shift),
        (zb, dres, wu, wd, da, src_t, q, gc.reshape(chunks * tiles, T, TILE), blk_t, do, dq),
        vec.at[0], store_task, (yl_out, ys_out), tick,
    )
    load_z1 = copies.start(z1_hbm, zb)
    for name in ("q", "k", "v", "t", "w"):
        loads_c[name] = copies.start(sources_c[name], homes[name])
    load_z1.wait()
    if not linked:
        for i in range(2 * tiles):
            copies.start(accs.at[i], gf_out.at[i, 0]).wait()
            copies.start(theirs(i), gf_out.at[i, 1]).wait()
    loads_s = {}

    def free_cross(name):
        if name in homes:
            loads_s[name] = copies.start(sources_s[name], homes[name])

    def free_self(name):
        if linked and name == "dblk":
            while tasks["dm"].stage <= tasks["dm"].last:
                tasks["dm"].advance()
            tasks["dm"].store.wait()

    backward_phase(
        dims, True, chunks, info, loads_c, (dres, zb, gain, shift, lse2l, lse2s),
        (q, o, w, wo, k, v, dq, do, da, blk_t, o_t, src_t, dblk, gc), vec.at[0], functools.partial(row_of, "c"), tick,
        free_cross,
    )
    if not linked:
        stores = [copies.start(gc, gc_out)]
        copies.start(dblk, dm_out).wait()
    backward_phase(
        dims, False, chunks, info, loads_s, (dres, None, None, None, lse1l, lse1s),
        (q, o, w, wo, k, v, dq, do, da, blk_t, o_t, src_t, dblk, gs), vec.at[0], functools.partial(row_of, "s"), tick,
        free_self,
    )
    if linked:
        for name in FINAL:
            tasks[name].advance()
        for task in tasks.values():
            while task.stage <= task.last:
                task.advance()
        copies.start(res, shares_out).wait()
        tasks["dx"].store.wait()
        vec_out[...] = vec[len(PATH_ALL)]
    else:
        vec_out[...] = vec[0]
        stores += [copies.start(gs, gs_out), copies.start(dblk, dx_out)]
        for item in stores:
            item.wait()


def backward_call(dims, linked, info, feed_hbm, cross_hbm, self_hbm, small):
    T, LL, LS, NS, D, n = dims
    full, own = (n * T, D), (T, D)
    tiles = D // TILE
    size = FFN_ROWS
    grads = (tiles, 8 * size, TILE)
    vec = jax.ShapeDtypeStruct((VEC_ROWS, D), F32)
    steps = len(PATH_ALL)
    out_shape = [jax.ShapeDtypeStruct((LL, D), BF16), jax.ShapeDtypeStruct((T - LL, D), BF16)]
    if linked:
        out_shape += [
            jax.ShapeDtypeStruct((4 * tiles, size, TILE), BF16),
            jax.ShapeDtypeStruct(own, BF16),
            jax.ShapeDtypeStruct(own, BF16),
            vec,
        ]
        landing = 7 * size + 3 * size // 4
        count = (4 * tiles + 1) * 7 + 4 + steps
        extra = [
            pltpu.VMEM((3 * tiles, landing, TILE), BF16),
            pltpu.VMEM((4 * T, D), BF16),
            pltpu.VMEM((4 * tiles, size, TILE), BF16),
            pltpu.VMEM((steps, VEC_ROWS, D), F32),
            pltpu.SemaphoreType.DMA((count,)),
            pltpu.SemaphoreType.DMA((count,)),
        ]
    else:
        out_shape += [
            jax.ShapeDtypeStruct((2 * tiles, 2, 4 * size, TILE), BF16),
            jax.ShapeDtypeStruct(grads, BF16),
            jax.ShapeDtypeStruct(grads, BF16),
            jax.ShapeDtypeStruct(full, BF16),
            jax.ShapeDtypeStruct(full, BF16),
            vec,
        ]
        extra = []
    params = {"collective_id": 0} if linked else {}
    return pl.pallas_call(
        functools.partial(backward_kernel, dims, linked),
        out_shape=out_shape,
        in_specs=[SMEM] * 2 + [HBM] * 20 + [VMEM] * 8,
        out_specs=[HBM] * (len(out_shape) - 1) + [VMEM],
        scratch_shapes=[
            pltpu.VMEM(own, BF16),
            pltpu.VMEM(own, BF16),
            pltpu.VMEM((3, D, D), BF16),
            pltpu.VMEM((D, D), BF16),
            pltpu.VMEM(full, BF16),
            pltpu.VMEM(full, BF16),
            pltpu.VMEM(own, BF16),
            pltpu.VMEM(own, BF16),
            pltpu.VMEM(own, BF16),
            pltpu.VMEM((D, n * T), BF16),
            pltpu.VMEM((D, T), BF16),
            pltpu.VMEM((D, T), BF16),
            pltpu.VMEM(full, BF16),
            pltpu.VMEM(own, F32),
            pltpu.VMEM(own, F32),
            pltpu.VMEM(grads, BF16),
            pltpu.VMEM(grads, BF16),
            pltpu.VMEM((2 * tiles, 4 * size, TILE), BF16),
            pltpu.VMEM((steps + 1, VEC_ROWS, D), F32),
            pltpu.SemaphoreType.DMA((48,)),
        ]
        + extra,
        compiler_params=pltpu.CompilerParams(
            vmem_limit_bytes=60 * MIB, has_side_effects=True, **params
        ),
        cost_estimate=pl.CostEstimate(
            flops=100 * 10**9, bytes_accessed=60 * 10**6, transcendentals=8 * 10**6
        ),
        name="backward",
    )(*info, *feed_hbm, *cross_hbm, *self_hbm, *small)


def finish_kernel(dims, mesh_sizes, yl, ys, shares_hbm, dm, dx, vec_hbm, *refs):
    T, LL, LS, NS, D, n = dims
    *outs, shares, vec, sems = refs
    (
        y_l, y_s, dx_l, dx_s, dm_l, dm_s, g_self, g_selfout, b_self, g_cross, g_crossout, b_cross,
        g_gain, g_shift, g_up, b_up, g_down, b_down,
    ) = outs
    shards = mesh_sizes[1] * mesh_sizes[2]
    mine = lax.axis_index("seq") * mesh_sizes[2] + lax.axis_index("rep")
    copies = Copies(sems)
    load_vec, load_shares = copies.start(vec_hbm, vec), copies.start(shares_hbm, shares)
    pairs = ((yl, y_l), (ys, y_s), (dx.at[0:LL], dx_l), (dx.at[LL:T], dx_s), (dm.at[0:LL], dm_l), (dm.at[LL:T], dm_s))
    moves = [copies.start(src, dst) for src, dst in pairs]
    load_shares.wait()
    rows = D // shards
    for t in range(D // TILE):
        c = slice(t * TILE, (t + 1) * TILE)
        for i in range(4):
            part = slice(i * rows, (i + 1) * rows)
            j = 4 * t + i
            g_up[:, j * TILE : (j + 1) * TILE] = shares[t, part, :].astype(F32)
            for first, whole, alone in ((6, g_cross, g_crossout), (9, g_self, g_selfout)):
                value = shares[first + t, part, :].astype(F32)
                if i == 0:
                    alone[:, c] = value
                else:
                    whole[i - 1, :, c] = value
        g_down[:, c] = shares[3 + t].astype(F32)
    load_vec.wait()
    turned = pltpu.roll(vec[...], D - mine * rows, 1)
    for i, out in enumerate((b_self, b_cross, g_gain, g_shift)):
        out[...] = turned[3 * i : 3 * i + 3, 0:rows]
    b_down[...] = turned[12:13, 0:rows]
    ups = vec[13:14, :]
    per_row = D // (4 * rows)
    for i in range(1, 4):
        ups = jnp.where(mine // per_row == i, vec[13 + i : 14 + i, :], ups)
    out = ups[:, 0 : 4 * rows]
    for i in range(1, per_row):
        out = jnp.where(mine % per_row == i, ups[:, i * 4 * rows : (i + 1) * 4 * rows], out)
    b_up[...] = out
    for item in moves:
        item.wait()


def finish_call(dims, sizes, yl, ys, shares, dm, dx, vec):
    T, LL, LS, NS, D, n = dims
    rows = D // (sizes[1] * sizes[2])

    def shape(*dims):
        return jax.ShapeDtypeStruct(dims, F32)

    tokens = [jax.ShapeDtypeStruct((LL, D), BF16), jax.ShapeDtypeStruct((T - LL, D), BF16)]
    out_shape = tokens + tokens + tokens + [
        shape(3, rows, D), shape(rows, D), shape(3, rows), shape(3, rows, D), shape(rows, D),
        shape(3, rows), shape(3, rows), shape(3, rows), shape(rows, 4 * D), shape(1, 4 * rows),
        shape(4 * rows, D), shape(1, rows),
    ]
    return pl.pallas_call(
        functools.partial(finish_kernel, dims, sizes),
        out_shape=out_shape,
        in_specs=[HBM] * 6,
        out_specs=[VMEM] * len(out_shape),
        scratch_shapes=[
            pltpu.VMEM(shares.shape, BF16),
            pltpu.VMEM(vec.shape, F32),
            pltpu.SemaphoreType.DMA((8,)),
        ],
        compiler_params=pltpu.CompilerParams(vmem_limit_bytes=58 * MIB),
        name="finish",
    )(yl, ys, shares, dm, dx, vec)


def swap(a, axis, bit, size):
    return lax.ppermute(a, axis, [(i, i ^ bit) for i in range(size)])


def bits_of(size):
    return [1 << i for i in range(size.bit_length() - 1)]


def add_low(a, b):
    return (a.astype(F32) + b.astype(F32)).astype(BF16)


def halve(a, steps):
    for axis, bit, size in steps:
        half = a.shape[0] // 2
        a = add_low(a[:half], swap(a[half:], axis, bit, size))
    return a[0]


def all_sum(a, axis, size):
    rows, cols = a.shape
    me = lax.axis_index(axis)
    steps = bits_of(size)
    sent = []
    for bit in steps:
        mine = (me // bit) % 2
        a = a.reshape(2, a.shape[0] // 2, cols)
        keep = lax.dynamic_index_in_dim(a, mine, 0, keepdims=False)
        give = lax.dynamic_index_in_dim(a, 1 - mine, 0, keepdims=False)
        a = add_low(keep, swap(give, axis, bit, size))
        sent.append(mine)
    for bit, mine in zip(reversed(steps), reversed(sent)):
        other = swap(a, axis, bit, size)
        first = jnp.where(mine == 0, a, other)
        second = jnp.where(mine == 0, other, a)
        a = jnp.concatenate([first, second], axis=0)
    return a.reshape(rows, cols)


def on_device(
    sizes,
    long_rows,
    short_rows,
    long_memory,
    short_memory,
    long_cotangent,
    short_cotangent,
    long_lengths,
    short_lengths,
    self_qkv,
    self_out,
    self_bias,
    cross_qkv,
    cross_out,
    cross_bias,
    norm_gain,
    norm_bias,
    up_proj,
    up_bias,
    down_proj,
    down_bias,
):
    n_dp, n, n_rep = sizes
    count_l, LL, D = long_rows.shape
    NS, LS, _ = short_rows.shape
    FF = up_proj.shape[1]
    T = LL + NS * LS
    dims = (T, LL, LS, NS, D, n)
    shards = n * n_rep

    def flat(a):
        return a.reshape(-1, D)

    me = lax.axis_index("seq")
    mine = me * n_rep + lax.axis_index("rep")
    info = (long_lengths, short_lengths)

    linked = (n_dp, n, n_rep) == (4, 4, 2)

    norm = (norm_gain, norm_bias)
    outs = forward_call(
        dims, *info, flat(long_rows), flat(short_rows), flat(long_memory), flat(short_memory),
        self_qkv, self_out, cross_qkv, cross_out, self_bias, cross_bias, *norm,
    )
    q1, k1, v1, o1, lse1l, lse1s, z1, xt = outs[:8]
    q2, k2, v2, o2, lse2l, lse2s, z2, mt = outs[8:]
    y_l, y_s, *results = backward_call(
        dims,
        linked,
        info,
        (z2, z1, flat(long_cotangent), flat(short_cotangent), up_proj, down_proj),
        (cross_qkv, cross_out, k2, v2, q2, o2, mt),
        (self_qkv, self_out, k1, v1, q1, o1, xt),
        (up_bias, down_bias, *norm, lse2l, lse2s, lse1l, lse1s),
    )
    rows = D // shards
    if linked:
        shares, dm, dx, small = results
        rest = finish_call(dims, sizes, y_l, y_s, shares, dm, dx, small)
        tokens, rest = rest[:6], list(rest[6:])
        rest[9], rest[11] = rest[9][0], rest[11][0]
        shapes = (long_rows.shape, short_rows.shape) * 3
        return tuple(a.reshape(b) for a, b in zip(tokens, shapes)) + tuple(rest)
    gf, gc, gs, dm, dx, small = results
    chunks = 8
    index = jnp.arange(shards, dtype=jnp.int32) ^ mine
    rel_seq, rel_rep = index // n_rep, index % n_rep
    core, rest = rel_seq % 2, rel_seq // 2
    pos_a = core * (shards // 2) + rest * n_rep + rel_rep
    pos_b = core * (shards // 2) + rel_rep * (n // 2) + rest
    steps_core = [("seq", 1, n)]
    steps_x = [("seq", bit, n) for bit in reversed(bits_of(n)[1:])]
    steps_y = [("rep", bit, n_rep) for bit in reversed(bits_of(n_rep))]

    def reduce_all(a, pos, steps):
        parts = a.reshape(shards, a.shape[0] // shards, a.shape[1])
        parts = jnp.zeros_like(parts).at[pos].set(parts)
        return all_sum(halve(parts, steps), "dp", n_dp)

    order_a = (pos_a, steps_core + steps_x + steps_y)
    order_b = (pos_b, steps_core + steps_y + steps_x)
    split = (D // TILE, chunks, 4, D // chunks, TILE)
    g_up = gf[: D // TILE].reshape(split).transpose(1, 3, 0, 2, 4).reshape(D, FF)
    g_down = gf[D // TILE :].reshape(D // TILE, chunks, FF // chunks, TILE)
    up_share = reduce_all(g_up, *order_a)
    down_share = reduce_all(g_down.transpose(1, 2, 0, 3).reshape(FF, D), *order_b)

    def four(g):
        mats = g.reshape(split).transpose(2, 1, 3, 0, 4).reshape(4, D, D)
        return jnp.stack([reduce_all(mats[i], *order_a) for i in range(4)])

    cross_share, self_share = four(gc), four(gs)
    seq_steps = [("seq", bit, n) for bit in bits_of(n)]
    dm = dm.reshape(n, T, D)
    dx = dx.reshape(n, T, D)
    dm = halve(dm, seq_steps)
    dx = halve(dx, seq_steps)
    small = lax.psum(small, ("dp", "seq", "rep"))

    def part(a, width):
        return lax.dynamic_slice_in_dim(a, mine * width, width, axis=-1)

    vecs = part(small[0:13], D // shards)
    upb_grad = part(small[13:17].reshape(-1), FF // shards)

    def unflat(a):
        return (
            a[:LL].reshape(count_l, LL, D),
            a[LL:].reshape(NS, LS, D),
        )

    y_l, y_s = y_l.reshape(long_rows.shape), y_s.reshape(short_rows.shape)
    dx_l, dx_s = unflat(dx)
    dm_l, dm_s = unflat(dm)
    cross_grad = cross_share.astype(F32)
    self_grad = self_share.astype(F32)
    return (
        y_l,
        y_s,
        dx_l,
        dx_s,
        dm_l,
        dm_s,
        self_grad[1:4],
        self_grad[0],
        vecs[0:3],
        cross_grad[1:4],
        cross_grad[0],
        vecs[3:6],
        vecs[6:9],
        vecs[9:12],
        up_share.astype(F32),
        upb_grad,
        down_share.astype(F32),
        vecs[12],
    )


def solution(mesh):
    rows = P(("dp", "rep"), "seq", None)
    lengths = P(("dp", "rep"))
    share = ("seq", "rep")
    in_specs = (rows,) * 6 + (lengths,) * 2 + (P(),) * 12
    out_specs = (rows,) * 6 + (
        P(None, share, None),
        P(share, None),
        P(None, share),
        P(None, share, None),
        P(share, None),
        P(None, share),
        P(None, share),
        P(None, share),
        P(share, None),
        P(share),
        P(share, None),
        P(share),
    )
    sizes = (mesh.shape["dp"], mesh.shape["seq"], mesh.shape["rep"])
    return jax.shard_map(
        functools.partial(on_device, sizes),
        mesh=mesh,
        in_specs=in_specs,
        out_specs=out_specs,
        check_vma=False,
    )
```
